256 devices in a mesh: ctx: 32 (over z, x_hi, core), head: 8 (over y, x_lo).
Axes of the slice: x: 4 (x_hi: 2, x_lo: 2; x = x_hi * 2 + x_lo), y: 4, z: 8, core: 2. Of those that a mesh axis runs over, the one named last changes fastest.
Arguments:
- queries: bfloat16 [16384, 8192], P(('ctx', 'head')), may hold values from -65 to 65
- key_codes: bfloat16 [16384, 1024], P(('ctx', 'head')), may hold values from -4 to 4
- rotated_value_codes: bfloat16 [16384, 1024], P(('ctx', 'head')), may hold values from -4 to 4
- key_exponents: int32 [16384, 8], P(('ctx', 'head')), may hold values from -2 to 2
- value_block_exponents: int32 [16384, 8], P(('ctx', 'head')), may hold values from -2 to 2
- trace_ids: int32 [16384], P('ctx'), may hold values from 0 to 15, never falling along the last dimension, each value on 1 to 2049 neighbouring positions
Outputs:
- attended: bfloat16 [16384, 8192], P('ctx', 'head')
The draws below stay inside these ranges and needn't reach their ends.
All inputs are finite; a program needn't handle non-finite values.
Results may differ from the reference program's by a relative error of at most 0.0022.
The reference program's roundings to bfloat16 on the way count: a program that leaves them out, or rounds other values in their place, can miss the bound.
Values may be sent and summed in bfloat16 or wider, within the bound.
A program may use at most 64 MiB of HBM per device.

```python
import math
import jax
import jax.numpy as jnp
import numpy as np
from jax import lax

QUERY_HEADS = 64
KEY_VALUE_HEADS = 8
HEAD_SIZE = 128
BLOCK_TOKENS = 512
STEPS = 4
SEQUENCE_TOKENS = 16384
SPAN_MOST = 2049
SPANS = 16
N_CTX = 32


def drawn(key):
    positions = lax.iota(jnp.int32, SEQUENCE_TOKENS)[:, None]
    selected_rows = jax.random.randint(jax.random.fold_in(key, 11), (SEQUENCE_TOKENS, KEY_VALUE_HEADS), 0, 16) == 0
    marked = selected_rows & (positions % 4 == 3)
    return marked


def draw_key_exponents(key, part):
    marked = drawn(key)
    key = jax.random.fold_in(key, 21)
    scale_exponents = jax.random.randint(key, (SEQUENCE_TOKENS, KEY_VALUE_HEADS), -2, 3)
    partner = jnp.roll(marked, -1, axis=0)
    return jnp.where(marked | partner, 2, scale_exponents).astype(jnp.int32)


def draw_key_codes(key, part):
    key = jax.random.fold_in(key, 22)
    quantized_codes = jnp.clip(jax.random.normal(key, (SEQUENCE_TOKENS, KEY_VALUE_HEADS, HEAD_SIZE), jnp.float32), -4.0, 4.0)
    return quantized_codes.reshape(SEQUENCE_TOKENS, KEY_VALUE_HEADS * HEAD_SIZE).astype(jnp.bfloat16)


def draw_queries(key, part):
    key = jax.random.fold_in(key, 23)
    query_groups = QUERY_HEADS // KEY_VALUE_HEADS
    value_rows = jnp.clip(jax.random.normal(key, (SEQUENCE_TOKENS, KEY_VALUE_HEADS, query_groups, HEAD_SIZE), jnp.float32), -6.0, 6.0)
    return value_rows.reshape(SEQUENCE_TOKENS, QUERY_HEADS * HEAD_SIZE).astype(jnp.bfloat16)


def touch_ends(values, rng, low, top_value):
    spot = [jax.random.randint(jax.random.fold_in(rng, axis), (), 0, length) for axis, length in enumerate(values.shape)]
    widest = values.shape.index(max(values.shape))
    beside = spot[:widest] + [(spot[widest] + 1) % values.shape[widest]] + spot[widest + 1:]
    return values.at[tuple(spot)].set(low).at[tuple(beside)].set(top_value)


def block_scale(rng, extent, cuts, low, high):
    def one(position, blocks):
        draws = jax.random.uniform(jax.random.fold_in(jax.random.fold_in(rng, 6), position), (blocks,), jnp.float32, low / len(cuts), high / len(cuts))
        return jnp.repeat(jnp.exp(draws), extent[position] // blocks).reshape((-1,) + (1,) * (len(extent) - position - 1))

    gain = one(*cuts[0])
    for cut in cuts[1:]:
        gain = gain * one(*cut)
    return gain


def profile(amount, total, bound, skew):
    weights = [(1 << 20) // math.isqrt(standing ** skew) + 1 for standing in range(2, amount + 1)]
    spare, counts = total - bound - (amount - 1), [1] * (amount - 1)
    while spare > 0:
        movable = [i for i in range(amount - 1) if counts[i] < bound]
        pool, left = sum([weights[i] for i in movable]), spare
        for i in movable:
            addition = min(bound - counts[i], max(1, left * weights[i] // pool), spare)
            counts[i] = counts[i] + addition
            spare = spare - addition
    return np.array([bound] + counts)


def ragged(stream_key, number_of, total, bound, slope):
    if number_of == 2:
        one = jax.random.randint(stream_key, (), max(1, total - bound), min(bound, total - 1) + 1)
        return jnp.stack([one, total - one])
    tallies = jnp.asarray(profile(number_of, total, bound, slope), jnp.int32)
    couples = (number_of - 1) // 2
    source_of, receiver = tallies[1:1 + 2 * couples:2], tallies[2:2 + 2 * couples:2]
    margin = jnp.minimum(source_of - 1, bound - receiver)
    moved = jax.random.randint(jax.random.fold_in(stream_key, 1), (couples,), 0, 1 << 20) % (margin + 1)
    tallies = tallies.at[1:1 + 2 * couples:2].set(source_of - moved).at[2:2 + 2 * couples:2].set(receiver + moved)
    return tallies[jax.random.permutation(jax.random.fold_in(stream_key, 2), number_of)]


def scatter_about(key, extent, width, bound, shards=(), kind=jnp.bfloat16):
    level = block_scale(key, extent, shards, -0.22, 0.18) if shards else 1.0
    values = jax.random.normal(key, extent, jnp.float32) * width * level
    return jnp.minimum(jnp.maximum(values, -bound), bound).astype(kind)


def setup_inputs(seed: int = 0) -> dict:
    streams_of = jax.random.split(jax.random.key(seed), 7)
    return {
        "queries": draw_queries(jax.random.fold_in(streams_of[6], 71), 0),
        "key_codes": draw_key_codes(jax.random.fold_in(streams_of[6], 71), 0),
        "rotated_value_codes": scatter_about(streams_of[2], (SEQUENCE_TOKENS, KEY_VALUE_HEADS * HEAD_SIZE), 1.0, 4.0, ((0, 256),)),
        "key_exponents": draw_key_exponents(jax.random.fold_in(streams_of[6], 71), 0),
        "value_block_exponents": touch_ends(jax.random.randint(streams_of[4], (SEQUENCE_TOKENS, KEY_VALUE_HEADS), -2, 3), jax.random.fold_in(streams_of[4], 1), -2, 2).astype(jnp.int32),
        "trace_ids": jnp.searchsorted(jnp.cumsum(ragged(streams_of[5], SPANS, SEQUENCE_TOKENS, SPAN_MOST, 1)), jnp.arange(SEQUENCE_TOKENS), side="right").astype(jnp.int32),
    }


def count_ones(value_rows, order):
    result = jnp.zeros_like(value_rows)
    for place in range(order.bit_length()):
        result = result + (value_rows >> place & 1)
    return result

def hadamard_signs(order):
    indices = lax.iota(jnp.int32, order)
    parity = count_ones(indices[:, None] & indices[None, :], order) % 2
    return (1 - 2 * parity).astype(jnp.bfloat16)

def dequantize(quantized_codes, scale_exponents):
    rows = quantized_codes.shape[0]
    heads = scale_exponents.shape[1]
    powers = jnp.exp2(scale_exponents.astype(jnp.float32)).astype(jnp.bfloat16)
    scaled = quantized_codes.reshape(rows, heads, HEAD_SIZE) * powers[:, :, None]
    rotated = jnp.dot(scaled.reshape(rows * heads, HEAD_SIZE), hadamard_signs(HEAD_SIZE), preferred_element_type=jnp.float32)
    rotated = rotated * (1.0 / math.sqrt(HEAD_SIZE))
    return rotated.astype(jnp.bfloat16).reshape(rows, heads, HEAD_SIZE)

def reference(queries, key_codes, rotated_value_codes, key_exponents, value_block_exponents, trace_ids):
    query_groups = QUERY_HEADS // KEY_VALUE_HEADS
    key_rows = dequantize(key_codes, key_exponents)
    value_rows = dequantize(rotated_value_codes, value_block_exponents)
    padding_margin = STEPS * BLOCK_TOKENS
    padded_key_rows = jnp.concatenate([jnp.zeros((padding_margin, KEY_VALUE_HEADS, HEAD_SIZE), jnp.bfloat16), key_rows], axis=0)
    padded_value_rows = jnp.concatenate([jnp.zeros((padding_margin, KEY_VALUE_HEADS, HEAD_SIZE), jnp.bfloat16), value_rows], axis=0)
    ids_padded = jnp.concatenate([jnp.full((padding_margin,), -1, jnp.int32), trace_ids], axis=0)
    offsets = lax.iota(jnp.int32, BLOCK_TOKENS)
    scale = 1.0 / math.sqrt(HEAD_SIZE)

    def one_block(block_number):
        block_number = block_number.astype(jnp.int32)
        query_vector = lax.dynamic_slice_in_dim(queries, block_number * BLOCK_TOKENS, BLOCK_TOKENS, 0).reshape(BLOCK_TOKENS, KEY_VALUE_HEADS, query_groups, HEAD_SIZE).astype(jnp.float32)
        query_ids = lax.dynamic_slice_in_dim(trace_ids, block_number * BLOCK_TOKENS, BLOCK_TOKENS, 0)
        query_pos = block_number * BLOCK_TOKENS + offsets
        running_maximum = jnp.full((BLOCK_TOKENS, KEY_VALUE_HEADS, query_groups), -jnp.inf, jnp.float32)
        weight_total = jnp.zeros((BLOCK_TOKENS, KEY_VALUE_HEADS, query_groups), jnp.float32)
        output_accumulator = jnp.zeros((BLOCK_TOKENS, KEY_VALUE_HEADS, query_groups, HEAD_SIZE), jnp.float32)
        for step in range(STEPS + 1):
            start = ((block_number - step) * BLOCK_TOKENS + padding_margin).astype(jnp.int32)
            key_block = lax.dynamic_slice_in_dim(padded_key_rows, start, BLOCK_TOKENS, 0).astype(jnp.float32)
            value_block = lax.dynamic_slice_in_dim(padded_value_rows, start, BLOCK_TOKENS, 0).astype(jnp.float32)
            key_ids = lax.dynamic_slice_in_dim(ids_padded, start, BLOCK_TOKENS, 0)
            key_pos = (block_number - step) * BLOCK_TOKENS + offsets
            allowed = (key_pos[None, :] <= query_pos[:, None]) & (key_pos[None, :] >= 0) & (key_ids[None, :] == query_ids[:, None])
            scores = jnp.einsum('qhgd,khd->qhgk', query_vector, key_block) * scale
            scores = jnp.where(allowed[:, None, None, :], scores, -jnp.inf)
            newmax = jnp.maximum(running_maximum, lax.optimization_barrier(jnp.max(scores, axis=-1)))
            weights = jnp.exp(scores - newmax[..., None])
            factor = jnp.exp(running_maximum - newmax)
            weight_total = weight_total * factor + lax.optimization_barrier(jnp.sum(weights, axis=-1))
            weights_low = weights.astype(jnp.bfloat16).astype(jnp.float32)
            output_accumulator = output_accumulator * factor[..., None] + jnp.einsum('qhgk,khd->qhgd', weights_low, value_block)
            running_maximum = newmax
        return (output_accumulator / weight_total[..., None]).astype(jnp.bfloat16).reshape(BLOCK_TOKENS, QUERY_HEADS * HEAD_SIZE)
    blocks = lax.map(one_block, jnp.arange(N_CTX, dtype=jnp.int32))
    return blocks.reshape(SEQUENCE_TOKENS, QUERY_HEADS * HEAD_SIZE)
```

```python
import math

import jax
import jax.numpy as jnp
from jax import lax
from jax.experimental import pallas as pl
from jax.experimental.pallas import tpu as pltpu
from jax.sharding import PartitionSpec as P

BLOCK = 512
ROWS = 64
PEERS = 8
GROUP = 8
D = 128
STEPS = 4
N_CTX = 32
SCALE = 1.0 / math.sqrt(D)
LOG2E_SCALE = SCALE * math.log2(math.e)
BIG = -1e30
META = BLOCK + 4 * D
KV_ROWS = META + 16
MESH = pl.DeviceIdType.MESH
F32 = jnp.float32
BF16 = jnp.bfloat16


def iota(shape, dimension):
    return lax.broadcasted_iota(jnp.int32, shape, dimension)


def nt_dot(a, b):
    return lax.dot_general(a, b, (((1,), (1,)), ((), ())), preferred_element_type=F32)


def kernel(
    q_hbm, kc_hbm, vc_hbm, ke_hbm, ve_hbm, ids_hbm, out_ref,
    q_ref, kc_ref, vc_ref, ke_ref, ve_ref, ids_ref,
    kvs, kvr, kvr2, kvb, qb, aug_q, aug_k, s_buf,
    in_sem, kv_send, kv_recv, q_send, q_recv, a_send, a_recv, c_send, c_recv,
):
    c = lax.axis_index("ctx")
    h = lax.axis_index("head")
    core = lax.rem(c, 2)
    hy, hx = h // 2, lax.rem(h, 2)

    def to_peer(r):
        ry, rx = r // 2, r % 2
        return lax.rem(hy + ry, 4) * 2 + lax.rem(hx + rx, 2)

    sibling = c + 1 - 2 * core

    barrier = pltpu.get_barrier_semaphore()
    for r in range(1, PEERS):
        pl.semaphore_signal(barrier, inc=1, device_id=(c, to_peer(r)), device_id_type=MESH)
    pl.semaphore_signal(barrier, inc=1, device_id=(sibling, h), device_id_type=MESH)
    @pl.when(c >= 2)
    def _():
        for j in range(PEERS):
            pl.semaphore_signal(barrier, inc=1, device_id=(c - 2, j), device_id_type=MESH)

    @pl.when(c < N_CTX - 2)
    def _():
        for j in range(PEERS):
            pl.semaphore_signal(barrier, inc=1, device_id=(c + 2, j), device_id_type=MESH)

    @pl.when(c >= 4)
    def _():
        pl.semaphore_signal(barrier, inc=1, device_id=(c - 4, h), device_id_type=MESH)

    @pl.when(c < N_CTX - 4)
    def _():
        pl.semaphore_signal(barrier, inc=1, device_id=(c + 4, h), device_id_type=MESH)

    fetches = [
        pltpu.make_async_copy(source, target, in_sem.at[number])
        for number, (source, target) in enumerate(
            (
                (ke_hbm, ke_ref), (ve_hbm, ve_ref), (kc_hbm, kc_ref), (vc_hbm, vc_ref), (ids_hbm, ids_ref),
                (q_hbm, q_ref),
            )
        )
    ]
    for fetch in fetches:
        fetch.start()

    def q_columns(peer):
        return q_ref.at[:, pl.ds(pl.multiple_of(peer * GROUP * D, GROUP * D), GROUP * D)]

    own_q = pltpu.make_async_copy(q_columns(h), qb.at[h], in_sem.at[6])

    bits = iota((D, D), 0) & iota((D, D), 1)
    bits = bits ^ (bits >> 4)
    bits = bits ^ (bits >> 2)
    bits = bits ^ (bits >> 1)
    signs = (1 - 2 * (bits & 1)).astype(F32).astype(BF16)

    for fetch in fetches[:5]:
        fetch.wait()
    k_powers = jnp.exp2(ke_ref[...].astype(F32)).astype(BF16).astype(F32).T
    v_powers = jnp.exp2(ve_ref[...].astype(F32)).astype(BF16).astype(F32).T
    for j in range(PEERS):
        columns = slice(j * D, (j + 1) * D)
        kvs[j, :, 0:D] = (kc_ref[:, columns].astype(F32) * k_powers[:, j:j + 1]).astype(BF16)
        kvs[j, :, D:2 * D] = (vc_ref[:, columns].astype(F32) * v_powers[:, j:j + 1]).astype(BF16)

    ids = ids_ref[...]
    term = iota((D, BLOCK), 0)
    below = jnp.where(ids < term, 1.0, 0.0).astype(F32).astype(BF16)
    upto = jnp.where(ids <= term, 1.0, 0.0).astype(F32).astype(BF16)
    ones = jnp.ones((16, BLOCK), BF16)
    lo, hi = nt_dot(ones, below), nt_dot(ones, upto)
    lo_part, hi_part = jnp.floor(lo * (1.0 / 16)), jnp.floor(hi * (1.0 / 16))
    row = iota((16, D), 0)
    meta = jnp.where(
        row < 4, lo_part,
        jnp.where(row < 8, lo - 16 * lo_part, jnp.where(row < 12, hi_part, hi - 16 * hi_part)),
    )
    kvb[0, META:KV_ROWS] = meta.astype(BF16)

    pl.semaphore_wait(
        barrier,
        PEERS
        + PEERS * (c >= 2).astype(jnp.int32) + (c >= 4).astype(jnp.int32)
        + PEERS * (c < N_CTX - 2).astype(jnp.int32) + (c < N_CTX - 4).astype(jnp.int32),
    )

    my_rows = pl.ds(pl.multiple_of(h * ROWS, ROWS), ROWS)
    kv_copies = {}
    for r in range(1, PEERS):
        peer = to_peer(r)
        kv_copies[r] = pltpu.make_async_remote_copy(
            src_ref=kvs.at[peer], dst_ref=kvr.at[my_rows],
            send_sem=kv_send.at[r], recv_sem=kv_recv.at[r],
            device_id=(c, peer), device_id_type=MESH,
        )
        kv_copies[r].start()

    after2 = lax.rem(c + 2, N_CTX)
    a_copies = [
        pltpu.make_async_remote_copy(
            src_ref=kvs.at[j], dst_ref=kvr2.at[my_rows],
            send_sem=a_send.at[j], recv_sem=a_recv.at[h],
            device_id=(after2, j), device_id_type=MESH,
        )
        for j in range(PEERS)
    ]
    a_copies.append(
        pltpu.make_async_remote_copy(
            src_ref=kvb.at[0, META:KV_ROWS], dst_ref=kvb.at[2, META:KV_ROWS],
            send_sem=a_send.at[PEERS], recv_sem=a_recv.at[PEERS],
            device_id=(after2, h), device_id_type=MESH,
        )
    )

    @pl.when(c < N_CTX - 2)
    def _():
        for copy in a_copies:
            copy.start()

    def q_copy(r):
        peer = to_peer(r)
        return pltpu.make_async_remote_copy(
            src_ref=q_columns(peer), dst_ref=qb.at[h],
            send_sem=q_send.at[r], recv_sem=q_recv.at[h],
            device_id=(c, peer), device_id_type=MESH,
        )

    q_copies = {r: q_copy(r) for r in range(1, PEERS)}
    fetches[5].wait()
    own_q.start()
    for r in (2, 6, 4):
        q_copies[r].start()
    kvr[my_rows] = kvs[h]

    token = iota((BLOCK, D), 0).astype(F32)
    lane = iota((BLOCK, D), 1)
    inside = (token >= lo[0:1]) & (token < hi[0:1])
    diagonal = (lane >= D - ROWS) & (lax.rem(iota((BLOCK, D), 0), ROWS) == lane - (D - ROWS))
    aug_q[...] = jnp.where(inside | diagonal, 1.0, 0.0).astype(F32).astype(BF16)

    def key_spans(d):
        spans = kvb[d, META:KV_ROWS].astype(F32)
        first = spans[0:1] * 16 + spans[4:5]
        last = spans[8:9] * 16 + spans[12:13]
        member = (token >= first) & (token < last)
        aug_k[d] = jnp.where(member | (lane >= D - ROWS), 0.0, BIG).astype(F32).astype(BF16)

    for r in range(1, PEERS):
        kv_copies[r].wait_recv()

    def rotate(codes, slot):
        keys = jnp.dot(codes[:, 0:D], signs, preferred_element_type=F32) * SCALE
        kvb[slot, 0:BLOCK] = keys.astype(BF16)
        values = (nt_dot(signs, codes[:, D:2 * D]) * SCALE).astype(BF16)
        for part in range(4):
            kvb[slot, BLOCK + part * D:BLOCK + (part + 1) * D] = values[:, part * D:(part + 1) * D]

    def c_copy(source, slot, target):
        return pltpu.make_async_remote_copy(
            src_ref=kvb.at[source], dst_ref=kvb.at[slot],
            send_sem=c_send.at[slot], recv_sem=c_recv.at[slot],
            device_id=(target, h), device_id_type=MESH,
        )

    c_copies = {
        1: c_copy(2 * core, 1, sibling),
        3: c_copy(2 + 2 * core, 3, sibling),
        4: c_copy(0, 4, lax.rem(c + 4, N_CTX)),
    }
    rotate(kvr, 0)

    @pl.when(c < N_CTX - 4)
    def _():
        c_copies[4].start()

    @pl.when(core == 0)
    def _():
        c_copies[1].start()

    for r in (1, 3, 7, 5):
        q_copies[r].start()
    key_spans(0)

    @pl.when(c >= 2)
    def _():
        for j in range(PEERS):
            pltpu.make_async_remote_copy(
                src_ref=kvs.at[0], dst_ref=kvr2.at[j * ROWS:(j + 1) * ROWS],
                send_sem=a_send.at[0], recv_sem=a_recv.at[j],
                device_id=(after2, h), device_id_type=MESH,
            ).wait_recv()
        a_copies[PEERS].wait_recv()
        rotate(kvr2, 2)

    @pl.when(c < 2)
    def _():
        kvb[2] = jnp.zeros((KV_ROWS, D), BF16)

    @pl.when(c < 4)
    def _():
        kvb[4] = jnp.zeros((KV_ROWS, D), BF16)

    @pl.when(core == 0)
    def _():
        c_copies[3].start()

    @pl.when(core == 1)
    def _():
        c_copies[1].start()

    key_spans(2)

    @pl.when(c >= 4)
    def _():
        c_copies[4].wait_recv()

    @pl.when(core == 1)
    def _():
        c_copies[3].start()

    key_spans(4)
    c_copies[1].wait_recv()
    key_spans(1)
    c_copies[3].wait_recv()
    key_spans(3)

    half = BLOCK // 2

    def attend(p, first_keys, last_keys):
        extra = aug_q[pl.ds(pl.multiple_of(p * ROWS, ROWS), ROWS)]
        extra = jnp.concatenate([extra] * (GROUP // 2), axis=0)
        spans = [(0, first_keys)] + [(0, BLOCK)] * 3 + [(last_keys, BLOCK)]

        def queries_of(g):
            heads = [qb[p, :, i * D:(i + 1) * D] for i in range(g * GROUP // 2, (g + 1) * GROUP // 2)]
            return jnp.concatenate([jnp.concatenate(heads, axis=0), extra], axis=1)

        def pieces(d):
            start, stop = spans[d]
            return [(k, g) for g in range(2) for k in range(start, stop, half)]

        def score(d, k, g, top):
            extra_keys = aug_k[d, k:k + half]
            if d == 0:
                column = iota((half, D), 1)
                late = (iota((half, D), 0) + k - p * ROWS > column - (D - ROWS)) & (column >= D - ROWS)
                extra_keys = jnp.where(late, BIG, extra_keys.astype(F32)).astype(BF16)
            keys = jnp.concatenate([kvb[d, k:k + half], extra_keys], axis=1)
            scores = nt_dot(keys, queries_of(g))
            s_buf[d % 2, k:k + half, g * half:(g + 1) * half] = scores
            here = jnp.max(scores.reshape(half // 8, 8, half), axis=0)
            top[g] = here if top[g] is None else jnp.maximum(top[g], here)

        def values_of(d, k):
            parts = [kvb[d, BLOCK + part * D:BLOCK + (part + 1) * D] for part in range(k // D, (k + half) // D)]
            return jnp.concatenate(parts, axis=1)

        top = [None, None]
        for k, g in pieces(0):
            score(0, k, g, top)
        running, total, accum = [None, None], [None, None], [None, None]
        for d in range(STEPS + 1):
            next_top = [None, None]
            now = pieces(d)
            following = pieces(d + 1) if d < STEPS else []
            for slot in range(max(len(now), len(following))):
                if slot < len(following):
                    score(d + 1, *following[slot], next_top)
                if slot >= len(now):
                    continue
                k, g = now[slot]
                if top[g] is not None:
                    newmax = jnp.max(top[g], axis=0, keepdims=True)
                    if d:
                        newmax = jnp.maximum(running[g], newmax)
                        factor = jnp.exp2((running[g] - newmax) * LOG2E_SCALE)
                        total[g] = total[g] * factor
                        accum[g] = accum[g] * factor
                    running[g] = newmax
                    top[g] = None
                scores = s_buf[d % 2, k:k + half, g * half:(g + 1) * half]
                weights = jnp.exp2((scores - running[g]) * LOG2E_SCALE)
                sums = jnp.sum(weights.reshape(half // 8, 8, half), axis=0)
                product = jnp.dot(values_of(d, k), weights.astype(BF16), preferred_element_type=F32)
                total[g] = sums if total[g] is None else total[g] + sums
                accum[g] = product if accum[g] is None else accum[g] + product
            top = next_top
        for g in range(2):
            attended = accum[g] * (1.0 / jnp.sum(total[g], axis=0, keepdims=True))
            attended = attended.T.astype(BF16)
            rows = pl.ds(pl.multiple_of(p * ROWS, ROWS), ROWS)
            for i in range(GROUP // 2):
                column = (g * GROUP // 2 + i) * D
                out_ref[rows, column:column + D] = attended[i * ROWS:(i + 1) * ROWS]

    def body(i, carry):
        turn, rx = lax.rem(i, 4), i // 4
        ry = turn + (turn // 2) * (5 - 2 * turn)
        p = lax.rem(hy + 4 - ry, 4) * 2 + lax.rem(hx + rx, 2)

        @pl.when(i == 0)
        def _():
            own_q.wait()

        @pl.when(i > 0)
        def _():
            pltpu.make_async_remote_copy(
                src_ref=q_columns(h), dst_ref=qb.at[p],
                send_sem=q_send.at[0], recv_sem=q_recv.at[p],
                device_id=(c, lax.rem(h + 1, PEERS)), device_id_type=MESH,
            ).wait_recv()

        @pl.when(p < PEERS // 2)
        def _():
            attend(p, half, 0)

        @pl.when(p >= PEERS // 2)
        def _():
            attend(p, BLOCK, half)

        return carry

    lax.fori_loop(0, PEERS, body, 0)

    for r in range(1, PEERS):
        kv_copies[r].wait_send()
        q_copies[r].wait_send()
    for step in (1, 3):
        c_copies[step].wait_send()

    @pl.when(c < N_CTX - 2)
    def _():
        for copy in a_copies:
            copy.wait_send()

    @pl.when(c < N_CTX - 4)
    def _():
        c_copies[4].wait_send()


def per_device(queries, key_codes, value_codes, key_exponents, value_exponents, trace_ids):
    hbm = pl.BlockSpec(memory_space=pl.ANY)
    dma = pltpu.SemaphoreType.DMA
    return pl.pallas_call(
        kernel,
        out_shape=jax.ShapeDtypeStruct((BLOCK, GROUP * D), BF16),
        in_specs=[hbm] * 6,
        out_specs=pl.BlockSpec(memory_space=pltpu.VMEM),
        scratch_shapes=[
            pltpu.VMEM((ROWS, PEERS * GROUP * D), BF16),
            pltpu.VMEM((ROWS, PEERS * D), BF16),
            pltpu.VMEM((ROWS, PEERS * D), BF16),
            pltpu.VMEM((PEERS, ROWS), jnp.int32),
            pltpu.VMEM((PEERS, ROWS), jnp.int32),
            pltpu.VMEM((1, BLOCK), jnp.int32),
            pltpu.VMEM((PEERS, ROWS, 2 * D), BF16),
            pltpu.VMEM((BLOCK, 2 * D), BF16),
            pltpu.VMEM((BLOCK, 2 * D), BF16),
            pltpu.VMEM((STEPS + 1, KV_ROWS, D), BF16),
            pltpu.VMEM((PEERS, ROWS, GROUP * D), BF16),
            pltpu.VMEM((BLOCK, D), BF16),
            pltpu.VMEM((STEPS + 1, BLOCK, D), BF16),
            pltpu.VMEM((2, BLOCK, BLOCK), F32),
            dma((7,)), dma((PEERS,)), dma((PEERS,)), dma((PEERS,)), dma((PEERS,)),
            dma((PEERS + 1,)), dma((PEERS + 1,)), dma((STEPS + 1,)), dma((STEPS + 1,)),
        ],
        compiler_params=pltpu.CompilerParams(
            collective_id=0, has_side_effects=True, vmem_limit_bytes=62 * 1024 * 1024
        ),
        cost_estimate=pl.CostEstimate(flops=9_000_000_000, bytes_accessed=4_000_000, transcendentals=8_700_000),
    )(
        queries, key_codes, value_codes, key_exponents.T, value_exponents.T, trace_ids.reshape(1, BLOCK)
    )


def solution(mesh):
    placed = (
        P(("ctx", "head"), None),
        P(("ctx", "head"), None),
        P(("ctx", "head"), None),
        P(("ctx", "head"), None),
        P(("ctx", "head"), None),
        P("ctx"),
    )
    return jax.shard_map(
        per_device, mesh=mesh, in_specs=placed, out_specs=P("ctx", "head"), check_vma=False
    )
```

```python
import math

import jax
import jax.numpy as jnp
from jax import lax
from jax.experimental import pallas as pl
from jax.experimental.pallas import tpu as pltpu
from jax.sharding import PartitionSpec as P

BLOCK = 512
ROWS = 64
PEERS = 8
GROUP = 8
D = 128
STEPS = 4
N_CTX = 32
SCALE = 1.0 / math.sqrt(D)
LOG2E_SCALE = SCALE * math.log2(math.e)
BIG = -1e30
META = BLOCK + 4 * D
KV_ROWS = META + 16
MESH = pl.DeviceIdType.MESH
F32 = jnp.float32
BF16 = jnp.bfloat16


def iota(shape, dimension):
    return lax.broadcasted_iota(jnp.int32, shape, dimension)


def nt_dot(a, b):
    return lax.dot_general(a, b, (((1,), (1,)), ((), ())), preferred_element_type=F32)


def kernel(
    q_hbm, kc_hbm, vc_hbm, ke_hbm, ve_hbm, ids_hbm, out_ref,
    q_ref, kc_ref, vc_ref, ke_ref, ve_ref, ids_ref,
    kvs, kvr, kvr2, kvb, qb, aug_q, aug_k, s_buf, top_s, m_s, l_s, o_s,
    in_sem, kv_send, kv_recv, q_send, q_recv, a_send, a_recv, c_send, c_recv,
):
    c = lax.axis_index("ctx")
    h = lax.axis_index("head")
    core = lax.rem(c, 2)
    hy, hx = h // 2, lax.rem(h, 2)

    y_low = lax.rem(hy, 2)

    def partner(turn, n):
        base = lax.rem(hy - y_low + 2 * turn, 4)
        flip = lax.rem(turn + n, 2)
        y = base + y_low + flip * (1 - 2 * y_low)
        return y * 2 + lax.rem(hx + n // 2, 2)

    others = [(turn, n) for turn in range(2) for n in range(4)][1:]
    peers = {r: partner(*others[r - 1]) for r in range(1, PEERS)}

    sibling = c + 1 - 2 * core

    barrier = pltpu.get_barrier_semaphore()
    for r in range(1, PEERS):
        pl.semaphore_signal(barrier, inc=1, device_id=(c, peers[r]), device_id_type=MESH)
    pl.semaphore_signal(barrier, inc=1, device_id=(sibling, h), device_id_type=MESH)
    @pl.when(c >= 2)
    def _():
        for j in range(PEERS):
            pl.semaphore_signal(barrier, inc=1, device_id=(c - 2, j), device_id_type=MESH)

    @pl.when(c < N_CTX - 2)
    def _():
        for j in range(PEERS):
            pl.semaphore_signal(barrier, inc=1, device_id=(c + 2, j), device_id_type=MESH)

    @pl.when(c >= 4)
    def _():
        pl.semaphore_signal(barrier, inc=1, device_id=(c - 4, h), device_id_type=MESH)

    @pl.when(c < N_CTX - 4)
    def _():
        pl.semaphore_signal(barrier, inc=1, device_id=(c + 4, h), device_id_type=MESH)

    fetches = [
        pltpu.make_async_copy(source, target, in_sem.at[number])
        for number, (source, target) in enumerate(
            (
                (ke_hbm, ke_ref), (ve_hbm, ve_ref), (kc_hbm, kc_ref), (vc_hbm, vc_ref), (ids_hbm, ids_ref),
                (q_hbm, q_ref),
            )
        )
    ]
    for fetch in fetches:
        fetch.start()

    def q_columns(peer):
        return q_ref.at[:, pl.ds(pl.multiple_of(peer * GROUP * D, GROUP * D), GROUP * D)]

    own_q = pltpu.make_async_copy(q_columns(h), qb.at[h], in_sem.at[6])

    bits = iota((D, D), 0) & iota((D, D), 1)
    bits = bits ^ (bits >> 4)
    bits = bits ^ (bits >> 2)
    bits = bits ^ (bits >> 1)
    signs = (1 - 2 * (bits & 1)).astype(F32).astype(BF16)

    for fetch in fetches[:5]:
        fetch.wait()
    k_powers = jnp.exp2(ke_ref[...].astype(F32)).astype(BF16).astype(F32).T
    v_powers = jnp.exp2(ve_ref[...].astype(F32)).astype(BF16).astype(F32).T
    for j in range(PEERS):
        columns = slice(j * D, (j + 1) * D)
        kvs[j, :, 0:D] = (kc_ref[:, columns].astype(F32) * k_powers[:, j:j + 1]).astype(BF16)
        kvs[j, :, D:2 * D] = (vc_ref[:, columns].astype(F32) * v_powers[:, j:j + 1]).astype(BF16)

    ids = ids_ref[...]
    term = iota((D, BLOCK), 0)
    below = jnp.where(ids < term, 1.0, 0.0).astype(F32).astype(BF16)
    upto = jnp.where(ids <= term, 1.0, 0.0).astype(F32).astype(BF16)
    ones = jnp.ones((16, BLOCK), BF16)
    lo, hi = nt_dot(ones, below), nt_dot(ones, upto)
    lo_part, hi_part = jnp.floor(lo * (1.0 / 16)), jnp.floor(hi * (1.0 / 16))
    row = iota((16, D), 0)
    meta = jnp.where(
        row < 4, lo_part,
        jnp.where(row < 8, lo - 16 * lo_part, jnp.where(row < 12, hi_part, hi - 16 * hi_part)),
    )
    kvb[0, META:KV_ROWS] = meta.astype(BF16)

    pl.semaphore_wait(
        barrier,
        PEERS
        + PEERS * (c >= 2).astype(jnp.int32) + (c >= 4).astype(jnp.int32)
        + PEERS * (c < N_CTX - 2).astype(jnp.int32) + (c < N_CTX - 4).astype(jnp.int32),
    )

    my_rows = pl.ds(pl.multiple_of(h * ROWS, ROWS), ROWS)
    kv_copies = {}
    for r in range(1, PEERS):
        peer = peers[r]
        kv_copies[r] = pltpu.make_async_remote_copy(
            src_ref=kvs.at[peer], dst_ref=kvr.at[my_rows],
            send_sem=kv_send.at[r], recv_sem=kv_recv.at[r],
            device_id=(c, peer), device_id_type=MESH,
        )
        kv_copies[r].start()

    after2 = lax.rem(c + 2, N_CTX)
    a_copies = [
        pltpu.make_async_remote_copy(
            src_ref=kvs.at[j], dst_ref=kvr2.at[my_rows],
            send_sem=a_send.at[j], recv_sem=a_recv.at[h],
            device_id=(after2, j), device_id_type=MESH,
        )
        for j in range(PEERS)
    ]
    a_copies.append(
        pltpu.make_async_remote_copy(
            src_ref=kvb.at[0, META:KV_ROWS], dst_ref=kvb.at[2, META:KV_ROWS],
            send_sem=a_send.at[PEERS], recv_sem=a_recv.at[PEERS],
            device_id=(after2, h), device_id_type=MESH,
        )
    )

    @pl.when(c < N_CTX - 2)
    def _():
        for copy in a_copies:
            copy.start()

    def q_copy(r):
        peer = peers[r]
        return pltpu.make_async_remote_copy(
            src_ref=q_columns(peer), dst_ref=qb.at[h],
            send_sem=q_send.at[r], recv_sem=q_recv.at[h],
            device_id=(c, peer), device_id_type=MESH,
        )

    q_copies = {r: q_copy(r) for r in range(1, PEERS)}
    fetches[5].wait()
    own_q.start()
    for r in (1, 4, 5):
        q_copies[r].start()
    kvr[my_rows] = kvs[h]

    token = iota((BLOCK, D), 0).astype(F32)
    lane = iota((BLOCK, D), 1)
    inside = (token >= lo[0:1]) & (token < hi[0:1])
    diagonal = (lane >= D - ROWS) & (lax.rem(iota((BLOCK, D), 0), ROWS) == lane - (D - ROWS))
    aug_q[...] = jnp.where(inside | diagonal, 1.0, 0.0).astype(F32).astype(BF16)

    def key_spans(d):
        spans = kvb[d, META:KV_ROWS].astype(F32)
        first = spans[0:1] * 16 + spans[4:5]
        last = spans[8:9] * 16 + spans[12:13]
        member = (token >= first) & (token < last)
        aug_k[d] = jnp.where(member | (lane >= D - ROWS), 0.0, BIG).astype(F32).astype(BF16)

    for r in range(1, PEERS):
        kv_copies[r].wait_recv()

    def rotate(codes, slot):
        keys = jnp.dot(codes[:, 0:D], signs, preferred_element_type=F32) * SCALE
        kvb[slot, 0:BLOCK] = keys.astype(BF16)
        values = (nt_dot(signs, codes[:, D:2 * D]) * SCALE).astype(BF16)
        for part in range(4):
            kvb[slot, BLOCK + part * D:BLOCK + (part + 1) * D] = values[:, part * D:(part + 1) * D]

    def c_copy(source, slot, target):
        return pltpu.make_async_remote_copy(
            src_ref=kvb.at[source], dst_ref=kvb.at[slot],
            send_sem=c_send.at[slot], recv_sem=c_recv.at[slot],
            device_id=(target, h), device_id_type=MESH,
        )

    c_copies = {
        1: c_copy(2 * core, 1, sibling),
        3: c_copy(2 + 2 * core, 3, sibling),
        4: c_copy(0, 4, lax.rem(c + 4, N_CTX)),
    }
    rotate(kvr, 0)

    @pl.when(c < N_CTX - 4)
    def _():
        c_copies[4].start()

    @pl.when(core == 0)
    def _():
        c_copies[1].start()

    for r in (2, 3, 6, 7):
        q_copies[r].start()
    key_spans(0)

    @pl.when(c >= 2)
    def _():
        for j in range(PEERS):
            pltpu.make_async_remote_copy(
                src_ref=kvs.at[0], dst_ref=kvr2.at[j * ROWS:(j + 1) * ROWS],
                send_sem=a_send.at[0], recv_sem=a_recv.at[j],
                device_id=(after2, h), device_id_type=MESH,
            ).wait_recv()
        a_copies[PEERS].wait_recv()
        rotate(kvr2, 2)

    @pl.when(c < 2)
    def _():
        kvb[2] = jnp.zeros((KV_ROWS, D), BF16)

    @pl.when(c < 4)
    def _():
        kvb[4] = jnp.zeros((KV_ROWS, D), BF16)

    @pl.when(core == 0)
    def _():
        c_copies[3].start()

    @pl.when(core == 1)
    def _():
        c_copies[1].start()

    key_spans(2)
    c_copies[1].wait_recv()
    key_spans(1)

    def receive_farther_blocks():
        @pl.when(c >= 4)
        def _():
            c_copies[4].wait_recv()

        @pl.when(core == 1)
        def _():
            c_copies[3].start()

        key_spans(4)
        c_copies[3].wait_recv()
        key_spans(3)

    half = BLOCK // 2

    rows_of = [slice(0, half), slice(half, BLOCK)]

    def score(p, d, k, g, top, buffer):
        extra = aug_q[pl.ds(pl.multiple_of(p * ROWS, ROWS), ROWS)]
        extra = jnp.concatenate([extra] * (GROUP // 2), axis=0)
        heads = [qb[p, :, n * D:(n + 1) * D] for n in range(g * GROUP // 2, (g + 1) * GROUP // 2)]
        queries = jnp.concatenate([jnp.concatenate(heads, axis=0), extra], axis=1)
        extra_keys = aug_k[d, k:k + half]
        if d == 0:
            column = iota((half, D), 1)
            late = (iota((half, D), 0) + k - p * ROWS > column - (D - ROWS)) & (column >= D - ROWS)
            extra_keys = jnp.where(late, BIG, extra_keys.astype(F32)).astype(BF16)
        keys = jnp.concatenate([kvb[d, k:k + half], extra_keys], axis=1)
        scores = nt_dot(keys, queries)
        s_buf[buffer, k:k + half, rows_of[g]] = scores
        here = jnp.max(scores.reshape(half // 8, 8, half), axis=0)
        top[g] = here if top[g] is None else jnp.maximum(top[g], here)

    def values_of(d, k):
        parts = [kvb[d, BLOCK + part * D:BLOCK + (part + 1) * D] for part in range(k // D, (k + half) // D)]
        return jnp.concatenate(parts, axis=1)

    def pieces(span):
        return [(k, g) for g in range(2) for k in range(*span, half)]

    def attend(n, p, following, steps, spans, buffers):
        top = [top_s[:, rows_of[g]] for g in range(2)]
        if steps[0]:
            running = [m_s[n, :, rows_of[g]] for g in range(2)]
            total = [l_s[n, :, rows_of[g]] for g in range(2)]
            accum = [o_s[n, :, rows_of[g]] for g in range(2)]
        else:
            running, total, accum = [None, None], [None, None], [None, None]
        for place, d in enumerate(steps):
            next_top = [None, None]
            later = (p, steps[place + 1]) if d != steps[-1] else (following, steps[0])
            now, ahead = pieces(spans[d]), pieces(spans[later[1]])
            for slot in range(max(len(now), len(ahead))):
                if slot < len(ahead):
                    score(*later, *ahead[slot], next_top, buffers[later[1]])
                if slot >= len(now):
                    continue
                k, g = now[slot]
                if top[g] is not None:
                    newmax = jnp.max(top[g], axis=0, keepdims=True)
                    if d:
                        newmax = jnp.maximum(running[g], newmax)
                        factor = jnp.exp2((running[g] - newmax) * LOG2E_SCALE)
                        total[g] = total[g] * factor
                        accum[g] = accum[g] * factor
                    running[g] = newmax
                    top[g] = None
                scores = s_buf[buffers[d], k:k + half, rows_of[g]]
                weights = jnp.exp2((scores - running[g]) * LOG2E_SCALE)
                sums = jnp.sum(weights.reshape(half // 8, 8, half), axis=0)
                product = jnp.dot(values_of(d, k), weights.astype(BF16), preferred_element_type=F32)
                total[g] = sums if total[g] is None else total[g] + sums
                accum[g] = product if accum[g] is None else accum[g] + product
            top = next_top
        rows = pl.ds(pl.multiple_of(p * ROWS, ROWS), ROWS)
        for g in range(2):
            top_s[:, rows_of[g]] = top[g]
            if steps[-1] < STEPS:
                m_s[n, :, rows_of[g]], l_s[n, :, rows_of[g]], o_s[n, :, rows_of[g]] = running[g], total[g], accum[g]
                continue
            attended = accum[g] * (1.0 / jnp.sum(total[g], axis=0, keepdims=True))
            attended = attended.T.astype(BF16)
            for member in range(GROUP // 2):
                column = (g * GROUP // 2 + member) * D
                out_ref[rows, column:column + D] = attended[member * ROWS:(member + 1) * ROWS]

    def await_queries(turn, n):
        p = partner(turn, n)
        pltpu.make_async_remote_copy(
            src_ref=q_columns(h), dst_ref=qb.at[p],
            send_sem=q_send.at[0], recv_sem=q_recv.at[p],
            device_id=(c, lax.rem(h + 1, PEERS)), device_id_type=MESH,
        ).wait_recv()

    def four_chunks(turn, steps, spans, buffers):
        top = [None, None]
        for k, g in pieces(spans[steps[0]]):
            score(partner(turn, 0), steps[0], k, g, top, buffers[steps[0]])
        for g in range(2):
            top_s[:, rows_of[g]] = top[g]

        def body(n, carry):
            if not steps[0]:
                @pl.when(n < 3)
                def _():
                    await_queries(turn, n + 1)

            attend(n, partner(turn, n), partner(turn, jnp.minimum(n + 1, 3)), steps, spans, buffers)
            return carry

        lax.fori_loop(0, 4, body, 0)

    whole = (0, BLOCK)
    early = {0: (0, half), 1: whole, 2: whole, 3: whole, 4: whole}
    late = {0: whole, 1: whole, 2: whole, 3: whole, 4: (half, BLOCK)}
    own_early = hy < 2

    def either(first, *arguments):
        @pl.when(first)
        def _():
            four_chunks(*arguments[:2], early, arguments[2])

        @pl.when(jnp.logical_not(first))
        def _():
            four_chunks(*arguments[:2], late, arguments[2])

    own_q.wait()
    either(own_early, 0, (0, 1, 2), {0: 0, 1: 1, 2: 2})
    receive_farther_blocks()
    either(own_early, 0, (3, 4), {3: 0, 4: 1})
    await_queries(1, 0)
    either(jnp.logical_not(own_early), 1, (0, 1, 2, 3, 4), {0: 0, 1: 1, 2: 0, 3: 1, 4: 2})

    for r in range(1, PEERS):
        kv_copies[r].wait_send()
        q_copies[r].wait_send()
    for step in (1, 3):
        c_copies[step].wait_send()

    @pl.when(c < N_CTX - 2)
    def _():
        for copy in a_copies:
            copy.wait_send()

    @pl.when(c < N_CTX - 4)
    def _():
        c_copies[4].wait_send()


def per_device(queries, key_codes, value_codes, key_exponents, value_exponents, trace_ids):
    hbm = pl.BlockSpec(memory_space=pl.ANY)
    dma = pltpu.SemaphoreType.DMA
    return pl.pallas_call(
        kernel,
        out_shape=jax.ShapeDtypeStruct((BLOCK, GROUP * D), BF16),
        in_specs=[hbm] * 6,
        out_specs=pl.BlockSpec(memory_space=pltpu.VMEM),
        scratch_shapes=[
            pltpu.VMEM((ROWS, PEERS * GROUP * D), BF16),
            pltpu.VMEM((ROWS, PEERS * D), BF16),
            pltpu.VMEM((ROWS, PEERS * D), BF16),
            pltpu.VMEM((PEERS, ROWS), jnp.int32),
            pltpu.VMEM((PEERS, ROWS), jnp.int32),
            pltpu.VMEM((1, BLOCK), jnp.int32),
            pltpu.VMEM((PEERS, ROWS, 2 * D), BF16),
            pltpu.VMEM((BLOCK, 2 * D), BF16),
            pltpu.VMEM((BLOCK, 2 * D), BF16),
            pltpu.VMEM((STEPS + 1, KV_ROWS, D), BF16),
            pltpu.VMEM((PEERS, ROWS, GROUP * D), BF16),
            pltpu.VMEM((BLOCK, D), BF16),
            pltpu.VMEM((STEPS + 1, BLOCK, D), BF16),
            pltpu.VMEM((3, BLOCK, BLOCK), F32),
            pltpu.VMEM((8, BLOCK), F32),
            pltpu.VMEM((4, 1, BLOCK), F32),
            pltpu.VMEM((4, 8, BLOCK), F32),
            pltpu.VMEM((4, D, BLOCK), F32),
            dma((7,)), dma((PEERS,)), dma((PEERS,)), dma((PEERS,)), dma((PEERS,)),
            dma((PEERS + 1,)), dma((PEERS + 1,)), dma((STEPS + 1,)), dma((STEPS + 1,)),
        ],
        compiler_params=pltpu.CompilerParams(
            collective_id=0, has_side_effects=True, vmem_limit_bytes=62 * 1024 * 1024
        ),
        cost_estimate=pl.CostEstimate(flops=9_000_000_000, bytes_accessed=4_000_000, transcendentals=8_700_000),
    )(
        queries, key_codes, value_codes, key_exponents.T, value_exponents.T, trace_ids.reshape(1, BLOCK)
    )


def solution(mesh):
    placed = (
        P(("ctx", "head"), None),
        P(("ctx", "head"), None),
        P(("ctx", "head"), None),
        P(("ctx", "head"), None),
        P(("ctx", "head"), None),
        P("ctx"),
    )
    return jax.shard_map(
        per_device, mesh=mesh, in_specs=placed, out_specs=P("ctx", "head"), check_vma=False
    )
```

```python
import math

import jax
import jax.numpy as jnp
from jax import lax
from jax.experimental import pallas as pl
from jax.experimental.pallas import tpu as pltpu
from jax.sharding import PartitionSpec as P

BLOCK = 512
ROWS = 64
PEERS = 8
GROUP = 8
D = 128
STEPS = 4
N_CTX = 32
SCALE = 1.0 / math.sqrt(D)
LOG2E_SCALE = SCALE * math.log2(math.e)
BIG = -1e30
META = BLOCK + 4 * D
KV_ROWS = META + 16
MESH = pl.DeviceIdType.MESH
F32 = jnp.float32
BF16 = jnp.bfloat16


def iota(shape, dimension):
    return lax.broadcasted_iota(jnp.int32, shape, dimension)


def nt_dot(a, b):
    return lax.dot_general(a, b, (((1,), (1,)), ((), ())), preferred_element_type=F32)


def kernel(
    q_hbm, kc_hbm, vc_hbm, ke_hbm, ve_hbm, ids_hbm, out_ref,
    q_ref, kc_ref, vc_ref, ke_ref, ve_ref, ids_ref,
    kvs, kvr, kvr2, kvb, qb, qt, aug_q, aug_k, s_buf, top_s, m_s, l_s, o_s,
    in_sem, kv_send, kv_recv, q_send, q_recv, a_send, a_recv, c_send, c_recv,
):
    c = lax.axis_index("ctx")
    h = lax.axis_index("head")
    core = lax.rem(c, 2)
    hy, hx = h // 2, lax.rem(h, 2)

    y_low = lax.rem(hy, 2)

    def partner(turn, n):
        base = lax.rem(hy - y_low + 2 * turn, 4)
        flip = lax.rem(turn + n, 2)
        y = base + y_low + flip * (1 - 2 * y_low)
        return y * 2 + lax.rem(hx + n // 2, 2)

    others = [(turn, n) for turn in range(2) for n in range(4)][1:]
    peers = {r: partner(*others[r - 1]) for r in range(1, PEERS)}

    sibling = c + 1 - 2 * core

    barrier = pltpu.get_barrier_semaphore()
    for r in range(1, PEERS):
        pl.semaphore_signal(barrier, inc=1, device_id=(c, peers[r]), device_id_type=MESH)
    pl.semaphore_signal(barrier, inc=1, device_id=(sibling, h), device_id_type=MESH)
    @pl.when(c >= 2)
    def _():
        for j in range(PEERS):
            pl.semaphore_signal(barrier, inc=1, device_id=(c - 2, j), device_id_type=MESH)

    @pl.when(c < N_CTX - 2)
    def _():
        for j in range(PEERS):
            pl.semaphore_signal(barrier, inc=1, device_id=(c + 2, j), device_id_type=MESH)

    @pl.when(c >= 4)
    def _():
        pl.semaphore_signal(barrier, inc=1, device_id=(c - 4, h), device_id_type=MESH)

    @pl.when(c < N_CTX - 4)
    def _():
        pl.semaphore_signal(barrier, inc=1, device_id=(c + 4, h), device_id_type=MESH)

    fetches = [
        pltpu.make_async_copy(source, target, in_sem.at[number])
        for number, (source, target) in enumerate(
            (
                (ke_hbm, ke_ref), (ve_hbm, ve_ref), (kc_hbm, kc_ref), (vc_hbm, vc_ref), (ids_hbm, ids_ref),
                (q_hbm, q_ref),
            )
        )
    ]
    for fetch in fetches:
        fetch.start()

    def q_columns(peer):
        return q_ref.at[:, pl.ds(pl.multiple_of(peer * GROUP * D, GROUP * D), GROUP * D)]

    own_q = pltpu.make_async_copy(q_columns(h), qb.at[h], in_sem.at[6])

    bits = iota((D, D), 0) & iota((D, D), 1)
    bits = bits ^ (bits >> 4)
    bits = bits ^ (bits >> 2)
    bits = bits ^ (bits >> 1)
    signs = (1 - 2 * (bits & 1)).astype(F32).astype(BF16)

    for fetch in fetches[:5]:
        fetch.wait()
    k_powers = jnp.exp2(ke_ref[...].astype(F32)).astype(BF16).astype(F32).T
    v_powers = jnp.exp2(ve_ref[...].astype(F32)).astype(BF16).astype(F32).T
    for j in range(PEERS):
        columns = slice(j * D, (j + 1) * D)
        kvs[j, :, 0:D] = (kc_ref[:, columns].astype(F32) * k_powers[:, j:j + 1]).astype(BF16)
        kvs[j, :, D:2 * D] = (vc_ref[:, columns].astype(F32) * v_powers[:, j:j + 1]).astype(BF16)

    ids = ids_ref[...]
    term = iota((D, BLOCK), 0)
    below = jnp.where(ids < term, 1.0, 0.0).astype(F32).astype(BF16)
    upto = jnp.where(ids <= term, 1.0, 0.0).astype(F32).astype(BF16)
    ones = jnp.ones((16, BLOCK), BF16)
    lo, hi = nt_dot(ones, below), nt_dot(ones, upto)
    lo_part, hi_part = jnp.floor(lo * (1.0 / 16)), jnp.floor(hi * (1.0 / 16))
    row = iota((16, D), 0)
    meta = jnp.where(
        row < 4, lo_part,
        jnp.where(row < 8, lo - 16 * lo_part, jnp.where(row < 12, hi_part, hi - 16 * hi_part)),
    )
    kvb[0, META:KV_ROWS] = meta.astype(BF16)

    pl.semaphore_wait(
        barrier,
        PEERS
        + PEERS * (c >= 2).astype(jnp.int32) + (c >= 4).astype(jnp.int32)
        + PEERS * (c < N_CTX - 2).astype(jnp.int32) + (c < N_CTX - 4).astype(jnp.int32),
    )

    my_rows = pl.ds(pl.multiple_of(h * ROWS, ROWS), ROWS)
    kv_copies = {}
    for r in range(1, PEERS):
        peer = peers[r]
        kv_copies[r] = pltpu.make_async_remote_copy(
            src_ref=kvs.at[peer], dst_ref=kvr.at[my_rows],
            send_sem=kv_send.at[r], recv_sem=kv_recv.at[r],
            device_id=(c, peer), device_id_type=MESH,
        )
        kv_copies[r].start()

    after2 = lax.rem(c + 2, N_CTX)
    a_copies = [
        pltpu.make_async_remote_copy(
            src_ref=kvs.at[j], dst_ref=kvr2.at[my_rows],
            send_sem=a_send.at[j], recv_sem=a_recv.at[h],
            device_id=(after2, j), device_id_type=MESH,
        )
        for j in range(PEERS)
    ]
    a_copies.append(
        pltpu.make_async_remote_copy(
            src_ref=kvb.at[0, META:KV_ROWS], dst_ref=kvb.at[2, META:KV_ROWS],
            send_sem=a_send.at[PEERS], recv_sem=a_recv.at[PEERS],
            device_id=(after2, h), device_id_type=MESH,
        )
    )

    @pl.when(c < N_CTX - 2)
    def _():
        for copy in a_copies:
            copy.start()

    def q_copy(r):
        peer = peers[r]
        return pltpu.make_async_remote_copy(
            src_ref=q_columns(peer), dst_ref=qb.at[h],
            send_sem=q_send.at[r], recv_sem=q_recv.at[h],
            device_id=(c, peer), device_id_type=MESH,
        )

    q_copies = {r: q_copy(r) for r in range(1, PEERS)}
    fetches[5].wait()
    own_q.start()
    for r in (1, 2, 3, 4, 5):
        q_copies[r].start()
    kvr[my_rows] = kvs[h]

    token = iota((BLOCK, D), 0).astype(F32)
    lane = iota((BLOCK, D), 1)
    inside = (token >= lo[0:1]) & (token < hi[0:1])
    diagonal = (lane >= D - ROWS) & (lax.rem(iota((BLOCK, D), 0), ROWS) == lane - (D - ROWS))
    aug_q[...] = jnp.where(inside | diagonal, 1.0, 0.0).astype(F32).astype(BF16)

    def key_spans(d):
        spans = kvb[d, META:KV_ROWS].astype(F32)
        first = spans[0:1] * 16 + spans[4:5]
        last = spans[8:9] * 16 + spans[12:13]
        member = (token >= first) & (token < last)
        aug_k[d] = jnp.where(member | (lane >= D - ROWS), 0.0, BIG).astype(F32).astype(BF16)

    for r in range(1, PEERS):
        kv_copies[r].wait_recv()

    def rotate(codes, slot):
        keys = jnp.dot(codes[:, 0:D], signs, preferred_element_type=F32) * SCALE
        kvb[slot, 0:BLOCK] = keys.astype(BF16)
        values = (nt_dot(signs, codes[:, D:2 * D]) * SCALE).astype(BF16)
        for part in range(4):
            kvb[slot, BLOCK + part * D:BLOCK + (part + 1) * D] = values[:, part * D:(part + 1) * D]

    def c_copy(source, slot, target):
        return pltpu.make_async_remote_copy(
            src_ref=kvb.at[source], dst_ref=kvb.at[slot],
            send_sem=c_send.at[slot], recv_sem=c_recv.at[slot],
            device_id=(target, h), device_id_type=MESH,
        )

    c_copies = {
        1: c_copy(2 * core, 1, sibling),
        3: c_copy(2 + 2 * core, 3, sibling),
        4: c_copy(0, 4, lax.rem(c + 4, N_CTX)),
    }
    rotate(kvr, 0)

    @pl.when(c < N_CTX - 4)
    def _():
        c_copies[4].start()

    @pl.when(core == 0)
    def _():
        c_copies[1].start()

    for r in (6, 7):
        q_copies[r].start()
    key_spans(0)

    @pl.when(c >= 2)
    def _():
        for j in range(PEERS):
            pltpu.make_async_remote_copy(
                src_ref=kvs.at[0], dst_ref=kvr2.at[j * ROWS:(j + 1) * ROWS],
                send_sem=a_send.at[0], recv_sem=a_recv.at[j],
                device_id=(after2, h), device_id_type=MESH,
            ).wait_recv()
        a_copies[PEERS].wait_recv()
        rotate(kvr2, 2)

    @pl.when(c < 2)
    def _():
        kvb[2] = jnp.zeros((KV_ROWS, D), BF16)

    @pl.when(c < 4)
    def _():
        kvb[4] = jnp.zeros((KV_ROWS, D), BF16)

    @pl.when(core == 0)
    def _():
        c_copies[3].start()

    @pl.when(core == 1)
    def _():
        c_copies[1].start()

    key_spans(2)
    c_copies[1].wait_recv()
    key_spans(1)

    def pass_on_farther_block():
        @pl.when(c >= 4)
        def _():
            c_copies[4].wait_recv()

        c_copies[3].start()

    def receive_farther_blocks():
        @pl.when((core == 0) & (c >= 4))
        def _():
            c_copies[4].wait_recv()

        key_spans(4)
        c_copies[3].wait_recv()
        key_spans(3)

    half = BLOCK // 2

    rows_of = [slice(0, half), slice(half, BLOCK)]

    def turn_queries(n, p):
        for g in range(2):
            heads = [qb[p, :, m * D:(m + 1) * D] for m in range(g * GROUP // 2, (g + 1) * GROUP // 2)]
            qt[n, g] = jnp.concatenate(heads, axis=0).T
        extra = aug_q[pl.ds(pl.multiple_of(p * ROWS, ROWS), ROWS)]
        qt[n, 2] = jnp.concatenate([extra] * (GROUP // 2), axis=0).T

    def score(n, p, d, k, g, top, buffer):
        queries = jnp.concatenate([qt[n, g], qt[n, 2]], axis=0)
        extra_keys = aug_k[d, k:k + half]
        if d == 0:
            column = iota((half, D), 1)
            late = (iota((half, D), 0) + k - p * ROWS > column - (D - ROWS)) & (column >= D - ROWS)
            extra_keys = jnp.where(late, BIG, extra_keys.astype(F32)).astype(BF16)
        keys = jnp.concatenate([kvb[d, k:k + half], extra_keys], axis=1)
        scores = jnp.dot(keys, queries, preferred_element_type=F32)
        s_buf[buffer, k:k + half, rows_of[g]] = scores
        here = jnp.max(scores.reshape(half // 8, 8, half), axis=0)
        top[g] = here if top[g] is None else jnp.maximum(top[g], here)

    def values_of(d, k):
        parts = [kvb[d, BLOCK + part * D:BLOCK + (part + 1) * D] for part in range(k // D, (k + half) // D)]
        return jnp.concatenate(parts, axis=1)

    def pieces(span):
        return [(k, g) for g in range(2) for k in range(*span, half)]

    def attend(n, p, following, steps, spans, buffers):
        top = [top_s[:, rows_of[g]] for g in range(2)]
        if steps[0]:
            running = [m_s[n, :, rows_of[g]] for g in range(2)]
            total = [l_s[n, :, rows_of[g]] for g in range(2)]
            accum = [o_s[n, :, rows_of[g]] for g in range(2)]
        else:
            running, total, accum = [None, None], [None, None], [None, None]
        for place, d in enumerate(steps):
            next_top = [None, None]
            later = (n, p, steps[place + 1]) if d != steps[-1] else (*following, steps[0])
            now, ahead = pieces(spans[d]), pieces(spans[later[2]])
            for slot in range(max(len(now), len(ahead))):
                if slot < len(ahead):
                    score(*later, *ahead[slot], next_top, buffers[later[2]])
                if slot >= len(now):
                    continue
                k, g = now[slot]
                if top[g] is not None:
                    newmax = jnp.max(top[g], axis=0, keepdims=True)
                    if d:
                        newmax = jnp.maximum(running[g], newmax)
                        factor = jnp.exp2((running[g] - newmax) * LOG2E_SCALE)
                        total[g] = total[g] * factor
                        accum[g] = accum[g] * factor
                    running[g] = newmax
                    top[g] = None
                scores = s_buf[buffers[d], k:k + half, rows_of[g]]
                weights = jnp.exp2((scores - running[g]) * LOG2E_SCALE)
                sums = jnp.sum(weights.reshape(half // 8, 8, half), axis=0)
                product = jnp.dot(values_of(d, k), weights.astype(BF16), preferred_element_type=F32)
                total[g] = sums if total[g] is None else total[g] + sums
                accum[g] = product if accum[g] is None else accum[g] + product
            top = next_top
        rows = pl.ds(pl.multiple_of(p * ROWS, ROWS), ROWS)
        for g in range(2):
            top_s[:, rows_of[g]] = top[g]
            if steps[-1] < STEPS:
                m_s[n, :, rows_of[g]], l_s[n, :, rows_of[g]], o_s[n, :, rows_of[g]] = running[g], total[g], accum[g]
                continue
            attended = accum[g] * (1.0 / jnp.sum(total[g], axis=0, keepdims=True))
            attended = attended.T.astype(BF16)
            for member in range(GROUP // 2):
                column = (g * GROUP // 2 + member) * D
                out_ref[rows, column:column + D] = attended[member * ROWS:(member + 1) * ROWS]

    def await_queries(turn, n):
        p = partner(turn, n)
        pltpu.make_async_remote_copy(
            src_ref=q_columns(h), dst_ref=qb.at[p],
            send_sem=q_send.at[0], recv_sem=q_recv.at[p],
            device_id=(c, lax.rem(h + 1, PEERS)), device_id_type=MESH,
        ).wait_recv()

    def four_chunks(turn, steps, spans, buffers):
        if not steps[0]:
            turn_queries(0, partner(turn, 0))
        top = [None, None]
        for k, g in pieces(spans[steps[0]]):
            score(0, partner(turn, 0), steps[0], k, g, top, buffers[steps[0]])
        for g in range(2):
            top_s[:, rows_of[g]] = top[g]

        def body(n, carry):
            if steps == (0, 1, 2):
                @pl.when((n == 2) & (core == 1))
                def _():
                    pass_on_farther_block()

            if not steps[0]:
                @pl.when(n < 3)
                def _():
                    await_queries(turn, n + 1)
                    turn_queries(n + 1, partner(turn, n + 1))

            after = jnp.minimum(n + 1, 3)
            attend(n, partner(turn, n), (after, partner(turn, after)), steps, spans, buffers)
            return carry

        lax.fori_loop(0, 4, body, 0)

    whole = (0, BLOCK)
    early = {0: (0, half), 1: whole, 2: whole, 3: whole, 4: whole}
    late = {0: whole, 1: whole, 2: whole, 3: whole, 4: (half, BLOCK)}
    own_early = hy < 2

    def either(first, *arguments):
        @pl.when(first)
        def _():
            four_chunks(*arguments[:2], early, arguments[2])

        @pl.when(jnp.logical_not(first))
        def _():
            four_chunks(*arguments[:2], late, arguments[2])

    own_q.wait()
    either(own_early, 0, (0, 1, 2), {0: 0, 1: 1, 2: 2})
    receive_farther_blocks()
    either(own_early, 0, (3, 4), {3: 0, 4: 1})
    await_queries(1, 0)
    either(jnp.logical_not(own_early), 1, (0, 1, 2, 3, 4), {0: 0, 1: 1, 2: 0, 3: 1, 4: 2})

    for r in range(1, PEERS):
        kv_copies[r].wait_send()
        q_copies[r].wait_send()
    for step in (1, 3):
        c_copies[step].wait_send()

    @pl.when(c < N_CTX - 2)
    def _():
        for copy in a_copies:
            copy.wait_send()

    @pl.when(c < N_CTX - 4)
    def _():
        c_copies[4].wait_send()


def per_device(queries, key_codes, value_codes, key_exponents, value_exponents, trace_ids):
    hbm = pl.BlockSpec(memory_space=pl.ANY)
    dma = pltpu.SemaphoreType.DMA
    return pl.pallas_call(
        kernel,
        out_shape=jax.ShapeDtypeStruct((BLOCK, GROUP * D), BF16),
        in_specs=[hbm] * 6,
        out_specs=pl.BlockSpec(memory_space=pltpu.VMEM),
        scratch_shapes=[
            pltpu.VMEM((ROWS, PEERS * GROUP * D), BF16),
            pltpu.VMEM((ROWS, PEERS * D), BF16),
            pltpu.VMEM((ROWS, PEERS * D), BF16),
            pltpu.VMEM((PEERS, ROWS), jnp.int32),
            pltpu.VMEM((PEERS, ROWS), jnp.int32),
            pltpu.VMEM((1, BLOCK), jnp.int32),
            pltpu.VMEM((PEERS, ROWS, 2 * D), BF16),
            pltpu.VMEM((BLOCK, 2 * D), BF16),
            pltpu.VMEM((BLOCK, 2 * D), BF16),
            pltpu.VMEM((STEPS + 1, KV_ROWS, D), BF16),
            pltpu.VMEM((PEERS, ROWS, GROUP * D), BF16),
            pltpu.VMEM((4, 3, D, BLOCK // 2), BF16),
            pltpu.VMEM((BLOCK, D), BF16),
            pltpu.VMEM((STEPS + 1, BLOCK, D), BF16),
            pltpu.VMEM((3, BLOCK, BLOCK), F32),
            pltpu.VMEM((8, BLOCK), F32),
            pltpu.VMEM((4, 1, BLOCK), F32),
            pltpu.VMEM((4, 8, BLOCK), F32),
            pltpu.VMEM((4, D, BLOCK), F32),
            dma((7,)), dma((PEERS,)), dma((PEERS,)), dma((PEERS,)), dma((PEERS,)),
            dma((PEERS + 1,)), dma((PEERS + 1,)), dma((STEPS + 1,)), dma((STEPS + 1,)),
        ],
        compiler_params=pltpu.CompilerParams(
            collective_id=0, has_side_effects=True, vmem_limit_bytes=62 * 1024 * 1024
        ),
        cost_estimate=pl.CostEstimate(flops=9_000_000_000, bytes_accessed=4_000_000, transcendentals=8_700_000),
    )(
        queries, key_codes, value_codes, key_exponents.T, value_exponents.T, trace_ids.reshape(1, BLOCK)
    )


def solution(mesh):
    placed = (
        P(("ctx", "head"), None),
        P(("ctx", "head"), None),
        P(("ctx", "head"), None),
        P(("ctx", "head"), None),
        P(("ctx", "head"), None),
        P("ctx"),
    )
    return jax.shard_map(
        per_device, mesh=mesh, in_specs=placed, out_specs=P("ctx", "head"), check_vma=False
    )
```

```python
import math

import jax
import jax.numpy as jnp
from jax import lax
from jax.experimental import pallas as pl
from jax.experimental.pallas import tpu as pltpu
from jax.sharding import PartitionSpec as P

BLOCK = 512
ROWS = 64
PEERS = 8
GROUP = 8
D = 128
STEPS = 4
N_CTX = 32
SCALE = 1.0 / math.sqrt(D)
LOG2E_SCALE = SCALE * math.log2(math.e)
BIG = -1e30
META = BLOCK + 4 * D
KV_ROWS = META + 16
MESH = pl.DeviceIdType.MESH
F32 = jnp.float32
BF16 = jnp.bfloat16


def iota(shape, dimension):
    return lax.broadcasted_iota(jnp.int32, shape, dimension)


def nt_dot(a, b):
    return lax.dot_general(a, b, (((1,), (1,)), ((), ())), preferred_element_type=F32)


def kernel(
    q_hbm, kc_hbm, vc_hbm, ke_hbm, ve_hbm, ids_hbm, out_hbm,
    q_ref, kc_ref, vc_ref, ke_ref, ve_ref, ids_ref,
    kvs, kvr, kvr2, kvb, qb, qt, aug_q, aug_k, s_buf, top_s, m_s, l_s, o_s, ob,
    in_sem, kv_send, kv_recv, q_send, q_recv, a_send, a_recv, c_send, c_recv, out_sem,
):
    c = lax.axis_index("ctx")
    h = lax.axis_index("head")
    core = lax.rem(c, 2)
    hy, hx = h // 2, lax.rem(h, 2)

    y_low = lax.rem(hy, 2)

    def partner(turn, n):
        base = lax.rem(hy - y_low + 2 * turn, 4)
        flip = lax.rem(turn + n, 2)
        y = base + y_low + flip * (1 - 2 * y_low)
        return y * 2 + lax.rem(hx + n // 2, 2)

    others = [(turn, n) for turn in range(2) for n in range(4)][1:]
    peers = {r: partner(*others[r - 1]) for r in range(1, PEERS)}

    sibling = c + 1 - 2 * core

    barrier = pltpu.get_barrier_semaphore()
    for r in range(1, PEERS):
        pl.semaphore_signal(barrier, inc=1, device_id=(c, peers[r]), device_id_type=MESH)
    pl.semaphore_signal(barrier, inc=1, device_id=(sibling, h), device_id_type=MESH)
    @pl.when(c >= 2)
    def _():
        for j in range(PEERS):
            pl.semaphore_signal(barrier, inc=1, device_id=(c - 2, j), device_id_type=MESH)

    @pl.when(c < N_CTX - 2)
    def _():
        for j in range(PEERS):
            pl.semaphore_signal(barrier, inc=1, device_id=(c + 2, j), device_id_type=MESH)

    @pl.when(c >= 4)
    def _():
        pl.semaphore_signal(barrier, inc=1, device_id=(c - 4, h), device_id_type=MESH)

    @pl.when(c < N_CTX - 4)
    def _():
        pl.semaphore_signal(barrier, inc=1, device_id=(c + 4, h), device_id_type=MESH)

    fetches = [
        pltpu.make_async_copy(source, target, in_sem.at[number])
        for number, (source, target) in enumerate(
            (
                (ke_hbm, ke_ref), (ve_hbm, ve_ref), (kc_hbm, kc_ref), (vc_hbm, vc_ref), (ids_hbm, ids_ref),
                (q_hbm, q_ref),
            )
        )
    ]
    for fetch in fetches:
        fetch.start()

    def q_columns(peer):
        return q_ref.at[:, pl.ds(pl.multiple_of(peer * GROUP * D, GROUP * D), GROUP * D)]

    own_q = pltpu.make_async_copy(q_columns(h), qb.at[h], in_sem.at[6])

    bits = iota((D, D), 0) & iota((D, D), 1)
    bits = bits ^ (bits >> 4)
    bits = bits ^ (bits >> 2)
    bits = bits ^ (bits >> 1)
    signs = (1 - 2 * (bits & 1)).astype(F32).astype(BF16)

    for fetch in fetches[:5]:
        fetch.wait()
    k_powers = jnp.exp2(ke_ref[...].astype(F32)).astype(BF16).astype(F32).T
    v_powers = jnp.exp2(ve_ref[...].astype(F32)).astype(BF16).astype(F32).T
    for j in range(PEERS):
        columns = slice(j * D, (j + 1) * D)
        kvs[j, :, 0:D] = (kc_ref[:, columns].astype(F32) * k_powers[:, j:j + 1]).astype(BF16)
        kvs[j, :, D:2 * D] = (vc_ref[:, columns].astype(F32) * v_powers[:, j:j + 1]).astype(BF16)

    ids = ids_ref[...]
    term = iota((D, BLOCK), 0)
    below = jnp.where(ids < term, 1.0, 0.0).astype(F32).astype(BF16)
    upto = jnp.where(ids <= term, 1.0, 0.0).astype(F32).astype(BF16)
    ones = jnp.ones((16, BLOCK), BF16)
    lo, hi = nt_dot(ones, below), nt_dot(ones, upto)
    lo_part, hi_part = jnp.floor(lo * (1.0 / 16)), jnp.floor(hi * (1.0 / 16))
    row = iota((16, D), 0)
    meta = jnp.where(
        row < 4, lo_part,
        jnp.where(row < 8, lo - 16 * lo_part, jnp.where(row < 12, hi_part, hi - 16 * hi_part)),
    )
    kvb[0, META:KV_ROWS] = meta.astype(BF16)

    pl.semaphore_wait(
        barrier,
        PEERS
        + PEERS * (c >= 2).astype(jnp.int32) + (c >= 4).astype(jnp.int32)
        + PEERS * (c < N_CTX - 2).astype(jnp.int32) + (c < N_CTX - 4).astype(jnp.int32),
    )

    my_rows = pl.ds(pl.multiple_of(h * ROWS, ROWS), ROWS)
    kv_copies = {}
    for r in range(1, PEERS):
        peer = peers[r]
        kv_copies[r] = pltpu.make_async_remote_copy(
            src_ref=kvs.at[peer], dst_ref=kvr.at[my_rows],
            send_sem=kv_send.at[r], recv_sem=kv_recv.at[r],
            device_id=(c, peer), device_id_type=MESH,
        )
        kv_copies[r].start()

    after2 = lax.rem(c + 2, N_CTX)
    a_copies = [
        pltpu.make_async_remote_copy(
            src_ref=kvs.at[j], dst_ref=kvr2.at[my_rows],
            send_sem=a_send.at[j], recv_sem=a_recv.at[h],
            device_id=(after2, j), device_id_type=MESH,
        )
        for j in range(PEERS)
    ]
    a_copies.append(
        pltpu.make_async_remote_copy(
            src_ref=kvb.at[0, META:KV_ROWS], dst_ref=kvb.at[2, META:KV_ROWS],
            send_sem=a_send.at[PEERS], recv_sem=a_recv.at[PEERS],
            device_id=(after2, h), device_id_type=MESH,
        )
    )

    @pl.when(c < N_CTX - 2)
    def _():
        for copy in a_copies:
            copy.start()

    def q_copy(r):
        peer = peers[r]
        return pltpu.make_async_remote_copy(
            src_ref=q_columns(peer), dst_ref=qb.at[h],
            send_sem=q_send.at[r], recv_sem=q_recv.at[h],
            device_id=(c, peer), device_id_type=MESH,
        )

    q_copies = {r: q_copy(r) for r in range(1, PEERS)}
    fetches[5].wait()
    own_q.start()
    for r in (1, 2, 3, 4, 5):
        q_copies[r].start()
    kvr[my_rows] = kvs[h]

    token = iota((BLOCK, D), 0).astype(F32)
    lane = iota((BLOCK, D), 1)
    inside = (token >= lo[0:1]) & (token < hi[0:1])
    diagonal = (lane >= D - ROWS) & (lax.rem(iota((BLOCK, D), 0), ROWS) == lane - (D - ROWS))
    aug_q[...] = jnp.where(inside | diagonal, 1.0, 0.0).astype(F32).astype(BF16)

    def key_spans(d):
        spans = kvb[d, META:KV_ROWS].astype(F32)
        first = spans[0:1] * 16 + spans[4:5]
        last = spans[8:9] * 16 + spans[12:13]
        member = (token >= first) & (token < last)
        aug_k[d] = jnp.where(member | (lane >= D - ROWS), 0.0, BIG).astype(F32).astype(BF16)

    for r in range(1, PEERS):
        kv_copies[r].wait_recv()

    def rotate(codes, slot):
        keys = jnp.dot(codes[:, 0:D], signs, preferred_element_type=F32) * SCALE
        kvb[slot, 0:BLOCK] = keys.astype(BF16)
        values = (nt_dot(signs, codes[:, D:2 * D]) * SCALE).astype(BF16)
        for part in range(4):
            kvb[slot, BLOCK + part * D:BLOCK + (part + 1) * D] = values[:, part * D:(part + 1) * D]

    def c_copy(source, slot, target):
        return pltpu.make_async_remote_copy(
            src_ref=kvb.at[source], dst_ref=kvb.at[slot],
            send_sem=c_send.at[slot], recv_sem=c_recv.at[slot],
            device_id=(target, h), device_id_type=MESH,
        )

    c_copies = {
        1: c_copy(2 * core, 1, sibling),
        3: c_copy(2 + 2 * core, 3, sibling),
        4: c_copy(0, 4, lax.rem(c + 4, N_CTX)),
    }
    rotate(kvr, 0)

    @pl.when(c < N_CTX - 4)
    def _():
        c_copies[4].start()

    @pl.when(core == 0)
    def _():
        c_copies[1].start()

    for r in (6, 7):
        q_copies[r].start()
    key_spans(0)

    @pl.when(c >= 2)
    def _():
        for j in range(PEERS):
            pltpu.make_async_remote_copy(
                src_ref=kvs.at[0], dst_ref=kvr2.at[j * ROWS:(j + 1) * ROWS],
                send_sem=a_send.at[0], recv_sem=a_recv.at[j],
                device_id=(after2, h), device_id_type=MESH,
            ).wait_recv()
        a_copies[PEERS].wait_recv()
        rotate(kvr2, 2)

    @pl.when(c < 2)
    def _():
        kvb[2] = jnp.zeros((KV_ROWS, D), BF16)

    @pl.when(c < 4)
    def _():
        kvb[4] = jnp.zeros((KV_ROWS, D), BF16)

    @pl.when(core == 0)
    def _():
        c_copies[3].start()

    @pl.when(core == 1)
    def _():
        c_copies[1].start()

    key_spans(2)
    c_copies[1].wait_recv()
    key_spans(1)

    def pass_on_farther_block():
        @pl.when(c >= 4)
        def _():
            c_copies[4].wait_recv()

        c_copies[3].start()

    def receive_farther_blocks():
        @pl.when((core == 0) & (c >= 4))
        def _():
            c_copies[4].wait_recv()

        key_spans(4)
        c_copies[3].wait_recv()
        key_spans(3)

    half = BLOCK // 2

    def turn_queries(n, p):
        qt[n, 0:D] = jnp.concatenate([qb[p, :, m * D:(m + 1) * D] for m in range(GROUP)], axis=0).T
        extra = aug_q[pl.ds(pl.multiple_of(p * ROWS, ROWS), ROWS)]
        extra = jnp.concatenate([extra] * 2, axis=0).T
        qt[n, D:2 * D] = jnp.concatenate([extra] * (GROUP // 2), axis=1)

    def score(n, p, d, k, top, buffer):
        extra_keys = aug_k[d, k:k + half]
        if d == 0:
            column = iota((half, D), 1)
            late = (iota((half, D), 0) + k - p * ROWS > column - (D - ROWS)) & (column >= D - ROWS)
            extra_keys = jnp.where(late, BIG, extra_keys.astype(F32)).astype(BF16)
        keys = jnp.concatenate([kvb[d, k:k + half], extra_keys], axis=1)
        scores = jnp.dot(keys, qt[n], preferred_element_type=F32)
        s_buf[buffer, k:k + half] = scores
        here = jnp.max(scores.reshape(half // 8, 8, BLOCK), axis=0)
        return here if top is None else jnp.maximum(top, here)

    def values_of(d, k):
        parts = [kvb[d, BLOCK + part * D:BLOCK + (part + 1) * D] for part in range(k // D, (k + half) // D)]
        return jnp.concatenate(parts, axis=1)

    def out_copy(p):
        rows = pl.ds(pl.multiple_of(p * ROWS, ROWS), ROWS)
        return pltpu.make_async_copy(ob.at[p], out_hbm.at[rows], out_sem.at[p])

    def attend(n, p, following, steps, spans, buffers):
        top = top_s[...]
        running, total, accum = (m_s[n], l_s[n], o_s[n]) if steps[0] else (None, None, None)
        for place, d in enumerate(steps):
            next_top = None
            later = (n, p, steps[place + 1]) if d != steps[-1] else (*following, steps[0])
            now, ahead = list(range(*spans[d], half)), list(range(*spans[later[2]], half))
            newmax = jnp.max(top, axis=0, keepdims=True)
            if d:
                newmax = jnp.maximum(running, newmax)
                factor = jnp.exp2((running - newmax) * LOG2E_SCALE)
                total = total * factor
                accum = accum * factor
            running = newmax
            for slot in range(max(len(now), len(ahead))):
                if slot < len(ahead):
                    next_top = score(*later, ahead[slot], next_top, buffers[later[2]])
                if slot >= len(now):
                    continue
                k = now[slot]
                weights = jnp.exp2((s_buf[buffers[d], k:k + half] - running) * LOG2E_SCALE)
                sums = jnp.sum(weights.reshape(half // 8, 8, BLOCK), axis=0)
                product = jnp.dot(values_of(d, k), weights.astype(BF16), preferred_element_type=F32)
                total = sums if total is None else total + sums
                accum = product if accum is None else accum + product
            top = next_top
        top_s[...] = top
        if steps[-1] < STEPS:
            m_s[n], l_s[n], o_s[n] = running, total, accum
            return
        attended = accum * (1.0 / jnp.sum(total, axis=0, keepdims=True))
        attended = attended.T.astype(BF16)
        for member in range(GROUP):
            ob[p, :, member * D:(member + 1) * D] = attended[member * ROWS:(member + 1) * ROWS]
        out_copy(p).start()

    def await_queries(turn, n):
        p = partner(turn, n)
        pltpu.make_async_remote_copy(
            src_ref=q_columns(h), dst_ref=qb.at[p],
            send_sem=q_send.at[0], recv_sem=q_recv.at[p],
            device_id=(c, lax.rem(h + 1, PEERS)), device_id_type=MESH,
        ).wait_recv()

    def four_chunks(turn, steps, spans, buffers):
        if not steps[0]:
            turn_queries(0, partner(turn, 0))
        top = None
        for k in range(*spans[steps[0]], half):
            top = score(0, partner(turn, 0), steps[0], k, top, buffers[steps[0]])
        top_s[...] = top

        def body(n, carry):
            if steps == (0, 1, 2):
                @pl.when((n == 2) & (core == 1))
                def _():
                    pass_on_farther_block()

            if not steps[0]:
                @pl.when(n < 3)
                def _():
                    await_queries(turn, n + 1)
                    turn_queries(n + 1, partner(turn, n + 1))

            after = jnp.minimum(n + 1, 3)
            attend(n, partner(turn, n), (after, partner(turn, after)), steps, spans, buffers)
            return carry

        lax.fori_loop(0, 4, body, 0)

    whole = (0, BLOCK)
    early = {0: (0, half), 1: whole, 2: whole, 3: whole, 4: whole}
    late = {0: whole, 1: whole, 2: whole, 3: whole, 4: (half, BLOCK)}
    own_early = hy < 2

    def either(first, *arguments):
        @pl.when(first)
        def _():
            four_chunks(*arguments[:2], early, arguments[2])

        @pl.when(jnp.logical_not(first))
        def _():
            four_chunks(*arguments[:2], late, arguments[2])

    own_q.wait()
    either(own_early, 0, (0, 1, 2), {0: 0, 1: 1, 2: 2})
    receive_farther_blocks()
    either(own_early, 0, (3, 4), {3: 0, 4: 1})
    await_queries(1, 0)
    either(jnp.logical_not(own_early), 1, (0, 1, 2, 3, 4), {0: 0, 1: 1, 2: 0, 3: 1, 4: 2})

    for p in range(PEERS):
        out_copy(p).wait()
    for r in range(1, PEERS):
        kv_copies[r].wait_send()
        q_copies[r].wait_send()
    for step in (1, 3):
        c_copies[step].wait_send()

    @pl.when(c < N_CTX - 2)
    def _():
        for copy in a_copies:
            copy.wait_send()

    @pl.when(c < N_CTX - 4)
    def _():
        c_copies[4].wait_send()


def per_device(queries, key_codes, value_codes, key_exponents, value_exponents, trace_ids):
    hbm = pl.BlockSpec(memory_space=pl.ANY)
    dma = pltpu.SemaphoreType.DMA
    return pl.pallas_call(
        kernel,
        out_shape=jax.ShapeDtypeStruct((BLOCK, GROUP * D), BF16),
        in_specs=[hbm] * 6,
        out_specs=hbm,
        scratch_shapes=[
            pltpu.VMEM((ROWS, PEERS * GROUP * D), BF16),
            pltpu.VMEM((ROWS, PEERS * D), BF16),
            pltpu.VMEM((ROWS, PEERS * D), BF16),
            pltpu.VMEM((PEERS, ROWS), jnp.int32),
            pltpu.VMEM((PEERS, ROWS), jnp.int32),
            pltpu.VMEM((1, BLOCK), jnp.int32),
            pltpu.VMEM((PEERS, ROWS, 2 * D), BF16),
            pltpu.VMEM((BLOCK, 2 * D), BF16),
            pltpu.VMEM((BLOCK, 2 * D), BF16),
            pltpu.VMEM((STEPS + 1, KV_ROWS, D), BF16),
            pltpu.VMEM((PEERS, ROWS, GROUP * D), BF16),
            pltpu.VMEM((4, 2 * D, BLOCK), BF16),
            pltpu.VMEM((BLOCK, D), BF16),
            pltpu.VMEM((STEPS + 1, BLOCK, D), BF16),
            pltpu.VMEM((3, BLOCK, BLOCK), F32),
            pltpu.VMEM((8, BLOCK), F32),
            pltpu.VMEM((4, 1, BLOCK), F32),
            pltpu.VMEM((4, 8, BLOCK), F32),
            pltpu.VMEM((4, D, BLOCK), F32),
            pltpu.VMEM((PEERS, ROWS, GROUP * D), BF16),
            dma((7,)), dma((PEERS,)), dma((PEERS,)), dma((PEERS,)), dma((PEERS,)),
            dma((PEERS + 1,)), dma((PEERS + 1,)), dma((STEPS + 1,)), dma((STEPS + 1,)), dma((PEERS,)),
        ],
        compiler_params=pltpu.CompilerParams(
            collective_id=0, has_side_effects=True, vmem_limit_bytes=62 * 1024 * 1024
        ),
        cost_estimate=pl.CostEstimate(flops=9_000_000_000, bytes_accessed=4_000_000, transcendentals=8_700_000),
    )(
        queries, key_codes, value_codes, key_exponents.T, value_exponents.T, trace_ids.reshape(1, BLOCK)
    )


def solution(mesh):
    placed = (
        P(("ctx", "head"), None),
        P(("ctx", "head"), None),
        P(("ctx", "head"), None),
        P(("ctx", "head"), None),
        P(("ctx", "head"), None),
        P("ctx"),
    )
    return jax.shard_map(
        per_device, mesh=mesh, in_specs=placed, out_specs=P("ctx", "head"), check_vma=False
    )
```

```python
import math

import jax
import jax.numpy as jnp
from jax import lax
from jax.experimental import pallas as pl
from jax.experimental.pallas import tpu as pltpu
from jax.sharding import PartitionSpec as P

BLOCK = 512
ROWS = 64
PEERS = 8
GROUP = 8
D = 128
STEPS = 4
N_CTX = 32
SCALE = 1.0 / math.sqrt(D)
LOG2E_SCALE = SCALE * math.log2(math.e)
BIG = -1e30
META = BLOCK + 4 * D
KV_ROWS = META + 16
MESH = pl.DeviceIdType.MESH
F32 = jnp.float32
BF16 = jnp.bfloat16


def iota(shape, dimension):
    return lax.broadcasted_iota(jnp.int32, shape, dimension)


def nt_dot(a, b):
    return lax.dot_general(a, b, (((1,), (1,)), ((), ())), preferred_element_type=F32)


def kernel(
    q_hbm, kc_hbm, vc_hbm, ke_hbm, ve_hbm, ids_hbm, out_hbm,
    q_ref, kc_ref, vc_ref, ke_ref, ve_ref, ids_ref,
    kvs, kvr, kvr2, kvb, qb, qt, aug_q, aug_k, s_buf, top_s, m_s, l_s, o_s, ob,
    in_sem, kv_send, kv_recv, q_send, q_recv, a_send, a_recv, c_send, c_recv, out_sem,
):
    c = lax.axis_index("ctx")
    h = lax.axis_index("head")
    core = lax.rem(c, 2)
    hy, hx = h // 2, lax.rem(h, 2)

    y_low = lax.rem(hy, 2)

    def partner(turn, n):
        base = lax.rem(hy - y_low + 2 * turn, 4)
        flip = lax.rem(turn + n, 2)
        y = base + y_low + flip * (1 - 2 * y_low)
        return y * 2 + lax.rem(hx + n // 2, 2)

    others = [(turn, n) for turn in range(2) for n in range(4)][1:]
    peers = {r: partner(*others[r - 1]) for r in range(1, PEERS)}

    sibling = c + 1 - 2 * core

    barrier = pltpu.get_barrier_semaphore()
    for r in range(1, PEERS):
        pl.semaphore_signal(barrier, inc=1, device_id=(c, peers[r]), device_id_type=MESH)
    pl.semaphore_signal(barrier, inc=1, device_id=(sibling, h), device_id_type=MESH)
    @pl.when(c >= 2)
    def _():
        for j in range(PEERS):
            pl.semaphore_signal(barrier, inc=1, device_id=(c - 2, j), device_id_type=MESH)

    @pl.when(c < N_CTX - 2)
    def _():
        for j in range(PEERS):
            pl.semaphore_signal(barrier, inc=1, device_id=(c + 2, j), device_id_type=MESH)

    @pl.when(c >= 4)
    def _():
        pl.semaphore_signal(barrier, inc=1, device_id=(c - 4, h), device_id_type=MESH)

    @pl.when(c < N_CTX - 4)
    def _():
        pl.semaphore_signal(barrier, inc=1, device_id=(c + 4, h), device_id_type=MESH)

    fetches = [
        pltpu.make_async_copy(source, target, in_sem.at[number])
        for number, (source, target) in enumerate(
            (
                (ke_hbm, ke_ref), (ve_hbm, ve_ref), (kc_hbm, kc_ref), (vc_hbm, vc_ref), (ids_hbm, ids_ref),
                (q_hbm, q_ref),
            )
        )
    ]
    for fetch in fetches:
        fetch.start()

    def q_columns(peer):
        return q_ref.at[:, pl.ds(pl.multiple_of(peer * GROUP * D, GROUP * D), GROUP * D)]

    own_q = pltpu.make_async_copy(q_columns(h), qb.at[h], in_sem.at[6])

    bits = iota((D, D), 0) & iota((D, D), 1)
    bits = bits ^ (bits >> 4)
    bits = bits ^ (bits >> 2)
    bits = bits ^ (bits >> 1)
    signs = (1 - 2 * (bits & 1)).astype(F32).astype(BF16)

    for fetch in fetches[:5]:
        fetch.wait()
    k_powers = jnp.exp2(ke_ref[...].astype(F32)).astype(BF16).astype(F32).T
    v_powers = jnp.exp2(ve_ref[...].astype(F32)).astype(BF16).astype(F32).T
    for j in range(PEERS):
        columns = slice(j * D, (j + 1) * D)
        kvs[j, :, 0:D] = (kc_ref[:, columns].astype(F32) * k_powers[:, j:j + 1]).astype(BF16)
        kvs[j, :, D:2 * D] = (vc_ref[:, columns].astype(F32) * v_powers[:, j:j + 1]).astype(BF16)

    ids = ids_ref[...]
    term = iota((D, BLOCK), 0)
    below = jnp.where(ids < term, 1.0, 0.0).astype(F32).astype(BF16)
    upto = jnp.where(ids <= term, 1.0, 0.0).astype(F32).astype(BF16)
    ones = jnp.ones((16, BLOCK), BF16)
    lo, hi = nt_dot(ones, below), nt_dot(ones, upto)
    lo_part, hi_part = jnp.floor(lo * (1.0 / 16)), jnp.floor(hi * (1.0 / 16))
    row = iota((16, D), 0)
    meta = jnp.where(
        row < 4, lo_part,
        jnp.where(row < 8, lo - 16 * lo_part, jnp.where(row < 12, hi_part, hi - 16 * hi_part)),
    )
    kvb[0, META:KV_ROWS] = meta.astype(BF16)

    pl.semaphore_wait(
        barrier,
        PEERS
        + PEERS * (c >= 2).astype(jnp.int32) + (c >= 4).astype(jnp.int32)
        + PEERS * (c < N_CTX - 2).astype(jnp.int32) + (c < N_CTX - 4).astype(jnp.int32),
    )

    my_rows = pl.ds(pl.multiple_of(h * ROWS, ROWS), ROWS)
    kv_copies = {}
    for r in range(1, PEERS):
        peer = peers[r]
        kv_copies[r] = pltpu.make_async_remote_copy(
            src_ref=kvs.at[peer], dst_ref=kvr.at[my_rows],
            send_sem=kv_send.at[r], recv_sem=kv_recv.at[r],
            device_id=(c, peer), device_id_type=MESH,
        )
        kv_copies[r].start()

    after2 = lax.rem(c + 2, N_CTX)
    a_copies = [
        pltpu.make_async_remote_copy(
            src_ref=kvs.at[j], dst_ref=kvr2.at[my_rows],
            send_sem=a_send.at[j], recv_sem=a_recv.at[h],
            device_id=(after2, j), device_id_type=MESH,
        )
        for j in range(PEERS)
    ]
    a_copies.append(
        pltpu.make_async_remote_copy(
            src_ref=kvb.at[0, META:KV_ROWS], dst_ref=kvb.at[2, META:KV_ROWS],
            send_sem=a_send.at[PEERS], recv_sem=a_recv.at[PEERS],
            device_id=(after2, h), device_id_type=MESH,
        )
    )

    @pl.when(c < N_CTX - 2)
    def _():
        for copy in a_copies:
            copy.start()

    def q_copy(r):
        peer = peers[r]
        return pltpu.make_async_remote_copy(
            src_ref=q_columns(peer), dst_ref=qb.at[h],
            send_sem=q_send.at[r], recv_sem=q_recv.at[h],
            device_id=(c, peer), device_id_type=MESH,
        )

    q_copies = {r: q_copy(r) for r in range(1, PEERS)}
    fetches[5].wait()
    own_q.start()
    for r in (1, 2, 3, 4, 5):
        q_copies[r].start()
    kvr[my_rows] = kvs[h]

    token = iota((BLOCK, D), 0).astype(F32)
    lane = iota((BLOCK, D), 1)
    inside = (token >= lo[0:1]) & (token < hi[0:1])
    diagonal = (lane >= D - ROWS) & (lax.rem(iota((BLOCK, D), 0), ROWS) == lane - (D - ROWS))
    aug_q[...] = jnp.where(inside | diagonal, 1.0, 0.0).astype(F32).astype(BF16)

    def key_spans(d):
        spans = kvb[d, META:KV_ROWS].astype(F32)
        first = spans[0:1] * 16 + spans[4:5]
        last = spans[8:9] * 16 + spans[12:13]
        member = (token >= first) & (token < last)
        aug_k[d] = jnp.where(member | (lane >= D - ROWS), 0.0, BIG).astype(F32).astype(BF16)

    for r in range(1, PEERS):
        kv_copies[r].wait_recv()

    def rotate(codes, slot):
        keys = jnp.dot(codes[:, 0:D], signs, preferred_element_type=F32) * SCALE
        kvb[slot, 0:BLOCK] = keys.astype(BF16)
        values = (nt_dot(signs, codes[:, D:2 * D]) * SCALE).astype(BF16)
        for part in range(4):
            kvb[slot, BLOCK + part * D:BLOCK + (part + 1) * D] = values[:, part * D:(part + 1) * D]

    def c_copy(source, slot, target):
        return pltpu.make_async_remote_copy(
            src_ref=kvb.at[source], dst_ref=kvb.at[slot],
            send_sem=c_send.at[slot], recv_sem=c_recv.at[slot],
            device_id=(target, h), device_id_type=MESH,
        )

    c_copies = {
        1: c_copy(2 * core, 1, sibling),
        3: c_copy(2 + 2 * core, 3, sibling),
        4: c_copy(0, 4, lax.rem(c + 4, N_CTX)),
    }
    rotate(kvr, 0)

    @pl.when(c < N_CTX - 4)
    def _():
        c_copies[4].start()

    @pl.when(core == 0)
    def _():
        c_copies[1].start()

    for r in (6, 7):
        q_copies[r].start()
    key_spans(0)

    def receive_nearer_blocks():
        @pl.when(c >= 2)
        def _():
            for j in range(PEERS):
                pltpu.make_async_remote_copy(
                    src_ref=kvs.at[0], dst_ref=kvr2.at[j * ROWS:(j + 1) * ROWS],
                    send_sem=a_send.at[0], recv_sem=a_recv.at[j],
                    device_id=(after2, h), device_id_type=MESH,
                ).wait_recv()
            a_copies[PEERS].wait_recv()
            rotate(kvr2, 2)

        @pl.when(c < 2)
        def _():
            kvb[2] = jnp.zeros((KV_ROWS, D), BF16)

        @pl.when(c < 4)
        def _():
            kvb[4] = jnp.zeros((KV_ROWS, D), BF16)

        @pl.when(core == 0)
        def _():
            c_copies[3].start()

        @pl.when(core == 1)
        def _():
            c_copies[1].start()

        key_spans(2)

    def pass_on_farther_block():
        @pl.when(c >= 4)
        def _():
            c_copies[4].wait_recv()

        c_copies[3].start()

    def receive_farther_blocks():
        @pl.when((core == 0) & (c >= 4))
        def _():
            c_copies[4].wait_recv()

        key_spans(4)
        c_copies[3].wait_recv()
        key_spans(3)

    half = BLOCK // 2

    rows_of = [slice(0, half), slice(half, BLOCK)]

    def turn_queries(n, p):
        for g in range(2):
            heads = [qb[p, :, m * D:(m + 1) * D] for m in range(g * GROUP // 2, (g + 1) * GROUP // 2)]
            qt[n, g] = jnp.concatenate(heads, axis=0).T
        extra = aug_q[pl.ds(pl.multiple_of(p * ROWS, ROWS), ROWS)]
        qt[n, 2] = jnp.concatenate([extra] * (GROUP // 2), axis=0).T

    def score(n, p, d, k, g, top, buffer):
        queries = jnp.concatenate([qt[n, g], qt[n, 2]], axis=0)
        extra_keys = aug_k[d, k:k + half]
        if d == 0:
            column = iota((half, D), 1)
            late = (iota((half, D), 0) + k - p * ROWS > column - (D - ROWS)) & (column >= D - ROWS)
            extra_keys = jnp.where(late, BIG, extra_keys.astype(F32)).astype(BF16)
        keys = jnp.concatenate([kvb[d, k:k + half], extra_keys], axis=1)
        scores = jnp.dot(keys, queries, preferred_element_type=F32)
        s_buf[buffer, k:k + half, rows_of[g]] = scores
        here = jnp.max(scores.reshape(half // 8, 8, half), axis=0)
        top[g] = here if top[g] is None else jnp.maximum(top[g], here)

    def values_of(d, k):
        parts = [kvb[d, BLOCK + part * D:BLOCK + (part + 1) * D] for part in range(k // D, (k + half) // D)]
        return jnp.concatenate(parts, axis=1)

    def out_copy(p):
        rows = pl.ds(pl.multiple_of(p * ROWS, ROWS), ROWS)
        return pltpu.make_async_copy(ob.at[p], out_hbm.at[rows], out_sem.at[p])

    def pieces(span):
        return [(k, g) for g in range(2) for k in range(*span, half)]

    def weigh(d, k, g, buffer, newmax):
        sums, low = None, []
        for row in range(k, k + half, ROWS):
            weights = jnp.exp2((s_buf[buffer, row:row + ROWS, rows_of[g]] - newmax) * LOG2E_SCALE)
            added = jnp.sum(weights.reshape(ROWS // 8, 8, half), axis=0)
            sums = added if sums is None else sums + added
            low.append(weights.astype(BF16))
        low = jnp.concatenate(low, axis=0)
        return sums, jnp.dot(values_of(d, k), low, preferred_element_type=F32)

    def attend(n, p, following, steps, spans, buffers):
        top = [top_s[:, rows_of[g]] for g in range(2)]
        if steps[0]:
            running = [m_s[n, :, rows_of[g]] for g in range(2)]
            total = [l_s[n, :, rows_of[g]] for g in range(2)]
            accum = [o_s[n, :, rows_of[g]] for g in range(2)]
        else:
            running, total, accum = [None, None], [None, None], [None, None]
        for place, d in enumerate(steps):
            next_top = [None, None]
            later = (n, p, steps[place + 1]) if d != steps[-1] else (*following, steps[0])
            now, ahead = pieces(spans[d]), pieces(spans[later[2]])
            for slot in range(max(len(now), len(ahead))):
                if slot < len(ahead):
                    score(*later, *ahead[slot], next_top, buffers[later[2]])
                if slot >= len(now):
                    continue
                k, g = now[slot]
                if top[g] is not None:
                    newmax = jnp.max(top[g], axis=0, keepdims=True)
                    if d:
                        newmax = jnp.maximum(running[g], newmax)
                        factor = jnp.exp2((running[g] - newmax) * LOG2E_SCALE)
                        total[g] = total[g] * factor
                        accum[g] = accum[g] * factor
                    running[g] = newmax
                    top[g] = None
                sums, product = weigh(d, k, g, buffers[d], running[g])
                total[g] = sums if total[g] is None else total[g] + sums
                accum[g] = product if accum[g] is None else accum[g] + product
            top = next_top
        for g in range(2):
            top_s[:, rows_of[g]] = top[g]
            if steps[-1] < STEPS:
                m_s[n, :, rows_of[g]], l_s[n, :, rows_of[g]], o_s[n, :, rows_of[g]] = running[g], total[g], accum[g]
                continue
            attended = accum[g] * (1.0 / jnp.sum(total[g], axis=0, keepdims=True))
            attended = attended.T.astype(BF16)
            for member in range(GROUP // 2):
                column = (g * GROUP // 2 + member) * D
                ob[p, :, column:column + D] = attended[member * ROWS:(member + 1) * ROWS]
        if steps[-1] == STEPS:
            out_copy(p).start()

    def await_queries(turn, n):
        p = partner(turn, n)
        pltpu.make_async_remote_copy(
            src_ref=q_columns(h), dst_ref=qb.at[p],
            send_sem=q_send.at[0], recv_sem=q_recv.at[p],
            device_id=(c, lax.rem(h + 1, PEERS)), device_id_type=MESH,
        ).wait_recv()

    def four_chunks(turn, steps, spans, buffers):
        if not steps[0]:
            turn_queries(0, partner(turn, 0))
        top = [None, None]
        for k, g in pieces(spans[steps[0]]):
            score(0, partner(turn, 0), steps[0], k, g, top, buffers[steps[0]])
        for g in range(2):
            top_s[:, rows_of[g]] = top[g]

        def body(n, carry):
            if steps == (1, 2):
                @pl.when((n == 2) & (core == 1))
                def _():
                    pass_on_farther_block()

            if not steps[0]:
                @pl.when(n < 3)
                def _():
                    await_queries(turn, n + 1)
                    turn_queries(n + 1, partner(turn, n + 1))

            after = jnp.minimum(n + 1, 3)
            attend(n, partner(turn, n), (after, partner(turn, after)), steps, spans, buffers)
            return carry

        lax.fori_loop(0, 4, body, 0)

    def own_block(chunks, span):
        tops = {}
        for n in chunks:
            p = partner(0, n)
            if n:
                await_queries(0, n)
            turn_queries(n, p)
            tops[n] = [None, None]
            for k, g in pieces(span):
                score(n, p, 0, k, g, tops[n], n % 2)
        for n in chunks:
            for g in range(2):
                newmax = jnp.max(tops[n][g], axis=0, keepdims=True)
                parts = [weigh(0, k, g, n % 2, newmax) for k in range(*span, half)]
                m_s[n, :, rows_of[g]] = newmax
                l_s[n, :, rows_of[g]] = sum([part[0] for part in parts[1:]], parts[0][0])
                o_s[n, :, rows_of[g]] = sum([part[1] for part in parts[1:]], parts[0][1])

    def either_own_block(chunks):
        @pl.when(own_early)
        def _():
            own_block(chunks, early[0])

        @pl.when(jnp.logical_not(own_early))
        def _():
            own_block(chunks, late[0])

    whole = (0, BLOCK)
    early = {0: (0, half), 1: whole, 2: whole, 3: whole, 4: whole}
    late = {0: whole, 1: whole, 2: whole, 3: whole, 4: (half, BLOCK)}
    own_early = hy < 2

    def either(first, *arguments):
        @pl.when(first)
        def _():
            four_chunks(*arguments[:2], early, arguments[2])

        @pl.when(jnp.logical_not(first))
        def _():
            four_chunks(*arguments[:2], late, arguments[2])

    own_q.wait()
    either_own_block((0, 1))
    receive_nearer_blocks()
    either_own_block((2, 3))
    c_copies[1].wait_recv()
    key_spans(1)
    either(own_early, 0, (1, 2), {1: 0, 2: 1})
    receive_farther_blocks()
    either(own_early, 0, (3, 4), {3: 0, 4: 1})
    await_queries(1, 0)
    either(jnp.logical_not(own_early), 1, (0, 1, 2, 3, 4), {0: 0, 1: 1, 2: 0, 3: 1, 4: 2})

    for p in range(PEERS):
        out_copy(p).wait()
    for r in range(1, PEERS):
        kv_copies[r].wait_send()
        q_copies[r].wait_send()
    for step in (1, 3):
        c_copies[step].wait_send()

    @pl.when(c < N_CTX - 2)
    def _():
        for copy in a_copies:
            copy.wait_send()

    @pl.when(c < N_CTX - 4)
    def _():
        c_copies[4].wait_send()


def per_device(queries, key_codes, value_codes, key_exponents, value_exponents, trace_ids):
    hbm = pl.BlockSpec(memory_space=pl.ANY)
    dma = pltpu.SemaphoreType.DMA
    return pl.pallas_call(
        kernel,
        out_shape=jax.ShapeDtypeStruct((BLOCK, GROUP * D), BF16),
        in_specs=[hbm] * 6,
        out_specs=hbm,
        scratch_shapes=[
            pltpu.VMEM((ROWS, PEERS * GROUP * D), BF16),
            pltpu.VMEM((ROWS, PEERS * D), BF16),
            pltpu.VMEM((ROWS, PEERS * D), BF16),
            pltpu.VMEM((PEERS, ROWS), jnp.int32),
            pltpu.VMEM((PEERS, ROWS), jnp.int32),
            pltpu.VMEM((1, BLOCK), jnp.int32),
            pltpu.VMEM((PEERS, ROWS, 2 * D), BF16),
            pltpu.VMEM((BLOCK, 2 * D), BF16),
            pltpu.VMEM((BLOCK, 2 * D), BF16),
            pltpu.VMEM((STEPS + 1, KV_ROWS, D), BF16),
            pltpu.VMEM((PEERS, ROWS, GROUP * D), BF16),
            pltpu.VMEM((4, 3, D, BLOCK // 2), BF16),
            pltpu.VMEM((BLOCK, D), BF16),
            pltpu.VMEM((STEPS + 1, BLOCK, D), BF16),
            pltpu.VMEM((3, BLOCK, BLOCK), F32),
            pltpu.VMEM((8, BLOCK), F32),
            pltpu.VMEM((4, 1, BLOCK), F32),
            pltpu.VMEM((4, 8, BLOCK), F32),
            pltpu.VMEM((4, D, BLOCK), F32),
            pltpu.VMEM((PEERS, ROWS, GROUP * D), BF16),
            dma((7,)), dma((PEERS,)), dma((PEERS,)), dma((PEERS,)), dma((PEERS,)),
            dma((PEERS + 1,)), dma((PEERS + 1,)), dma((STEPS + 1,)), dma((STEPS + 1,)), dma((PEERS,)),
        ],
        compiler_params=pltpu.CompilerParams(
            collective_id=0, has_side_effects=True, vmem_limit_bytes=62 * 1024 * 1024
        ),
        cost_estimate=pl.CostEstimate(flops=9_000_000_000, bytes_accessed=4_000_000, transcendentals=8_700_000),
    )(
        queries, key_codes, value_codes, key_exponents.T, value_exponents.T, trace_ids.reshape(1, BLOCK)
    )


def solution(mesh):
    placed = (
        P(("ctx", "head"), None),
        P(("ctx", "head"), None),
        P(("ctx", "head"), None),
        P(("ctx", "head"), None),
        P(("ctx", "head"), None),
        P("ctx"),
    )
    return jax.shard_map(
        per_device, mesh=mesh, in_specs=placed, out_specs=P("ctx", "head"), check_vma=False
    )
```

```python
import math

import jax
import jax.numpy as jnp
from jax import lax
from jax.experimental import pallas as pl
from jax.experimental.pallas import tpu as pltpu
from jax.sharding import PartitionSpec as P

BLOCK = 512
ROWS = 64
PEERS = 8
GROUP = 8
D = 128
STEPS = 4
N_CTX = 32
SCALE = 1.0 / math.sqrt(D)
LOG2E_SCALE = SCALE * math.log2(math.e)
BIG = -1e30
META = BLOCK + 4 * D
KV_ROWS = META + 16
MESH = pl.DeviceIdType.MESH
F32 = jnp.float32
BF16 = jnp.bfloat16


def iota(shape, dimension):
    return lax.broadcasted_iota(jnp.int32, shape, dimension)


def nt_dot(a, b):
    return lax.dot_general(a, b, (((1,), (1,)), ((), ())), preferred_element_type=F32)


def kernel(
    q_hbm, kc_hbm, vc_hbm, ke_hbm, ve_hbm, ids_hbm, out_hbm,
    q_ref, kc_ref, vc_ref, ke_ref, ve_ref, ids_ref,
    kvs, kvr, kvr2, kvb, qb, aug_q, aug_k, s_buf, ob,
    in_sem, kv_send, kv_recv, q_send, q_recv, a_send, a_recv, c_send, c_recv, out_sem,
):
    c = lax.axis_index("ctx")
    h = lax.axis_index("head")
    core = lax.rem(c, 2)
    hy, hx = h // 2, lax.rem(h, 2)

    def to_peer(r):
        ry, rx = r // 2, r % 2
        return lax.rem(hy + ry, 4) * 2 + lax.rem(hx + rx, 2)

    sibling = c + 1 - 2 * core

    barrier = pltpu.get_barrier_semaphore()
    for r in range(1, PEERS):
        pl.semaphore_signal(barrier, inc=1, device_id=(c, to_peer(r)), device_id_type=MESH)
    pl.semaphore_signal(barrier, inc=1, device_id=(sibling, h), device_id_type=MESH)

    for step in (2, 4):
        @pl.when(c >= step)
        def _():
            for j in range(PEERS):
                pl.semaphore_signal(barrier, inc=1, device_id=(c - step, j), device_id_type=MESH)

        @pl.when(c < N_CTX - step)
        def _():
            for j in range(PEERS):
                pl.semaphore_signal(barrier, inc=1, device_id=(c + step, j), device_id_type=MESH)

    fetches = [
        pltpu.make_async_copy(source, target, in_sem.at[number])
        for number, (source, target) in enumerate(
            (
                (ke_hbm, ke_ref), (ve_hbm, ve_ref), (kc_hbm, kc_ref), (vc_hbm, vc_ref), (ids_hbm, ids_ref),
                (q_hbm, q_ref),
            )
        )
    ]
    for fetch in fetches:
        fetch.start()

    def q_columns(peer):
        return q_ref.at[:, pl.ds(pl.multiple_of(peer * GROUP * D, GROUP * D), GROUP * D)]

    own_q = pltpu.make_async_copy(q_columns(h), qb.at[h], in_sem.at[6])

    bits = iota((D, D), 0) & iota((D, D), 1)
    bits = bits ^ (bits >> 4)
    bits = bits ^ (bits >> 2)
    bits = bits ^ (bits >> 1)
    signs = (1 - 2 * (bits & 1)).astype(F32).astype(BF16)

    for fetch in fetches[:5]:
        fetch.wait()
    k_powers = jnp.exp2(ke_ref[...].astype(F32)).astype(BF16).astype(F32).T
    v_powers = jnp.exp2(ve_ref[...].astype(F32)).astype(BF16).astype(F32).T
    for j in range(PEERS):
        columns = slice(j * D, (j + 1) * D)
        kvs[j, :, 0:D] = (kc_ref[:, columns].astype(F32) * k_powers[:, j:j + 1]).astype(BF16)
        kvs[j, :, D:2 * D] = (vc_ref[:, columns].astype(F32) * v_powers[:, j:j + 1]).astype(BF16)

    ids = ids_ref[...]
    term = iota((D, BLOCK), 0)
    below = jnp.where(ids < term, 1.0, 0.0).astype(F32).astype(BF16)
    upto = jnp.where(ids <= term, 1.0, 0.0).astype(F32).astype(BF16)
    ones = jnp.ones((16, BLOCK), BF16)
    lo, hi = nt_dot(ones, below), nt_dot(ones, upto)
    lo_part, hi_part = jnp.floor(lo * (1.0 / 16)), jnp.floor(hi * (1.0 / 16))
    row = iota((16, D), 0)
    meta = jnp.where(
        row < 4, lo_part,
        jnp.where(row < 8, lo - 16 * lo_part, jnp.where(row < 12, hi_part, hi - 16 * hi_part)),
    )
    kvb[0, META:KV_ROWS] = meta.astype(BF16)

    pl.semaphore_wait(
        barrier,
        PEERS
        + PEERS * ((c >= 2).astype(jnp.int32) + (c >= 4).astype(jnp.int32))
        + PEERS * ((c < N_CTX - 2).astype(jnp.int32) + (c < N_CTX - 4).astype(jnp.int32)),
    )

    my_rows = pl.ds(pl.multiple_of(h * ROWS, ROWS), ROWS)
    kv_copies = {}
    for r in range(1, PEERS):
        peer = to_peer(r)
        kv_copies[r] = pltpu.make_async_remote_copy(
            src_ref=kvs.at[peer], dst_ref=kvr.at[my_rows],
            send_sem=kv_send.at[r], recv_sem=kv_recv.at[r],
            device_id=(c, peer), device_id_type=MESH,
        )
        kv_copies[r].start()

    def code_copies(step):
        place, after = step // 2 - 1, lax.rem(c + step, N_CTX)
        copies = [
            pltpu.make_async_remote_copy(
                src_ref=kvs.at[j], dst_ref=kvr2.at[place, my_rows],
                send_sem=a_send.at[place, j], recv_sem=a_recv.at[place, h],
                device_id=(after, j), device_id_type=MESH,
            )
            for j in range(PEERS)
        ]
        copies.append(
            pltpu.make_async_remote_copy(
                src_ref=kvb.at[0, META:KV_ROWS], dst_ref=kvb.at[step, META:KV_ROWS],
                send_sem=a_send.at[place, PEERS], recv_sem=a_recv.at[place, PEERS],
                device_id=(after, h), device_id_type=MESH,
            )
        )
        return copies

    a_copies = {step: code_copies(step) for step in (2, 4)}
    for step in (2, 4):
        @pl.when(c < N_CTX - step)
        def _():
            for copy in a_copies[step]:
                copy.start()

    def q_copy(r):
        peer = to_peer(r)
        return pltpu.make_async_remote_copy(
            src_ref=q_columns(peer), dst_ref=qb.at[h],
            send_sem=q_send.at[r], recv_sem=q_recv.at[h],
            device_id=(c, peer), device_id_type=MESH,
        )

    q_copies = {r: q_copy(r) for r in range(1, PEERS)}
    fetches[5].wait()
    own_q.start()
    for r in (2, 6, 4):
        q_copies[r].start()
    kvr[my_rows] = kvs[h]

    token = iota((BLOCK, D), 0).astype(F32)
    lane = iota((BLOCK, D), 1)
    inside = (token >= lo[0:1]) & (token < hi[0:1])
    diagonal = (lane >= D - ROWS) & (lax.rem(iota((BLOCK, D), 0), ROWS) == lane - (D - ROWS))
    aug_q[...] = jnp.where(inside | diagonal, 1.0, 0.0).astype(F32).astype(BF16)

    def key_spans(d):
        spans = kvb[d, META:KV_ROWS].astype(F32)
        first = spans[0:1] * 16 + spans[4:5]
        last = spans[8:9] * 16 + spans[12:13]
        member = (token >= first) & (token < last)
        aug_k[d] = jnp.where(member | (lane >= D - ROWS), 0.0, BIG).astype(F32).astype(BF16)

    for r in range(1, PEERS):
        kv_copies[r].wait_recv()

    def rotate(codes, slot):
        keys = jnp.dot(codes[:, 0:D], signs, preferred_element_type=F32) * SCALE
        kvb[slot, 0:BLOCK] = keys.astype(BF16)
        values = (nt_dot(signs, codes[:, D:2 * D]) * SCALE).astype(BF16)
        for part in range(4):
            kvb[slot, BLOCK + part * D:BLOCK + (part + 1) * D] = values[:, part * D:(part + 1) * D]

    def c_copy(source, slot, target):
        return pltpu.make_async_remote_copy(
            src_ref=kvb.at[source], dst_ref=kvb.at[slot],
            send_sem=c_send.at[slot], recv_sem=c_recv.at[slot],
            device_id=(target, h), device_id_type=MESH,
        )

    c_copies = {1: c_copy(2 * core, 1, sibling), 3: c_copy(2 + 2 * core, 3, sibling)}
    rotate(kvr, 0)

    @pl.when(core == 0)
    def _():
        c_copies[1].start()

    for r in (1, 3, 7, 5):
        q_copies[r].start()
    key_spans(0)

    def receive(step):
        @pl.when(c >= step)
        def _():
            place = step // 2 - 1
            for j in range(PEERS):
                pltpu.make_async_remote_copy(
                    src_ref=kvs.at[0], dst_ref=kvr2.at[place, j * ROWS:(j + 1) * ROWS],
                    send_sem=a_send.at[place, 0], recv_sem=a_recv.at[place, j],
                    device_id=(lax.rem(c + step, N_CTX), h), device_id_type=MESH,
                ).wait_recv()
            a_copies[step][PEERS].wait_recv()
            rotate(kvr2.at[place], step)

        @pl.when(c < step)
        def _():
            kvb[step] = jnp.zeros((KV_ROWS, D), BF16)

    receive(2)

    @pl.when(core == 0)
    def _():
        c_copies[3].start()

    @pl.when(core == 1)
    def _():
        c_copies[1].start()

    key_spans(2)
    receive(4)

    @pl.when(core == 1)
    def _():
        c_copies[3].start()

    key_spans(4)
    c_copies[1].wait_recv()
    key_spans(1)
    c_copies[3].wait_recv()
    key_spans(3)

    half = BLOCK // 2

    def attend(p, first_keys, last_keys):
        extra = aug_q[pl.ds(pl.multiple_of(p * ROWS, ROWS), ROWS)]
        extra = jnp.concatenate([extra] * (GROUP // 2), axis=0)
        spans = [(0, first_keys)] + [(0, BLOCK)] * 3 + [(last_keys, BLOCK)]

        def queries_of(g):
            heads = [qb[p, :, i * D:(i + 1) * D] for i in range(g * GROUP // 2, (g + 1) * GROUP // 2)]
            return jnp.concatenate([jnp.concatenate(heads, axis=0), extra], axis=1)

        def pieces(d):
            start, stop = spans[d]
            return [(k, g) for g in range(2) for k in range(start, stop, half)]

        def score(d, k, g, top):
            extra_keys = aug_k[d, k:k + half]
            if d == 0:
                column = iota((half, D), 1)
                late = (iota((half, D), 0) + k - p * ROWS > column - (D - ROWS)) & (column >= D - ROWS)
                extra_keys = jnp.where(late, BIG, extra_keys.astype(F32)).astype(BF16)
            keys = jnp.concatenate([kvb[d, k:k + half], extra_keys], axis=1)
            scores = nt_dot(keys, queries_of(g))
            s_buf[d % 2, k:k + half, g * half:(g + 1) * half] = scores
            here = jnp.max(scores.reshape(half // 8, 8, half), axis=0)
            top[g] = here if top[g] is None else jnp.maximum(top[g], here)

        def values_of(d, k):
            parts = [kvb[d, BLOCK + part * D:BLOCK + (part + 1) * D] for part in range(k // D, (k + half) // D)]
            return jnp.concatenate(parts, axis=1)

        top = [None, None]
        for k, g in pieces(0):
            score(0, k, g, top)
        running, total, accum = [None, None], [None, None], [None, None]
        for d in range(STEPS + 1):
            next_top = [None, None]
            now = pieces(d)
            following = pieces(d + 1) if d < STEPS else []
            for slot in range(max(len(now), len(following))):
                if slot < len(following):
                    score(d + 1, *following[slot], next_top)
                if slot >= len(now):
                    continue
                k, g = now[slot]
                if top[g] is not None:
                    newmax = jnp.max(top[g], axis=0, keepdims=True)
                    if d:
                        newmax = jnp.maximum(running[g], newmax)
                        factor = jnp.exp2((running[g] - newmax) * LOG2E_SCALE)
                        total[g] = total[g] * factor
                        accum[g] = accum[g] * factor
                    running[g] = newmax
                    top[g] = None
                scores = s_buf[d % 2, k:k + half, g * half:(g + 1) * half]
                weights = jnp.exp2((scores - running[g]) * LOG2E_SCALE)
                sums = jnp.sum(weights.reshape(half // 8, 8, half), axis=0)
                product = jnp.dot(values_of(d, k), weights.astype(BF16), preferred_element_type=F32)
                total[g] = sums if total[g] is None else total[g] + sums
                accum[g] = product if accum[g] is None else accum[g] + product
            top = next_top
        for g in range(2):
            attended = accum[g] * (1.0 / jnp.sum(total[g], axis=0, keepdims=True))
            attended = attended.T.astype(BF16)
            for i in range(GROUP // 2):
                column = (g * GROUP // 2 + i) * D
                ob[p, :, column:column + D] = attended[i * ROWS:(i + 1) * ROWS]

    def out_copy(p):
        rows = pl.ds(pl.multiple_of(p * ROWS, ROWS), ROWS)
        return pltpu.make_async_copy(ob.at[p], out_hbm.at[rows], out_sem.at[p])

    def body(i, carry):
        turn, rx = lax.rem(i, 4), i // 4
        ry = turn + (turn // 2) * (5 - 2 * turn)
        p = lax.rem(hy + 4 - ry, 4) * 2 + lax.rem(hx + rx, 2)

        @pl.when(i == 0)
        def _():
            own_q.wait()

        @pl.when(i > 0)
        def _():
            pltpu.make_async_remote_copy(
                src_ref=q_columns(h), dst_ref=qb.at[p],
                send_sem=q_send.at[0], recv_sem=q_recv.at[p],
                device_id=(c, lax.rem(h + 1, PEERS)), device_id_type=MESH,
            ).wait_recv()

        @pl.when(p < PEERS // 2)
        def _():
            attend(p, half, 0)

        @pl.when(p >= PEERS // 2)
        def _():
            attend(p, BLOCK, half)

        out_copy(p).start()
        return carry

    lax.fori_loop(0, PEERS, body, 0)

    for p in range(PEERS):
        out_copy(p).wait()
    for r in range(1, PEERS):
        kv_copies[r].wait_send()
        q_copies[r].wait_send()
    for step in (1, 3):
        c_copies[step].wait_send()

    for step in (2, 4):
        @pl.when(c < N_CTX - step)
        def _():
            for copy in a_copies[step]:
                copy.wait_send()


def hand_over(source, target, held, in_sem, out_sem):
    rows = [pl.ds(p * ROWS, ROWS) for p in range(PEERS)]
    arrive = [pltpu.make_async_copy(source.at[r], held.at[r], in_sem.at[n]) for n, r in enumerate(rows)]
    leave = [pltpu.make_async_copy(held.at[r], target.at[r], out_sem.at[n]) for n, r in enumerate(rows)]
    for copy in arrive:
        copy.start()
    for n in range(PEERS):
        arrive[n].wait()
        leave[n].start()
    for copy in leave:
        copy.wait()


def per_device(queries, key_codes, value_codes, key_exponents, value_exponents, trace_ids):
    hbm = pl.BlockSpec(memory_space=pl.ANY)
    dma = pltpu.SemaphoreType.DMA
    attended = pl.pallas_call(
        kernel,
        out_shape=jax.ShapeDtypeStruct((BLOCK, GROUP * D), BF16),
        in_specs=[hbm] * 6,
        out_specs=hbm,
        scratch_shapes=[
            pltpu.VMEM((ROWS, PEERS * GROUP * D), BF16),
            pltpu.VMEM((ROWS, PEERS * D), BF16),
            pltpu.VMEM((ROWS, PEERS * D), BF16),
            pltpu.VMEM((PEERS, ROWS), jnp.int32),
            pltpu.VMEM((PEERS, ROWS), jnp.int32),
            pltpu.VMEM((1, BLOCK), jnp.int32),
            pltpu.VMEM((PEERS, ROWS, 2 * D), BF16),
            pltpu.VMEM((BLOCK, 2 * D), BF16),
            pltpu.VMEM((2, BLOCK, 2 * D), BF16),
            pltpu.VMEM((STEPS + 1, KV_ROWS, D), BF16),
            pltpu.VMEM((PEERS, ROWS, GROUP * D), BF16),
            pltpu.VMEM((BLOCK, D), BF16),
            pltpu.VMEM((STEPS + 1, BLOCK, D), BF16),
            pltpu.VMEM((2, BLOCK, BLOCK), F32),
            pltpu.VMEM((PEERS, ROWS, GROUP * D), BF16),
            dma((7,)), dma((PEERS,)), dma((PEERS,)), dma((PEERS,)), dma((PEERS,)),
            dma((2, PEERS + 1)), dma((2, PEERS + 1)), dma((STEPS + 1,)), dma((STEPS + 1,)), dma((PEERS,)),
        ],
        compiler_params=pltpu.CompilerParams(
            collective_id=0, has_side_effects=True, vmem_limit_bytes=62 * 1024 * 1024
        ),
        cost_estimate=pl.CostEstimate(flops=9_000_000_000, bytes_accessed=4_000_000, transcendentals=8_700_000),
    )(
        queries, key_codes, value_codes, key_exponents.T, value_exponents.T, trace_ids.reshape(1, BLOCK)
    )
    return pl.pallas_call(
        hand_over,
        out_shape=jax.ShapeDtypeStruct((BLOCK, GROUP * D), BF16),
        in_specs=[hbm],
        out_specs=hbm,
        scratch_shapes=[pltpu.VMEM((BLOCK, GROUP * D), BF16), dma((PEERS,)), dma((PEERS,))],
        compiler_params=pltpu.CompilerParams(vmem_limit_bytes=62 * 1024 * 1024),
    )(attended)


def solution(mesh):
    placed = (
        P(("ctx", "head"), None),
        P(("ctx", "head"), None),
        P(("ctx", "head"), None),
        P(("ctx", "head"), None),
        P(("ctx", "head"), None),
        P("ctx"),
    )
    return jax.shard_map(
        per_device, mesh=mesh, in_specs=placed, out_specs=P("ctx", "head"), check_vma=False
    )
```

```python
import math

import jax
import jax.numpy as jnp
from jax import lax
from jax.experimental import pallas as pl
from jax.experimental.pallas import tpu as pltpu
from jax.sharding import PartitionSpec as P

BLOCK = 512
ROWS = 64
PEERS = 8
GROUP = 8
D = 128
STEPS = 4
N_CTX = 32
SCALE = 1.0 / math.sqrt(D)
LOG2E_SCALE = SCALE * math.log2(math.e)
BIG = -1e30
META = BLOCK + 4 * D
KV_ROWS = META + 16
MESH = pl.DeviceIdType.MESH
F32 = jnp.float32
BF16 = jnp.bfloat16


def iota(shape, dimension):
    return lax.broadcasted_iota(jnp.int32, shape, dimension)


def nt_dot(a, b):
    return lax.dot_general(a, b, (((1,), (1,)), ((), ())), preferred_element_type=F32)


def kernel(
    q_hbm, kc_hbm, vc_hbm, ke_hbm, ve_hbm, ids_hbm, out_hbm,
    q_ref, kc_ref, vc_ref, ke_ref, ve_ref, ids_ref,
    kvs, kvr, kvr2, kvb, qb, aug_q, aug_k, s_buf, ob,
    in_sem, kv_send, kv_recv, q_send, q_recv, a_send, a_recv, c_send, c_recv, out_sem,
):
    c = lax.axis_index("ctx")
    h = lax.axis_index("head")
    core = lax.rem(c, 2)
    hy, hx = h // 2, lax.rem(h, 2)

    def to_peer(r):
        ry, rx = r // 2, r % 2
        return lax.rem(hy + ry, 4) * 2 + lax.rem(hx + rx, 2)

    sibling = c + 1 - 2 * core

    barrier = pltpu.get_barrier_semaphore()
    for r in range(1, PEERS):
        pl.semaphore_signal(barrier, inc=1, device_id=(c, to_peer(r)), device_id_type=MESH)
    pl.semaphore_signal(barrier, inc=1, device_id=(sibling, h), device_id_type=MESH)

    @pl.when(c >= 2)
    def _():
        for j in range(PEERS):
            pl.semaphore_signal(barrier, inc=1, device_id=(c - 2, j), device_id_type=MESH)

    @pl.when(c < N_CTX - 2)
    def _():
        for j in range(PEERS):
            pl.semaphore_signal(barrier, inc=1, device_id=(c + 2, j), device_id_type=MESH)

    @pl.when(c >= 4)
    def _():
        pl.semaphore_signal(barrier, inc=1, device_id=(c - 4, h), device_id_type=MESH)

    @pl.when(c < N_CTX - 4)
    def _():
        pl.semaphore_signal(barrier, inc=1, device_id=(c + 4, h), device_id_type=MESH)

    fetches = [
        pltpu.make_async_copy(source, target, in_sem.at[number])
        for number, (source, target) in enumerate(
            (
                (ke_hbm, ke_ref), (ve_hbm, ve_ref), (kc_hbm, kc_ref), (vc_hbm, vc_ref), (ids_hbm, ids_ref),
                (q_hbm, q_ref),
            )
        )
    ]
    for fetch in fetches:
        fetch.start()

    def q_columns(peer):
        return q_ref.at[:, pl.ds(pl.multiple_of(peer * GROUP * D, GROUP * D), GROUP * D)]

    own_q = pltpu.make_async_copy(q_columns(h), qb.at[h], in_sem.at[6])

    bits = iota((D, D), 0) & iota((D, D), 1)
    bits = bits ^ (bits >> 4)
    bits = bits ^ (bits >> 2)
    bits = bits ^ (bits >> 1)
    signs = (1 - 2 * (bits & 1)).astype(F32).astype(BF16)

    for fetch in fetches[:5]:
        fetch.wait()
    k_powers = jnp.exp2(ke_ref[...].astype(F32)).astype(BF16).astype(F32).T
    v_powers = jnp.exp2(ve_ref[...].astype(F32)).astype(BF16).astype(F32).T
    for j in range(PEERS):
        columns = slice(j * D, (j + 1) * D)
        kvs[j, :, 0:D] = (kc_ref[:, columns].astype(F32) * k_powers[:, j:j + 1]).astype(BF16)
        kvs[j, :, D:2 * D] = (vc_ref[:, columns].astype(F32) * v_powers[:, j:j + 1]).astype(BF16)

    ids = ids_ref[...]
    term = iota((D, BLOCK), 0)
    below = jnp.where(ids < term, 1.0, 0.0).astype(F32).astype(BF16)
    upto = jnp.where(ids <= term, 1.0, 0.0).astype(F32).astype(BF16)
    ones = jnp.ones((16, BLOCK), BF16)
    lo, hi = nt_dot(ones, below), nt_dot(ones, upto)
    lo_part, hi_part = jnp.floor(lo * (1.0 / 16)), jnp.floor(hi * (1.0 / 16))
    row = iota((16, D), 0)
    meta = jnp.where(
        row < 4, lo_part,
        jnp.where(row < 8, lo - 16 * lo_part, jnp.where(row < 12, hi_part, hi - 16 * hi_part)),
    )
    kvb[0, META:KV_ROWS] = meta.astype(BF16)

    pl.semaphore_wait(
        barrier,
        PEERS
        + PEERS * (c >= 2).astype(jnp.int32) + (c >= 4).astype(jnp.int32)
        + PEERS * (c < N_CTX - 2).astype(jnp.int32) + (c < N_CTX - 4).astype(jnp.int32),
    )

    my_rows = pl.ds(pl.multiple_of(h * ROWS, ROWS), ROWS)
    kv_copies = {}
    for r in range(1, PEERS):
        peer = to_peer(r)
        kv_copies[r] = pltpu.make_async_remote_copy(
            src_ref=kvs.at[peer], dst_ref=kvr.at[my_rows],
            send_sem=kv_send.at[r], recv_sem=kv_recv.at[r],
            device_id=(c, peer), device_id_type=MESH,
        )
        kv_copies[r].start()

    def code_copies(step):
        after = lax.rem(c + step, N_CTX)
        copies = [
            pltpu.make_async_remote_copy(
                src_ref=kvs.at[j], dst_ref=kvr2.at[my_rows],
                send_sem=a_send.at[j], recv_sem=a_recv.at[h],
                device_id=(after, j), device_id_type=MESH,
            )
            for j in range(PEERS)
        ]
        copies.append(
            pltpu.make_async_remote_copy(
                src_ref=kvb.at[0, META:KV_ROWS], dst_ref=kvb.at[step, META:KV_ROWS],
                send_sem=a_send.at[PEERS], recv_sem=a_recv.at[PEERS],
                device_id=(after, h), device_id_type=MESH,
            )
        )
        return copies

    a_copies = code_copies(2)

    @pl.when(c < N_CTX - 2)
    def _():
        for copy in a_copies:
            copy.start()

    def q_copy(r):
        peer = to_peer(r)
        return pltpu.make_async_remote_copy(
            src_ref=q_columns(peer), dst_ref=qb.at[h],
            send_sem=q_send.at[r], recv_sem=q_recv.at[h],
            device_id=(c, peer), device_id_type=MESH,
        )

    q_copies = {r: q_copy(r) for r in range(1, PEERS)}
    fetches[5].wait()
    own_q.start()
    kvr[my_rows] = kvs[h]

    token = iota((BLOCK, D), 0).astype(F32)
    lane = iota((BLOCK, D), 1)
    inside = (token >= lo[0:1]) & (token < hi[0:1])
    diagonal = (lane >= D - ROWS) & (lax.rem(iota((BLOCK, D), 0), ROWS) == lane - (D - ROWS))
    aug_q[...] = jnp.where(inside | diagonal, 1.0, 0.0).astype(F32).astype(BF16)

    def key_spans(d):
        spans = kvb[d, META:KV_ROWS].astype(F32)
        first = spans[0:1] * 16 + spans[4:5]
        last = spans[8:9] * 16 + spans[12:13]
        member = (token >= first) & (token < last)
        aug_k[d] = jnp.where(member | (lane >= D - ROWS), 0.0, BIG).astype(F32).astype(BF16)

    for r in range(1, PEERS):
        kv_copies[r].wait_recv()

    def rotate(codes, slot):
        keys = jnp.dot(codes[:, 0:D], signs, preferred_element_type=F32) * SCALE
        kvb[slot, 0:BLOCK] = keys.astype(BF16)
        values = (nt_dot(signs, codes[:, D:2 * D]) * SCALE).astype(BF16)
        for part in range(4):
            kvb[slot, BLOCK + part * D:BLOCK + (part + 1) * D] = values[:, part * D:(part + 1) * D]

    def c_copy(source, slot, target):
        return pltpu.make_async_remote_copy(
            src_ref=kvb.at[source], dst_ref=kvb.at[slot],
            send_sem=c_send.at[slot], recv_sem=c_recv.at[slot],
            device_id=(target, h), device_id_type=MESH,
        )

    c_copies = {
        1: c_copy(2 * core, 1, sibling),
        3: c_copy(2 + 2 * core, 3, sibling),
        4: c_copy(0, 4, lax.rem(c + 4, N_CTX)),
    }
    rotate(kvr, 0)

    @pl.when(c < N_CTX - 4)
    def _():
        c_copies[4].start()

    @pl.when(core == 0)
    def _():
        c_copies[1].start()

    for r in (2, 6, 1, 4, 3, 7, 5):
        q_copies[r].start()
    key_spans(0)

    @pl.when(c >= 2)
    def _():
        for j in range(PEERS):
            pltpu.make_async_remote_copy(
                src_ref=kvs.at[0], dst_ref=kvr2.at[j * ROWS:(j + 1) * ROWS],
                send_sem=a_send.at[0], recv_sem=a_recv.at[j],
                device_id=(lax.rem(c + 2, N_CTX), h), device_id_type=MESH,
            ).wait_recv()
        a_copies[PEERS].wait_recv()
        rotate(kvr2, 2)

    @pl.when(c < 2)
    def _():
        kvb[2] = jnp.zeros((KV_ROWS, D), BF16)

    @pl.when(c < 4)
    def _():
        kvb[4] = jnp.zeros((KV_ROWS, D), BF16)

    @pl.when(core == 0)
    def _():
        c_copies[3].start()

    @pl.when(core == 1)
    def _():
        c_copies[1].start()

    key_spans(2)

    @pl.when(c >= 4)
    def _():
        c_copies[4].wait_recv()

    @pl.when(core == 1)
    def _():
        c_copies[3].start()

    key_spans(4)
    c_copies[1].wait_recv()
    key_spans(1)
    c_copies[3].wait_recv()
    key_spans(3)

    half = BLOCK // 2

    def attend(p, first_keys, last_keys):
        extra = aug_q[pl.ds(pl.multiple_of(p * ROWS, ROWS), ROWS)]
        extra = jnp.concatenate([extra] * (GROUP // 2), axis=0)
        spans = [(0, first_keys)] + [(0, BLOCK)] * 3 + [(last_keys, BLOCK)]

        def queries_of(g):
            heads = [qb[p, :, i * D:(i + 1) * D] for i in range(g * GROUP // 2, (g + 1) * GROUP // 2)]
            return jnp.concatenate([jnp.concatenate(heads, axis=0), extra], axis=1)

        def pieces(d):
            start, stop = spans[d]
            return [(k, g) for g in range(2) for k in range(start, stop, half)]

        def score(d, k, g, top):
            extra_keys = aug_k[d, k:k + half]
            if d == 0:
                column = iota((half, D), 1)
                late = (iota((half, D), 0) + k - p * ROWS > column - (D - ROWS)) & (column >= D - ROWS)
                extra_keys = jnp.where(late, BIG, extra_keys.astype(F32)).astype(BF16)
            keys = jnp.concatenate([kvb[d, k:k + half], extra_keys], axis=1)
            scores = nt_dot(keys, queries_of(g))
            s_buf[d % 2, k:k + half, g * half:(g + 1) * half] = scores
            here = jnp.max(scores.reshape(half // 8, 8, half), axis=0)
            top[g] = here if top[g] is None else jnp.maximum(top[g], here)

        def values_of(d, k):
            parts = [kvb[d, BLOCK + part * D:BLOCK + (part + 1) * D] for part in range(k // D, (k + half) // D)]
            return jnp.concatenate(parts, axis=1)

        top = [None, None]
        for k, g in pieces(0):
            score(0, k, g, top)
        running, total, accum = [None, None], [None, None], [None, None]
        for d in range(STEPS + 1):
            next_top = [None, None]
            now = pieces(d)
            following = pieces(d + 1) if d < STEPS else []
            for slot in range(max(len(now), len(following))):
                if slot < len(following):
                    score(d + 1, *following[slot], next_top)
                if slot >= len(now):
                    continue
                k, g = now[slot]
                if top[g] is not None:
                    newmax = jnp.max(top[g], axis=0, keepdims=True)
                    if d:
                        newmax = jnp.maximum(running[g], newmax)
                        factor = jnp.exp2((running[g] - newmax) * LOG2E_SCALE)
                        total[g] = total[g] * factor
                        accum[g] = accum[g] * factor
                    running[g] = newmax
                    top[g] = None
                scores = s_buf[d % 2, k:k + half, g * half:(g + 1) * half]
                weights = jnp.exp2((scores - running[g]) * LOG2E_SCALE)
                sums = jnp.sum(weights.reshape(half // 8, 8, half), axis=0)
                product = jnp.dot(values_of(d, k), weights.astype(BF16), preferred_element_type=F32)
                total[g] = sums if total[g] is None else total[g] + sums
                accum[g] = product if accum[g] is None else accum[g] + product
            top = next_top
        for g in range(2):
            attended = accum[g] * (1.0 / jnp.sum(total[g], axis=0, keepdims=True))
            attended = attended.T.astype(BF16)
            for i in range(GROUP // 2):
                column = (g * GROUP // 2 + i) * D
                ob[p, :, column:column + D] = attended[i * ROWS:(i + 1) * ROWS]

    def out_copy(p):
        rows = pl.ds(pl.multiple_of(p * ROWS, ROWS), ROWS)
        return pltpu.make_async_copy(ob.at[p], out_hbm.at[rows], out_sem.at[p])

    def body(i, carry):
        turn, rx = lax.rem(i, 4), i // 4
        ry = turn + (turn // 2) * (5 - 2 * turn)
        p = lax.rem(hy + 4 - ry, 4) * 2 + lax.rem(hx + rx, 2)

        @pl.when(i == 0)
        def _():
            own_q.wait()

        @pl.when(i > 0)
        def _():
            pltpu.make_async_remote_copy(
                src_ref=q_columns(h), dst_ref=qb.at[p],
                send_sem=q_send.at[0], recv_sem=q_recv.at[p],
                device_id=(c, lax.rem(h + 1, PEERS)), device_id_type=MESH,
            ).wait_recv()

        @pl.when(p < PEERS // 2)
        def _():
            attend(p, half, 0)

        @pl.when(p >= PEERS // 2)
        def _():
            attend(p, BLOCK, half)

        out_copy(p).start()
        return carry

    lax.fori_loop(0, PEERS, body, 0)

    for p in range(PEERS):
        out_copy(p).wait()
    for r in range(1, PEERS):
        kv_copies[r].wait_send()
        q_copies[r].wait_send()
    for step in (1, 3):
        c_copies[step].wait_send()

    @pl.when(c < N_CTX - 2)
    def _():
        for copy in a_copies:
            copy.wait_send()

    @pl.when(c < N_CTX - 4)
    def _():
        c_copies[4].wait_send()


def hand_over(source, target, held, in_sem, out_sem):
    rows = [pl.ds(p * ROWS, ROWS) for p in range(PEERS)]
    arrive = [pltpu.make_async_copy(source.at[r], held.at[r], in_sem.at[n]) for n, r in enumerate(rows)]
    leave = [pltpu.make_async_copy(held.at[r], target.at[r], out_sem.at[n]) for n, r in enumerate(rows)]
    for copy in arrive:
        copy.start()
    for n in range(PEERS):
        arrive[n].wait()
        leave[n].start()
    for copy in leave:
        copy.wait()


def per_device(queries, key_codes, value_codes, key_exponents, value_exponents, trace_ids):
    hbm = pl.BlockSpec(memory_space=pl.ANY)
    dma = pltpu.SemaphoreType.DMA
    attended = pl.pallas_call(
        kernel,
        out_shape=jax.ShapeDtypeStruct((BLOCK, GROUP * D), BF16),
        in_specs=[hbm] * 6,
        out_specs=hbm,
        scratch_shapes=[
            pltpu.VMEM((ROWS, PEERS * GROUP * D), BF16),
            pltpu.VMEM((ROWS, PEERS * D), BF16),
            pltpu.VMEM((ROWS, PEERS * D), BF16),
            pltpu.VMEM((PEERS, ROWS), jnp.int32),
            pltpu.VMEM((PEERS, ROWS), jnp.int32),
            pltpu.VMEM((1, BLOCK), jnp.int32),
            pltpu.VMEM((PEERS, ROWS, 2 * D), BF16),
            pltpu.VMEM((BLOCK, 2 * D), BF16),
            pltpu.VMEM((BLOCK, 2 * D), BF16),
            pltpu.VMEM((STEPS + 1, KV_ROWS, D), BF16),
            pltpu.VMEM((PEERS, ROWS, GROUP * D), BF16),
            pltpu.VMEM((BLOCK, D), BF16),
            pltpu.VMEM((STEPS + 1, BLOCK, D), BF16),
            pltpu.VMEM((2, BLOCK, BLOCK), F32),
            pltpu.VMEM((PEERS, ROWS, GROUP * D), BF16),
            dma((7,)), dma((PEERS,)), dma((PEERS,)), dma((PEERS,)), dma((PEERS,)),
            dma((PEERS + 1,)), dma((PEERS + 1,)), dma((STEPS + 1,)), dma((STEPS + 1,)), dma((PEERS,)),
        ],
        compiler_params=pltpu.CompilerParams(
            collective_id=0, has_side_effects=True, vmem_limit_bytes=62 * 1024 * 1024
        ),
        cost_estimate=pl.CostEstimate(flops=9_000_000_000, bytes_accessed=4_000_000, transcendentals=8_700_000),
    )(
        queries, key_codes, value_codes, key_exponents.T, value_exponents.T, trace_ids.reshape(1, BLOCK)
    )
    return pl.pallas_call(
        hand_over,
        out_shape=jax.ShapeDtypeStruct((BLOCK, GROUP * D), BF16),
        in_specs=[hbm],
        out_specs=hbm,
        scratch_shapes=[pltpu.VMEM((BLOCK, GROUP * D), BF16), dma((PEERS,)), dma((PEERS,))],
        compiler_params=pltpu.CompilerParams(vmem_limit_bytes=62 * 1024 * 1024),
    )(attended)


def solution(mesh):
    placed = (
        P(("ctx", "head"), None),
        P(("ctx", "head"), None),
        P(("ctx", "head"), None),
        P(("ctx", "head"), None),
        P(("ctx", "head"), None),
        P("ctx"),
    )
    return jax.shard_map(
        per_device, mesh=mesh, in_specs=placed, out_specs=P("ctx", "head"), check_vma=False
    )
```

```python
import math

import jax
import jax.numpy as jnp
from jax import lax
from jax.experimental import pallas as pl
from jax.experimental.pallas import tpu as pltpu
from jax.sharding import PartitionSpec as P

BLOCK = 512
ROWS = 64
PEERS = 8
GROUP = 8
D = 128
STEPS = 4
N_CTX = 32
SCALE = 1.0 / math.sqrt(D)
LOG2E_SCALE = SCALE * math.log2(math.e)
BIG = -1e30
META = BLOCK + 4 * D
KV_ROWS = META + 16
MESH = pl.DeviceIdType.MESH
F32 = jnp.float32
BF16 = jnp.bfloat16


def iota(shape, dimension):
    return lax.broadcasted_iota(jnp.int32, shape, dimension)


def nt_dot(a, b):
    return lax.dot_general(a, b, (((1,), (1,)), ((), ())), preferred_element_type=F32)


def kernel(
    q_hbm, kc_hbm, vc_hbm, ke_hbm, ve_hbm, ids_hbm, out_hbm,
    q_ref, kc_ref, vc_ref, ke_ref, ve_ref, ids_ref,
    kvs, kvr, kvr2, kvb, qb, qt, aug_q, aug_k, s_buf, top_s, m_s, l_s, o_s, ob,
    in_sem, kv_send, kv_recv, q_send, q_recv, a_send, a_recv, c_send, c_recv, out_sem,
):
    c = lax.axis_index("ctx")
    h = lax.axis_index("head")
    core = lax.rem(c, 2)
    hy, hx = h // 2, lax.rem(h, 2)

    y_low = lax.rem(hy, 2)

    def partner(turn, n):
        base = lax.rem(hy - y_low + 2 * turn, 4)
        flip = lax.rem(turn + n, 2)
        y = base + y_low + flip * (1 - 2 * y_low)
        return y * 2 + lax.rem(hx + n // 2, 2)

    others = [(turn, n) for turn in range(2) for n in range(4)][1:]
    peers = {r: partner(*others[r - 1]) for r in range(1, PEERS)}

    sibling = c + 1 - 2 * core

    barrier = pltpu.get_barrier_semaphore()
    for r in range(1, PEERS):
        pl.semaphore_signal(barrier, inc=1, device_id=(c, peers[r]), device_id_type=MESH)
    pl.semaphore_signal(barrier, inc=1, device_id=(sibling, h), device_id_type=MESH)
    @pl.when(c >= 2)
    def _():
        for j in range(PEERS):
            pl.semaphore_signal(barrier, inc=1, device_id=(c - 2, j), device_id_type=MESH)

    @pl.when(c < N_CTX - 2)
    def _():
        for j in range(PEERS):
            pl.semaphore_signal(barrier, inc=1, device_id=(c + 2, j), device_id_type=MESH)

    @pl.when(c >= 4)
    def _():
        pl.semaphore_signal(barrier, inc=1, device_id=(c - 4, h), device_id_type=MESH)

    @pl.when(c < N_CTX - 4)
    def _():
        pl.semaphore_signal(barrier, inc=1, device_id=(c + 4, h), device_id_type=MESH)

    fetches = [
        pltpu.make_async_copy(source, target, in_sem.at[number])
        for number, (source, target) in enumerate(
            (
                (ke_hbm, ke_ref), (ve_hbm, ve_ref), (kc_hbm, kc_ref), (vc_hbm, vc_ref), (ids_hbm, ids_ref),
                (q_hbm, q_ref),
            )
        )
    ]
    for fetch in fetches:
        fetch.start()

    def q_columns(peer):
        return q_ref.at[:, pl.ds(pl.multiple_of(peer * GROUP * D, GROUP * D), GROUP * D)]

    own_q = pltpu.make_async_copy(q_columns(h), qb.at[h], in_sem.at[6])

    bits = iota((D, D), 0) & iota((D, D), 1)
    bits = bits ^ (bits >> 4)
    bits = bits ^ (bits >> 2)
    bits = bits ^ (bits >> 1)
    signs = (1 - 2 * (bits & 1)).astype(F32).astype(BF16)

    for fetch in fetches[:5]:
        fetch.wait()
    k_powers = jnp.exp2(ke_ref[...].astype(F32)).astype(BF16).astype(F32).T
    v_powers = jnp.exp2(ve_ref[...].astype(F32)).astype(BF16).astype(F32).T
    for j in range(PEERS):
        columns = slice(j * D, (j + 1) * D)
        kvs[j, :, 0:D] = (kc_ref[:, columns].astype(F32) * k_powers[:, j:j + 1]).astype(BF16)
        kvs[j, :, D:2 * D] = (vc_ref[:, columns].astype(F32) * v_powers[:, j:j + 1]).astype(BF16)

    ids = ids_ref[...]
    term = iota((D, BLOCK), 0)
    below = jnp.where(ids < term, 1.0, 0.0).astype(F32).astype(BF16)
    upto = jnp.where(ids <= term, 1.0, 0.0).astype(F32).astype(BF16)
    ones = jnp.ones((16, BLOCK), BF16)
    lo, hi = nt_dot(ones, below), nt_dot(ones, upto)
    lo_part, hi_part = jnp.floor(lo * (1.0 / 16)), jnp.floor(hi * (1.0 / 16))
    row = iota((16, D), 0)
    meta = jnp.where(
        row < 4, lo_part,
        jnp.where(row < 8, lo - 16 * lo_part, jnp.where(row < 12, hi_part, hi - 16 * hi_part)),
    )
    kvb[0, META:KV_ROWS] = meta.astype(BF16)

    pl.semaphore_wait(
        barrier,
        PEERS
        + PEERS * (c >= 2).astype(jnp.int32) + (c >= 4).astype(jnp.int32)
        + PEERS * (c < N_CTX - 2).astype(jnp.int32) + (c < N_CTX - 4).astype(jnp.int32),
    )

    my_rows = pl.ds(pl.multiple_of(h * ROWS, ROWS), ROWS)
    kv_copies = {}
    for r in range(1, PEERS):
        peer = peers[r]
        kv_copies[r] = pltpu.make_async_remote_copy(
            src_ref=kvs.at[peer], dst_ref=kvr.at[my_rows],
            send_sem=kv_send.at[r], recv_sem=kv_recv.at[r],
            device_id=(c, peer), device_id_type=MESH,
        )
        kv_copies[r].start()

    after2 = lax.rem(c + 2, N_CTX)
    a_copies = [
        pltpu.make_async_remote_copy(
            src_ref=kvs.at[j], dst_ref=kvr2.at[my_rows],
            send_sem=a_send.at[j], recv_sem=a_recv.at[h],
            device_id=(after2, j), device_id_type=MESH,
        )
        for j in range(PEERS)
    ]
    a_copies.append(
        pltpu.make_async_remote_copy(
            src_ref=kvb.at[0, META:KV_ROWS], dst_ref=kvb.at[2, META:KV_ROWS],
            send_sem=a_send.at[PEERS], recv_sem=a_recv.at[PEERS],
            device_id=(after2, h), device_id_type=MESH,
        )
    )

    @pl.when(c < N_CTX - 2)
    def _():
        for copy in a_copies:
            copy.start()

    def q_copy(r):
        peer = peers[r]
        return pltpu.make_async_remote_copy(
            src_ref=q_columns(peer), dst_ref=qb.at[h],
            send_sem=q_send.at[r], recv_sem=q_recv.at[h],
            device_id=(c, peer), device_id_type=MESH,
        )

    q_copies = {r: q_copy(r) for r in range(1, PEERS)}
    fetches[5].wait()
    own_q.start()
    for r in (1, 4, 5):
        q_copies[r].start()
    kvr[my_rows] = kvs[h]

    token = iota((BLOCK, D), 0).astype(F32)
    lane = iota((BLOCK, D), 1)
    inside = (token >= lo[0:1]) & (token < hi[0:1])
    diagonal = (lane >= D - ROWS) & (lax.rem(iota((BLOCK, D), 0), ROWS) == lane - (D - ROWS))
    aug_q[...] = jnp.where(inside | diagonal, 1.0, 0.0).astype(F32).astype(BF16)

    def key_spans(d):
        spans = kvb[d, META:KV_ROWS].astype(F32)
        first = spans[0:1] * 16 + spans[4:5]
        last = spans[8:9] * 16 + spans[12:13]
        member = (token >= first) & (token < last)
        aug_k[d] = jnp.where(member | (lane >= D - ROWS), 0.0, BIG).astype(F32).astype(BF16)

    for r in range(1, PEERS):
        kv_copies[r].wait_recv()

    def rotate(codes, slot):
        keys = jnp.dot(codes[:, 0:D], signs, preferred_element_type=F32) * SCALE
        kvb[slot, 0:BLOCK] = keys.astype(BF16)
        values = (nt_dot(signs, codes[:, D:2 * D]) * SCALE).astype(BF16)
        for part in range(4):
            kvb[slot, BLOCK + part * D:BLOCK + (part + 1) * D] = values[:, part * D:(part + 1) * D]

    def c_copy(source, slot, target):
        return pltpu.make_async_remote_copy(
            src_ref=kvb.at[source], dst_ref=kvb.at[slot],
            send_sem=c_send.at[slot], recv_sem=c_recv.at[slot],
            device_id=(target, h), device_id_type=MESH,
        )

    c_copies = {
        1: c_copy(2 * core, 1, sibling),
        3: c_copy(2 + 2 * core, 3, sibling),
        4: c_copy(0, 4, lax.rem(c + 4, N_CTX)),
    }
    rotate(kvr, 0)

    @pl.when(c < N_CTX - 4)
    def _():
        c_copies[4].start()

    @pl.when(core == 0)
    def _():
        c_copies[1].start()

    for r in (2, 3, 6, 7):
        q_copies[r].start()
    key_spans(0)

    @pl.when(c >= 2)
    def _():
        for j in range(PEERS):
            pltpu.make_async_remote_copy(
                src_ref=kvs.at[0], dst_ref=kvr2.at[j * ROWS:(j + 1) * ROWS],
                send_sem=a_send.at[0], recv_sem=a_recv.at[j],
                device_id=(after2, h), device_id_type=MESH,
            ).wait_recv()
        a_copies[PEERS].wait_recv()
        rotate(kvr2, 2)

    @pl.when(c < 2)
    def _():
        kvb[2] = jnp.zeros((KV_ROWS, D), BF16)

    @pl.when(c < 4)
    def _():
        kvb[4] = jnp.zeros((KV_ROWS, D), BF16)

    @pl.when(core == 0)
    def _():
        c_copies[3].start()

    @pl.when(core == 1)
    def _():
        c_copies[1].start()

    key_spans(2)
    c_copies[1].wait_recv()
    key_spans(1)

    def pass_on_farther_block():
        @pl.when(c >= 4)
        def _():
            c_copies[4].wait_recv()

        c_copies[3].start()

    def receive_farther_blocks():
        @pl.when((core == 0) & (c >= 4))
        def _():
            c_copies[4].wait_recv()

        key_spans(4)
        c_copies[3].wait_recv()
        key_spans(3)

    half = BLOCK // 2

    rows_of = [slice(0, half), slice(half, BLOCK)]

    def turn_queries(n, p):
        for g in range(2):
            heads = [qb[p, :, m * D:(m + 1) * D] for m in range(g * GROUP // 2, (g + 1) * GROUP // 2)]
            qt[n, g] = jnp.concatenate(heads, axis=0).T
        extra = aug_q[pl.ds(pl.multiple_of(p * ROWS, ROWS), ROWS)]
        qt[n, 2] = jnp.concatenate([extra] * (GROUP // 2), axis=0).T

    def score(n, p, d, k, g, top, buffer):
        queries = jnp.concatenate([qt[n, g], qt[n, 2]], axis=0)
        extra_keys = aug_k[d, k:k + half]
        if d == 0:
            column = iota((half, D), 1)
            late = (iota((half, D), 0) + k - p * ROWS > column - (D - ROWS)) & (column >= D - ROWS)
            extra_keys = jnp.where(late, BIG, extra_keys.astype(F32)).astype(BF16)
        keys = jnp.concatenate([kvb[d, k:k + half], extra_keys], axis=1)
        scores = jnp.dot(keys, queries, preferred_element_type=F32)
        s_buf[buffer, k:k + half, rows_of[g]] = scores
        here = jnp.max(scores.reshape(half // 8, 8, half), axis=0)
        top[g] = here if top[g] is None else jnp.maximum(top[g], here)

    def values_of(d, k):
        parts = [kvb[d, BLOCK + part * D:BLOCK + (part + 1) * D] for part in range(k // D, (k + half) // D)]
        return jnp.concatenate(parts, axis=1)

    def out_copy(p):
        rows = pl.ds(pl.multiple_of(p * ROWS, ROWS), ROWS)
        return pltpu.make_async_copy(ob.at[p], out_hbm.at[rows], out_sem.at[p])

    def pieces(span):
        return [(k, g) for g in range(2) for k in range(*span, half)]

    def attend(n, p, following, steps, spans, buffers):
        top = [top_s[:, rows_of[g]] for g in range(2)]
        if steps[0]:
            running = [m_s[n, :, rows_of[g]] for g in range(2)]
            total = [l_s[n, :, rows_of[g]] for g in range(2)]
            accum = [o_s[n, :, rows_of[g]] for g in range(2)]
        else:
            running, total, accum = [None, None], [None, None], [None, None]
        for place, d in enumerate(steps):
            next_top = [None, None]
            later = (n, p, steps[place + 1]) if d != steps[-1] else (*following, steps[0])
            now, ahead = pieces(spans[d]), pieces(spans[later[2]])
            for slot in range(max(len(now), len(ahead))):
                if slot < len(ahead):
                    score(*later, *ahead[slot], next_top, buffers[later[2]])
                if slot >= len(now):
                    continue
                k, g = now[slot]
                if top[g] is not None:
                    newmax = jnp.max(top[g], axis=0, keepdims=True)
                    if d:
                        newmax = jnp.maximum(running[g], newmax)
                        factor = jnp.exp2((running[g] - newmax) * LOG2E_SCALE)
                        total[g] = total[g] * factor
                        accum[g] = accum[g] * factor
                    running[g] = newmax
                    top[g] = None
                scores = s_buf[buffers[d], k:k + half, rows_of[g]]
                weights = jnp.exp2((scores - running[g]) * LOG2E_SCALE)
                sums = jnp.sum(weights.reshape(half // 8, 8, half), axis=0)
                product = jnp.dot(values_of(d, k), weights.astype(BF16), preferred_element_type=F32)
                total[g] = sums if total[g] is None else total[g] + sums
                accum[g] = product if accum[g] is None else accum[g] + product
            top = next_top
        for g in range(2):
            top_s[:, rows_of[g]] = top[g]
            if steps[-1] < STEPS:
                m_s[n, :, rows_of[g]], l_s[n, :, rows_of[g]], o_s[n, :, rows_of[g]] = running[g], total[g], accum[g]
                continue
            attended = accum[g] * (1.0 / jnp.sum(total[g], axis=0, keepdims=True))
            attended = attended.T.astype(BF16)
            for member in range(GROUP // 2):
                column = (g * GROUP // 2 + member) * D
                ob[p, :, column:column + D] = attended[member * ROWS:(member + 1) * ROWS]
        if steps[-1] == STEPS:
            out_copy(p).start()

    def await_queries(turn, n):
        p = partner(turn, n)
        pltpu.make_async_remote_copy(
            src_ref=q_columns(h), dst_ref=qb.at[p],
            send_sem=q_send.at[0], recv_sem=q_recv.at[p],
            device_id=(c, lax.rem(h + 1, PEERS)), device_id_type=MESH,
        ).wait_recv()

    def four_chunks(turn, steps, spans, buffers):
        if not steps[0]:
            turn_queries(0, partner(turn, 0))
        top = [None, None]
        for k, g in pieces(spans[steps[0]]):
            score(0, partner(turn, 0), steps[0], k, g, top, buffers[steps[0]])
        for g in range(2):
            top_s[:, rows_of[g]] = top[g]

        def body(n, carry):
            if steps == (0, 1, 2):
                @pl.when((n == 2) & (core == 1))
                def _():
                    pass_on_farther_block()

            if not steps[0]:
                @pl.when(n < 3)
                def _():
                    await_queries(turn, n + 1)
                    turn_queries(n + 1, partner(turn, n + 1))

            after = jnp.minimum(n + 1, 3)
            attend(n, partner(turn, n), (after, partner(turn, after)), steps, spans, buffers)
            return carry

        lax.fori_loop(0, 4, body, 0)

    whole = (0, BLOCK)
    early = {0: (0, half), 1: whole, 2: whole, 3: whole, 4: whole}
    late = {0: whole, 1: whole, 2: whole, 3: whole, 4: (half, BLOCK)}
    own_early = hy < 2

    def either(first, *arguments):
        @pl.when(first)
        def _():
            four_chunks(*arguments[:2], early, arguments[2])

        @pl.when(jnp.logical_not(first))
        def _():
            four_chunks(*arguments[:2], late, arguments[2])

    own_q.wait()
    either(own_early, 0, (0, 1, 2), {0: 0, 1: 1, 2: 2})
    receive_farther_blocks()
    either(own_early, 0, (3, 4), {3: 0, 4: 1})
    await_queries(1, 0)
    either(jnp.logical_not(own_early), 1, (0, 1, 2, 3, 4), {0: 0, 1: 1, 2: 0, 3: 1, 4: 2})

    for p in range(PEERS):
        out_copy(p).wait()
    for r in range(1, PEERS):
        kv_copies[r].wait_send()
        q_copies[r].wait_send()
    for step in (1, 3):
        c_copies[step].wait_send()

    @pl.when(c < N_CTX - 2)
    def _():
        for copy in a_copies:
            copy.wait_send()

    @pl.when(c < N_CTX - 4)
    def _():
        c_copies[4].wait_send()


def hand_over(source, target, held, in_sem, out_sem):
    rows = [pl.ds(p * ROWS, ROWS) for p in range(PEERS)]
    arrive = [pltpu.make_async_copy(source.at[r], held.at[r], in_sem.at[n]) for n, r in enumerate(rows)]
    leave = [pltpu.make_async_copy(held.at[r], target.at[r], out_sem.at[n]) for n, r in enumerate(rows)]
    for copy in arrive:
        copy.start()
    for n in range(PEERS):
        arrive[n].wait()
        leave[n].start()
    for copy in leave:
        copy.wait()


def per_device(queries, key_codes, value_codes, key_exponents, value_exponents, trace_ids):
    hbm = pl.BlockSpec(memory_space=pl.ANY)
    dma = pltpu.SemaphoreType.DMA
    attended = pl.pallas_call(
        kernel,
        out_shape=jax.ShapeDtypeStruct((BLOCK, GROUP * D), BF16),
        in_specs=[hbm] * 6,
        out_specs=hbm,
        scratch_shapes=[
            pltpu.VMEM((ROWS, PEERS * GROUP * D), BF16),
            pltpu.VMEM((ROWS, PEERS * D), BF16),
            pltpu.VMEM((ROWS, PEERS * D), BF16),
            pltpu.VMEM((PEERS, ROWS), jnp.int32),
            pltpu.VMEM((PEERS, ROWS), jnp.int32),
            pltpu.VMEM((1, BLOCK), jnp.int32),
            pltpu.VMEM((PEERS, ROWS, 2 * D), BF16),
            pltpu.VMEM((BLOCK, 2 * D), BF16),
            pltpu.VMEM((BLOCK, 2 * D), BF16),
            pltpu.VMEM((STEPS + 1, KV_ROWS, D), BF16),
            pltpu.VMEM((PEERS, ROWS, GROUP * D), BF16),
            pltpu.VMEM((4, 3, D, BLOCK // 2), BF16),
            pltpu.VMEM((BLOCK, D), BF16),
            pltpu.VMEM((STEPS + 1, BLOCK, D), BF16),
            pltpu.VMEM((3, BLOCK, BLOCK), F32),
            pltpu.VMEM((8, BLOCK), F32),
            pltpu.VMEM((4, 1, BLOCK), F32),
            pltpu.VMEM((4, 8, BLOCK), F32),
            pltpu.VMEM((4, D, BLOCK), F32),
            pltpu.VMEM((PEERS, ROWS, GROUP * D), BF16),
            dma((7,)), dma((PEERS,)), dma((PEERS,)), dma((PEERS,)), dma((PEERS,)),
            dma((PEERS + 1,)), dma((PEERS + 1,)), dma((STEPS + 1,)), dma((STEPS + 1,)), dma((PEERS,)),
        ],
        compiler_params=pltpu.CompilerParams(
            collective_id=0, has_side_effects=True, vmem_limit_bytes=62 * 1024 * 1024
        ),
        cost_estimate=pl.CostEstimate(flops=9_000_000_000, bytes_accessed=4_000_000, transcendentals=8_700_000),
    )(
        queries, key_codes, value_codes, key_exponents.T, value_exponents.T, trace_ids.reshape(1, BLOCK)
    )
    return pl.pallas_call(
        hand_over,
        out_shape=jax.ShapeDtypeStruct((BLOCK, GROUP * D), BF16),
        in_specs=[hbm],
        out_specs=hbm,
        scratch_shapes=[pltpu.VMEM((BLOCK, GROUP * D), BF16), dma((PEERS,)), dma((PEERS,))],
        compiler_params=pltpu.CompilerParams(vmem_limit_bytes=62 * 1024 * 1024),
    )(attended)


def solution(mesh):
    placed = (
        P(("ctx", "head"), None),
        P(("ctx", "head"), None),
        P(("ctx", "head"), None),
        P(("ctx", "head"), None),
        P(("ctx", "head"), None),
        P("ctx"),
    )
    return jax.shard_map(
        per_device, mesh=mesh, in_specs=placed, out_specs=P("ctx", "head"), check_vma=False
    )
```

```python
import math

import jax
import jax.numpy as jnp
from jax import lax
from jax.experimental import pallas as pl
from jax.experimental.pallas import tpu as pltpu
from jax.sharding import PartitionSpec as P

BLOCK = 512
ROWS = 64
PEERS = 8
GROUP = 8
D = 128
STEPS = 4
N_CTX = 32
SCALE = 1.0 / math.sqrt(D)
LOG2E_SCALE = SCALE * math.log2(math.e)
BIG = -1e30
META = BLOCK + 4 * D
KV_ROWS = META + 16
MESH = pl.DeviceIdType.MESH
F32 = jnp.float32
BF16 = jnp.bfloat16


def iota(shape, dimension):
    return lax.broadcasted_iota(jnp.int32, shape, dimension)


def nt_dot(a, b):
    return lax.dot_general(a, b, (((1,), (1,)), ((), ())), preferred_element_type=F32)


def kernel(
    q_hbm, kc_hbm, vc_hbm, ke_hbm, ve_hbm, ids_hbm, out_hbm,
    q_ref, kc_ref, vc_ref, ke_ref, ve_ref, ids_ref,
    kvs, kvr, kvr2, kvb, qb, qt, aug_q, aug_k, s_buf, top_s, m_s, l_s, o_s, ob,
    in_sem, kv_send, kv_recv, q_send, q_recv, a_send, a_recv, c_send, c_recv, out_sem,
):
    c = lax.axis_index("ctx")
    h = lax.axis_index("head")
    core = lax.rem(c, 2)
    hy, hx = h // 2, lax.rem(h, 2)

    y_low = lax.rem(hy, 2)

    def partner(turn, n):
        base = lax.rem(hy - y_low + 2 * turn, 4)
        flip = lax.rem(turn + n, 2)
        y = base + y_low + flip * (1 - 2 * y_low)
        return y * 2 + lax.rem(hx + n // 2, 2)

    others = [(turn, n) for turn in range(2) for n in range(4)][1:]
    peers = {r: partner(*others[r - 1]) for r in range(1, PEERS)}

    sibling = c + 1 - 2 * core

    barrier = pltpu.get_barrier_semaphore()
    for r in range(1, PEERS):
        pl.semaphore_signal(barrier, inc=1, device_id=(c, peers[r]), device_id_type=MESH)
    pl.semaphore_signal(barrier, inc=1, device_id=(sibling, h), device_id_type=MESH)
    @pl.when(c >= 2)
    def _():
        for j in range(PEERS):
            pl.semaphore_signal(barrier, inc=1, device_id=(c - 2, j), device_id_type=MESH)

    @pl.when(c < N_CTX - 2)
    def _():
        for j in range(PEERS):
            pl.semaphore_signal(barrier, inc=1, device_id=(c + 2, j), device_id_type=MESH)

    @pl.when(c >= 4)
    def _():
        pl.semaphore_signal(barrier, inc=1, device_id=(c - 4, h), device_id_type=MESH)

    @pl.when(c < N_CTX - 4)
    def _():
        pl.semaphore_signal(barrier, inc=1, device_id=(c + 4, h), device_id_type=MESH)

    fetches = [
        pltpu.make_async_copy(source, target, in_sem.at[number])
        for number, (source, target) in enumerate(
            (
                (ke_hbm, ke_ref), (ve_hbm, ve_ref), (kc_hbm, kc_ref), (vc_hbm, vc_ref), (ids_hbm, ids_ref),
                (q_hbm, q_ref),
            )
        )
    ]
    for fetch in fetches:
        fetch.start()

    def q_columns(peer):
        return q_ref.at[:, pl.ds(pl.multiple_of(peer * GROUP * D, GROUP * D), GROUP * D)]

    own_q = pltpu.make_async_copy(q_columns(h), qb.at[h], in_sem.at[6])

    bits = iota((D, D), 0) & iota((D, D), 1)
    bits = bits ^ (bits >> 4)
    bits = bits ^ (bits >> 2)
    bits = bits ^ (bits >> 1)
    signs = (1 - 2 * (bits & 1)).astype(F32).astype(BF16)

    for fetch in fetches[:5]:
        fetch.wait()
    k_powers = jnp.exp2(ke_ref[...].astype(F32)).astype(BF16).astype(F32).T
    v_powers = jnp.exp2(ve_ref[...].astype(F32)).astype(BF16).astype(F32).T
    for j in range(PEERS):
        columns = slice(j * D, (j + 1) * D)
        kvs[j, :, 0:D] = (kc_ref[:, columns].astype(F32) * k_powers[:, j:j + 1]).astype(BF16)
        kvs[j, :, D:2 * D] = (vc_ref[:, columns].astype(F32) * v_powers[:, j:j + 1]).astype(BF16)

    ids = ids_ref[...]
    term = iota((D, BLOCK), 0)
    below = jnp.where(ids < term, 1.0, 0.0).astype(F32).astype(BF16)
    upto = jnp.where(ids <= term, 1.0, 0.0).astype(F32).astype(BF16)
    ones = jnp.ones((16, BLOCK), BF16)
    lo, hi = nt_dot(ones, below), nt_dot(ones, upto)
    lo_part, hi_part = jnp.floor(lo * (1.0 / 16)), jnp.floor(hi * (1.0 / 16))
    row = iota((16, D), 0)
    meta = jnp.where(
        row < 4, lo_part,
        jnp.where(row < 8, lo - 16 * lo_part, jnp.where(row < 12, hi_part, hi - 16 * hi_part)),
    )
    kvb[0, META:KV_ROWS] = meta.astype(BF16)

    pl.semaphore_wait(
        barrier,
        PEERS
        + PEERS * (c >= 2).astype(jnp.int32) + (c >= 4).astype(jnp.int32)
        + PEERS * (c < N_CTX - 2).astype(jnp.int32) + (c < N_CTX - 4).astype(jnp.int32),
    )

    my_rows = pl.ds(pl.multiple_of(h * ROWS, ROWS), ROWS)
    kv_copies = {}
    for r in range(1, PEERS):
        peer = peers[r]
        kv_copies[r] = pltpu.make_async_remote_copy(
            src_ref=kvs.at[peer], dst_ref=kvr.at[my_rows],
            send_sem=kv_send.at[r], recv_sem=kv_recv.at[r],
            device_id=(c, peer), device_id_type=MESH,
        )
        kv_copies[r].start()

    after2 = lax.rem(c + 2, N_CTX)
    a_copies = [
        pltpu.make_async_remote_copy(
            src_ref=kvs.at[j], dst_ref=kvr2.at[my_rows],
            send_sem=a_send.at[j], recv_sem=a_recv.at[h],
            device_id=(after2, j), device_id_type=MESH,
        )
        for j in range(PEERS)
    ]
    a_copies.append(
        pltpu.make_async_remote_copy(
            src_ref=kvb.at[0, META:KV_ROWS], dst_ref=kvb.at[2, META:KV_ROWS],
            send_sem=a_send.at[PEERS], recv_sem=a_recv.at[PEERS],
            device_id=(after2, h), device_id_type=MESH,
        )
    )

    @pl.when(c < N_CTX - 2)
    def _():
        for copy in a_copies:
            copy.start()

    def q_copy(r):
        peer = peers[r]
        return pltpu.make_async_remote_copy(
            src_ref=q_columns(peer), dst_ref=qb.at[h],
            send_sem=q_send.at[r], recv_sem=q_recv.at[h],
            device_id=(c, peer), device_id_type=MESH,
        )

    q_copies = {r: q_copy(r) for r in range(1, PEERS)}
    fetches[5].wait()
    own_q.start()
    for r in (1, 4, 5):
        q_copies[r].start()
    kvr[my_rows] = kvs[h]

    token = iota((BLOCK, D), 0).astype(F32)
    lane = iota((BLOCK, D), 1)
    inside = (token >= lo[0:1]) & (token < hi[0:1])
    diagonal = (lane >= D - ROWS) & (lax.rem(iota((BLOCK, D), 0), ROWS) == lane - (D - ROWS))
    aug_q[...] = jnp.where(inside | diagonal, 1.0, 0.0).astype(F32).astype(BF16)

    def key_spans(d):
        spans = kvb[d, META:KV_ROWS].astype(F32)
        first = spans[0:1] * 16 + spans[4:5]
        last = spans[8:9] * 16 + spans[12:13]
        member = (token >= first) & (token < last)
        aug_k[d] = jnp.where(member | (lane >= D - ROWS), 0.0, BIG).astype(F32).astype(BF16)

    for r in range(1, PEERS):
        kv_copies[r].wait_recv()

    def rotate(codes, slot):
        keys = jnp.dot(codes[:, 0:D], signs, preferred_element_type=F32) * SCALE
        kvb[slot, 0:BLOCK] = keys.astype(BF16)
        values = (nt_dot(signs, codes[:, D:2 * D]) * SCALE).astype(BF16)
        for part in range(4):
            kvb[slot, BLOCK + part * D:BLOCK + (part + 1) * D] = values[:, part * D:(part + 1) * D]

    def c_copy(source, slot, target):
        return pltpu.make_async_remote_copy(
            src_ref=kvb.at[source], dst_ref=kvb.at[slot],
            send_sem=c_send.at[slot], recv_sem=c_recv.at[slot],
            device_id=(target, h), device_id_type=MESH,
        )

    c_copies = {
        1: c_copy(2 * core, 1, sibling),
        3: c_copy(2 + 2 * core, 3, sibling),
        4: c_copy(0, 4, lax.rem(c + 4, N_CTX)),
    }
    rotate(kvr, 0)

    @pl.when(c < N_CTX - 4)
    def _():
        c_copies[4].start()

    @pl.when(core == 0)
    def _():
        c_copies[1].start()

    for r in (2, 3, 6, 7):
        q_copies[r].start()
    key_spans(0)

    @pl.when(c >= 2)
    def _():
        for j in range(PEERS):
            pltpu.make_async_remote_copy(
                src_ref=kvs.at[0], dst_ref=kvr2.at[j * ROWS:(j + 1) * ROWS],
                send_sem=a_send.at[0], recv_sem=a_recv.at[j],
                device_id=(after2, h), device_id_type=MESH,
            ).wait_recv()
        a_copies[PEERS].wait_recv()
        rotate(kvr2, 2)

    @pl.when(c < 2)
    def _():
        kvb[2] = jnp.zeros((KV_ROWS, D), BF16)

    @pl.when(c < 4)
    def _():
        kvb[4] = jnp.zeros((KV_ROWS, D), BF16)

    @pl.when(core == 0)
    def _():
        c_copies[3].start()

    @pl.when(core == 1)
    def _():
        c_copies[1].start()

    key_spans(2)
    c_copies[1].wait_recv()
    key_spans(1)

    def pass_on_farther_block():
        @pl.when(c >= 4)
        def _():
            c_copies[4].wait_recv()

        c_copies[3].start()

    def receive_farther_blocks():
        @pl.when((core == 0) & (c >= 4))
        def _():
            c_copies[4].wait_recv()

        key_spans(4)
        c_copies[3].wait_recv()
        key_spans(3)

    half = BLOCK // 2

    rows_of = [slice(0, half), slice(half, BLOCK)]

    def turn_queries(n, p):
        for g in range(2):
            heads = [qb[p, :, m * D:(m + 1) * D] for m in range(g * GROUP // 2, (g + 1) * GROUP // 2)]
            qt[n, g] = jnp.concatenate(heads, axis=0).T
        extra = aug_q[pl.ds(pl.multiple_of(p * ROWS, ROWS), ROWS)]
        qt[n, 2] = jnp.concatenate([extra] * (GROUP // 2), axis=0).T

    def score(n, p, d, k, g, top, buffer):
        queries = jnp.concatenate([qt[n, g], qt[n, 2]], axis=0)
        extra_keys = aug_k[d, k:k + half]
        if d == 0:
            column = iota((half, D), 1)
            late = (iota((half, D), 0) + k - p * ROWS > column - (D - ROWS)) & (column >= D - ROWS)
            extra_keys = jnp.where(late, BIG, extra_keys.astype(F32)).astype(BF16)
        keys = jnp.concatenate([kvb[d, k:k + half], extra_keys], axis=1)
        scores = jnp.dot(keys, queries, preferred_element_type=F32)
        s_buf[buffer, k:k + half, rows_of[g]] = scores
        here = jnp.max(scores.reshape(half // 8, 8, half), axis=0)
        top[g] = here if top[g] is None else jnp.maximum(top[g], here)

    def values_of(d, k):
        parts = [kvb[d, BLOCK + part * D:BLOCK + (part + 1) * D] for part in range(k // D, (k + half) // D)]
        return jnp.concatenate(parts, axis=1)

    def out_copy(p):
        rows = pl.ds(pl.multiple_of(p * ROWS, ROWS), ROWS)
        return pltpu.make_async_copy(ob.at[p], out_hbm.at[rows], out_sem.at[p])

    def pieces(span):
        return [(k, g) for g in range(2) for k in range(*span, half)]

    def attend(n, p, following, steps, spans, buffers):
        top = [top_s[:, rows_of[g]] for g in range(2)]
        if steps[0]:
            running = [m_s[n, :, rows_of[g]] for g in range(2)]
            total = [l_s[n, :, rows_of[g]] for g in range(2)]
            accum = [o_s[n, :, rows_of[g]] for g in range(2)]
        else:
            running, total, accum = [None, None], [None, None], [None, None]
        for place, d in enumerate(steps):
            next_top = [None, None]
            later = (n, p, steps[place + 1]) if d != steps[-1] else (*following, steps[0])
            now, ahead = pieces(spans[d]), pieces(spans[later[2]])
            for slot in range(max(len(now), len(ahead))):
                if slot < len(ahead):
                    score(*later, *ahead[slot], next_top, buffers[later[2]])
                if slot >= len(now):
                    continue
                k, g = now[slot]
                if top[g] is not None:
                    newmax = jnp.max(top[g], axis=0, keepdims=True)
                    if d:
                        newmax = jnp.maximum(running[g], newmax)
                        factor = jnp.exp2((running[g] - newmax) * LOG2E_SCALE)
                        total[g] = total[g] * factor
                        accum[g] = accum[g] * factor
                    running[g] = newmax
                    top[g] = None
                scores = s_buf[buffers[d], k:k + half, rows_of[g]]
                weights = jnp.exp2((scores - running[g]) * LOG2E_SCALE)
                sums = jnp.sum(weights.reshape(half // 8, 8, half), axis=0)
                product = jnp.dot(values_of(d, k), weights.astype(BF16), preferred_element_type=F32)
                total[g] = sums if total[g] is None else total[g] + sums
                accum[g] = product if accum[g] is None else accum[g] + product
            top = next_top
        for g in range(2):
            top_s[:, rows_of[g]] = top[g]
            if steps[-1] < STEPS:
                m_s[n, :, rows_of[g]], l_s[n, :, rows_of[g]], o_s[n, :, rows_of[g]] = running[g], total[g], accum[g]
                continue
            attended = accum[g] * (1.0 / jnp.sum(total[g], axis=0, keepdims=True))
            attended = attended.T.astype(BF16)
            for member in range(GROUP // 2):
                column = (g * GROUP // 2 + member) * D
                ob[p, :, column:column + D] = attended[member * ROWS:(member + 1) * ROWS]
        if steps[-1] == STEPS:
            out_copy(p).start()

    def await_queries(turn, n):
        p = partner(turn, n)
        pltpu.make_async_remote_copy(
            src_ref=q_columns(h), dst_ref=qb.at[p],
            send_sem=q_send.at[0], recv_sem=q_recv.at[p],
            device_id=(c, lax.rem(h + 1, PEERS)), device_id_type=MESH,
        ).wait_recv()

    def four_chunks(turn, steps, spans, buffers):
        if not steps[0]:
            turn_queries(0, partner(turn, 0))
        top = [None, None]
        for k, g in pieces(spans[steps[0]]):
            score(0, partner(turn, 0), steps[0], k, g, top, buffers[steps[0]])
        for g in range(2):
            top_s[:, rows_of[g]] = top[g]

        def body(n, carry):
            if steps == (0, 1, 2):
                @pl.when((n == 1) & (core == 1))
                def _():
                    pass_on_farther_block()

            if not steps[0]:
                @pl.when(n < 3)
                def _():
                    await_queries(turn, n + 1)
                    turn_queries(n + 1, partner(turn, n + 1))

            after = jnp.minimum(n + 1, 3)
            attend(n, partner(turn, n), (after, partner(turn, after)), steps, spans, buffers)
            return carry

        lax.fori_loop(0, 4, body, 0)

    whole = (0, BLOCK)
    early = {0: (0, half), 1: whole, 2: whole, 3: whole, 4: whole}
    late = {0: whole, 1: whole, 2: whole, 3: whole, 4: (half, BLOCK)}
    own_early = hy < 2

    def either(first, *arguments):
        @pl.when(first)
        def _():
            four_chunks(*arguments[:2], early, arguments[2])

        @pl.when(jnp.logical_not(first))
        def _():
            four_chunks(*arguments[:2], late, arguments[2])

    own_q.wait()
    either(own_early, 0, (0, 1, 2), {0: 0, 1: 1, 2: 2})
    receive_farther_blocks()
    either(own_early, 0, (3, 4), {3: 0, 4: 1})
    await_queries(1, 0)
    either(jnp.logical_not(own_early), 1, (0, 1, 2, 3, 4), {0: 0, 1: 1, 2: 0, 3: 1, 4: 2})

    for p in range(PEERS):
        out_copy(p).wait()
    for r in range(1, PEERS):
        kv_copies[r].wait_send()
        q_copies[r].wait_send()
    for step in (1, 3):
        c_copies[step].wait_send()

    @pl.when(c < N_CTX - 2)
    def _():
        for copy in a_copies:
            copy.wait_send()

    @pl.when(c < N_CTX - 4)
    def _():
        c_copies[4].wait_send()


def hand_over(source, target, held, in_sem, out_sem):
    rows = [pl.ds(p * ROWS, ROWS) for p in range(PEERS)]
    arrive = [pltpu.make_async_copy(source.at[r], held.at[r], in_sem.at[n]) for n, r in enumerate(rows)]
    leave = [pltpu.make_async_copy(held.at[r], target.at[r], out_sem.at[n]) for n, r in enumerate(rows)]
    for copy in arrive:
        copy.start()
    for n in range(PEERS):
        arrive[n].wait()
        leave[n].start()
    for copy in leave:
        copy.wait()


def per_device(queries, key_codes, value_codes, key_exponents, value_exponents, trace_ids):
    hbm = pl.BlockSpec(memory_space=pl.ANY)
    dma = pltpu.SemaphoreType.DMA
    attended = pl.pallas_call(
        kernel,
        out_shape=jax.ShapeDtypeStruct((BLOCK, GROUP * D), BF16),
        in_specs=[hbm] * 6,
        out_specs=hbm,
        scratch_shapes=[
            pltpu.VMEM((ROWS, PEERS * GROUP * D), BF16),
            pltpu.VMEM((ROWS, PEERS * D), BF16),
            pltpu.VMEM((ROWS, PEERS * D), BF16),
            pltpu.VMEM((PEERS, ROWS), jnp.int32),
            pltpu.VMEM((PEERS, ROWS), jnp.int32),
            pltpu.VMEM((1, BLOCK), jnp.int32),
            pltpu.VMEM((PEERS, ROWS, 2 * D), BF16),
            pltpu.VMEM((BLOCK, 2 * D), BF16),
            pltpu.VMEM((BLOCK, 2 * D), BF16),
            pltpu.VMEM((STEPS + 1, KV_ROWS, D), BF16),
            pltpu.VMEM((PEERS, ROWS, GROUP * D), BF16),
            pltpu.VMEM((4, 3, D, BLOCK // 2), BF16),
            pltpu.VMEM((BLOCK, D), BF16),
            pltpu.VMEM((STEPS + 1, BLOCK, D), BF16),
            pltpu.VMEM((3, BLOCK, BLOCK), F32),
            pltpu.VMEM((8, BLOCK), F32),
            pltpu.VMEM((4, 1, BLOCK), F32),
            pltpu.VMEM((4, 8, BLOCK), F32),
            pltpu.VMEM((4, D, BLOCK), F32),
            pltpu.VMEM((PEERS, ROWS, GROUP * D), BF16),
            dma((7,)), dma((PEERS,)), dma((PEERS,)), dma((PEERS,)), dma((PEERS,)),
            dma((PEERS + 1,)), dma((PEERS + 1,)), dma((STEPS + 1,)), dma((STEPS + 1,)), dma((PEERS,)),
        ],
        compiler_params=pltpu.CompilerParams(
            collective_id=0, has_side_effects=True, vmem_limit_bytes=62 * 1024 * 1024
        ),
        cost_estimate=pl.CostEstimate(flops=9_000_000_000, bytes_accessed=4_000_000, transcendentals=8_700_000),
    )(
        queries, key_codes, value_codes, key_exponents.T, value_exponents.T, trace_ids.reshape(1, BLOCK)
    )
    return pl.pallas_call(
        hand_over,
        out_shape=jax.ShapeDtypeStruct((BLOCK, GROUP * D), BF16),
        in_specs=[hbm],
        out_specs=hbm,
        scratch_shapes=[pltpu.VMEM((BLOCK, GROUP * D), BF16), dma((PEERS,)), dma((PEERS,))],
        compiler_params=pltpu.CompilerParams(vmem_limit_bytes=62 * 1024 * 1024),
    )(attended)


def solution(mesh):
    placed = (
        P(("ctx", "head"), None),
        P(("ctx", "head"), None),
        P(("ctx", "head"), None),
        P(("ctx", "head"), None),
        P(("ctx", "head"), None),
        P("ctx"),
    )
    return jax.shard_map(
        per_device, mesh=mesh, in_specs=placed, out_specs=P("ctx", "head"), check_vma=False
    )
```

```python
import math

import jax
import jax.numpy as jnp
from jax import lax
from jax.experimental import pallas as pl
from jax.experimental.pallas import tpu as pltpu
from jax.sharding import PartitionSpec as P

BLOCK = 512
ROWS = 64
PEERS = 8
GROUP = 8
D = 128
STEPS = 4
N_CTX = 32
SCALE = 1.0 / math.sqrt(D)
LOG2E_SCALE = SCALE * math.log2(math.e)
BIG = -1e30
META = BLOCK + 4 * D
KV_ROWS = META + 16
MESH = pl.DeviceIdType.MESH
F32 = jnp.float32
BF16 = jnp.bfloat16


def iota(shape, dimension):
    return lax.broadcasted_iota(jnp.int32, shape, dimension)


def nt_dot(a, b):
    return lax.dot_general(a, b, (((1,), (1,)), ((), ())), preferred_element_type=F32)


def kernel(
    q_hbm, kc_hbm, vc_hbm, ke_hbm, ve_hbm, ids_hbm, out_hbm,
    q_ref, kc_ref, vc_ref, ke_ref, ve_ref, ids_ref,
    kvs, kvr, kvr2, kvb, qb, qt, aug_q, aug_k, s_buf, top_s, m_s, l_s, o_s, ob,
    in_sem, kv_send, kv_recv, q_send, q_recv, a_send, a_recv, c_send, c_recv, out_sem,
):
    c = lax.axis_index("ctx")
    h = lax.axis_index("head")
    core = lax.rem(c, 2)
    hy, hx = h // 2, lax.rem(h, 2)

    y_low = lax.rem(hy, 2)

    def partner(turn, n):
        base = lax.rem(hy - y_low + 2 * turn, 4)
        flip = lax.rem(turn + n, 2)
        y = base + y_low + flip * (1 - 2 * y_low)
        return y * 2 + lax.rem(hx + n // 2, 2)

    others = [(turn, n) for turn in range(2) for n in range(4)][1:]
    peers = {r: partner(*others[r - 1]) for r in range(1, PEERS)}

    sibling = c + 1 - 2 * core

    barrier = pltpu.get_barrier_semaphore()
    for r in range(1, PEERS):
        pl.semaphore_signal(barrier, inc=1, device_id=(c, peers[r]), device_id_type=MESH)
    pl.semaphore_signal(barrier, inc=1, device_id=(sibling, h), device_id_type=MESH)
    @pl.when(c >= 2)
    def _():
        for j in range(PEERS):
            pl.semaphore_signal(barrier, inc=1, device_id=(c - 2, j), device_id_type=MESH)

    @pl.when(c < N_CTX - 2)
    def _():
        for j in range(PEERS):
            pl.semaphore_signal(barrier, inc=1, device_id=(c + 2, j), device_id_type=MESH)

    @pl.when(c >= 4)
    def _():
        pl.semaphore_signal(barrier, inc=1, device_id=(c - 4, h), device_id_type=MESH)

    @pl.when(c < N_CTX - 4)
    def _():
        pl.semaphore_signal(barrier, inc=1, device_id=(c + 4, h), device_id_type=MESH)

    fetches = [
        pltpu.make_async_copy(source, target, in_sem.at[number])
        for number, (source, target) in enumerate(
            (
                (ke_hbm, ke_ref), (ve_hbm, ve_ref), (kc_hbm, kc_ref), (vc_hbm, vc_ref), (ids_hbm, ids_ref),
                (q_hbm, q_ref),
            )
        )
    ]
    for fetch in fetches:
        fetch.start()

    def q_columns(peer):
        return q_ref.at[:, pl.ds(pl.multiple_of(peer * GROUP * D, GROUP * D), GROUP * D)]

    own_q = pltpu.make_async_copy(q_columns(h), qb.at[h], in_sem.at[6])

    bits = iota((D, D), 0) & iota((D, D), 1)
    bits = bits ^ (bits >> 4)
    bits = bits ^ (bits >> 2)
    bits = bits ^ (bits >> 1)
    signs = (1 - 2 * (bits & 1)).astype(F32).astype(BF16)

    for fetch in fetches[:5]:
        fetch.wait()
    k_powers = jnp.exp2(ke_ref[...].astype(F32)).astype(BF16).astype(F32).T
    v_powers = jnp.exp2(ve_ref[...].astype(F32)).astype(BF16).astype(F32).T
    for j in range(PEERS):
        columns = slice(j * D, (j + 1) * D)
        kvs[j, :, 0:D] = (kc_ref[:, columns].astype(F32) * k_powers[:, j:j + 1]).astype(BF16)
        kvs[j, :, D:2 * D] = (vc_ref[:, columns].astype(F32) * v_powers[:, j:j + 1]).astype(BF16)

    ids = ids_ref[...]
    term = iota((D, BLOCK), 0)
    below = jnp.where(ids < term, 1.0, 0.0).astype(F32).astype(BF16)
    upto = jnp.where(ids <= term, 1.0, 0.0).astype(F32).astype(BF16)
    ones = jnp.ones((16, BLOCK), BF16)
    lo, hi = nt_dot(ones, below), nt_dot(ones, upto)
    lo_part, hi_part = jnp.floor(lo * (1.0 / 16)), jnp.floor(hi * (1.0 / 16))
    row = iota((16, D), 0)
    meta = jnp.where(
        row < 4, lo_part,
        jnp.where(row < 8, lo - 16 * lo_part, jnp.where(row < 12, hi_part, hi - 16 * hi_part)),
    )
    kvb[0, META:KV_ROWS] = meta.astype(BF16)

    pl.semaphore_wait(
        barrier,
        PEERS
        + PEERS * (c >= 2).astype(jnp.int32) + (c >= 4).astype(jnp.int32)
        + PEERS * (c < N_CTX - 2).astype(jnp.int32) + (c < N_CTX - 4).astype(jnp.int32),
    )

    my_rows = pl.ds(pl.multiple_of(h * ROWS, ROWS), ROWS)
    kv_copies = {}
    for r in range(1, PEERS):
        peer = peers[r]
        kv_copies[r] = pltpu.make_async_remote_copy(
            src_ref=kvs.at[peer], dst_ref=kvr.at[my_rows],
            send_sem=kv_send.at[r], recv_sem=kv_recv.at[r],
            device_id=(c, peer), device_id_type=MESH,
        )
        kv_copies[r].start()

    after2 = lax.rem(c + 2, N_CTX)
    a_copies = [
        pltpu.make_async_remote_copy(
            src_ref=kvs.at[j], dst_ref=kvr2.at[my_rows],
            send_sem=a_send.at[j], recv_sem=a_recv.at[h],
            device_id=(after2, j), device_id_type=MESH,
        )
        for j in range(PEERS)
    ]
    a_copies.append(
        pltpu.make_async_remote_copy(
            src_ref=kvb.at[0, META:KV_ROWS], dst_ref=kvb.at[2, META:KV_ROWS],
            send_sem=a_send.at[PEERS], recv_sem=a_recv.at[PEERS],
            device_id=(after2, h), device_id_type=MESH,
        )
    )

    @pl.when(c < N_CTX - 2)
    def _():
        for copy in a_copies:
            copy.start()

    def q_copy(r):
        peer = peers[r]
        return pltpu.make_async_remote_copy(
            src_ref=q_columns(peer), dst_ref=qb.at[h],
            send_sem=q_send.at[r], recv_sem=q_recv.at[h],
            device_id=(c, peer), device_id_type=MESH,
        )

    q_copies = {r: q_copy(r) for r in range(1, PEERS)}
    fetches[5].wait()
    own_q.start()
    for r in (1, 4, 5):
        q_copies[r].start()
    kvr[my_rows] = kvs[h]

    token = iota((BLOCK, D), 0).astype(F32)
    lane = iota((BLOCK, D), 1)
    inside = (token >= lo[0:1]) & (token < hi[0:1])
    diagonal = (lane >= D - ROWS) & (lax.rem(iota((BLOCK, D), 0), ROWS) == lane - (D - ROWS))
    aug_q[...] = jnp.where(inside | diagonal, 1.0, 0.0).astype(F32).astype(BF16)

    def key_spans(d):
        spans = kvb[d, META:KV_ROWS].astype(F32)
        first = spans[0:1] * 16 + spans[4:5]
        last = spans[8:9] * 16 + spans[12:13]
        member = (token >= first) & (token < last)
        aug_k[d] = jnp.where(member | (lane >= D - ROWS), 0.0, BIG).astype(F32).astype(BF16)

    for r in range(1, PEERS):
        kv_copies[r].wait_recv()

    def rotate(codes, slot):
        keys = jnp.dot(codes[:, 0:D], signs, preferred_element_type=F32) * SCALE
        kvb[slot, 0:BLOCK] = keys.astype(BF16)
        values = (nt_dot(signs, codes[:, D:2 * D]) * SCALE).astype(BF16)
        for part in range(4):
            kvb[slot, BLOCK + part * D:BLOCK + (part + 1) * D] = values[:, part * D:(part + 1) * D]

    def c_copy(source, slot, target):
        return pltpu.make_async_remote_copy(
            src_ref=kvb.at[source], dst_ref=kvb.at[slot],
            send_sem=c_send.at[slot], recv_sem=c_recv.at[slot],
            device_id=(target, h), device_id_type=MESH,
        )

    c_copies = {
        1: c_copy(2 * core, 1, sibling),
        3: c_copy(2 + 2 * core, 3, sibling),
        4: c_copy(0, 4, lax.rem(c + 4, N_CTX)),
    }
    rotate(kvr, 0)

    @pl.when(c < N_CTX - 4)
    def _():
        c_copies[4].start()

    @pl.when(core == 0)
    def _():
        c_copies[1].start()

    for r in (2, 3):
        q_copies[r].start()

    @pl.when(core == 0)
    def _():
        for r in (6, 7):
            q_copies[r].start()

    key_spans(0)

    @pl.when(c >= 2)
    def _():
        for j in range(PEERS):
            pltpu.make_async_remote_copy(
                src_ref=kvs.at[0], dst_ref=kvr2.at[j * ROWS:(j + 1) * ROWS],
                send_sem=a_send.at[0], recv_sem=a_recv.at[j],
                device_id=(after2, h), device_id_type=MESH,
            ).wait_recv()
        a_copies[PEERS].wait_recv()
        rotate(kvr2, 2)

    @pl.when(c < 2)
    def _():
        kvb[2] = jnp.zeros((KV_ROWS, D), BF16)

    @pl.when(c < 4)
    def _():
        kvb[4] = jnp.zeros((KV_ROWS, D), BF16)

    @pl.when(core == 0)
    def _():
        c_copies[3].start()

    @pl.when(core == 1)
    def _():
        c_copies[1].start()
        for r in (6, 7):
            q_copies[r].start()

    key_spans(2)
    c_copies[1].wait_recv()
    key_spans(1)

    def pass_on_farther_block():
        @pl.when(c >= 4)
        def _():
            c_copies[4].wait_recv()

        c_copies[3].start()

    def receive_farther_blocks():
        @pl.when((core == 0) & (c >= 4))
        def _():
            c_copies[4].wait_recv()

        key_spans(4)
        c_copies[3].wait_recv()
        key_spans(3)

    half = BLOCK // 2

    rows_of = [slice(0, half), slice(half, BLOCK)]

    def turn_queries(n, p):
        for g in range(2):
            heads = [qb[p, :, m * D:(m + 1) * D] for m in range(g * GROUP // 2, (g + 1) * GROUP // 2)]
            qt[n, g] = jnp.concatenate(heads, axis=0).T
        extra = aug_q[pl.ds(pl.multiple_of(p * ROWS, ROWS), ROWS)]
        qt[n, 2] = jnp.concatenate([extra] * (GROUP // 2), axis=0).T

    def score(n, p, d, k, g, top, buffer):
        queries = jnp.concatenate([qt[n, g], qt[n, 2]], axis=0)
        extra_keys = aug_k[d, k:k + half]
        if d == 0:
            column = iota((half, D), 1)
            late = (iota((half, D), 0) + k - p * ROWS > column - (D - ROWS)) & (column >= D - ROWS)
            extra_keys = jnp.where(late, BIG, extra_keys.astype(F32)).astype(BF16)
        keys = jnp.concatenate([kvb[d, k:k + half], extra_keys], axis=1)
        scores = jnp.dot(keys, queries, preferred_element_type=F32)
        s_buf[buffer, k:k + half, rows_of[g]] = scores
        here = jnp.max(scores.reshape(half // 8, 8, half), axis=0)
        top[g] = here if top[g] is None else jnp.maximum(top[g], here)

    def values_of(d, k):
        parts = [kvb[d, BLOCK + part * D:BLOCK + (part + 1) * D] for part in range(k // D, (k + half) // D)]
        return jnp.concatenate(parts, axis=1)

    def out_copy(p):
        rows = pl.ds(pl.multiple_of(p * ROWS, ROWS), ROWS)
        return pltpu.make_async_copy(ob.at[p], out_hbm.at[rows], out_sem.at[p])

    def pieces(span):
        return [(k, g) for g in range(2) for k in range(*span, half)]

    def attend(n, p, following, steps, spans, buffers):
        top = [top_s[:, rows_of[g]] for g in range(2)]
        if steps[0]:
            running = [m_s[n, :, rows_of[g]] for g in range(2)]
            total = [l_s[n, :, rows_of[g]] for g in range(2)]
            accum = [o_s[n, :, rows_of[g]] for g in range(2)]
        else:
            running, total, accum = [None, None], [None, None], [None, None]
        for place, d in enumerate(steps):
            next_top = [None, None]
            later = (n, p, steps[place + 1]) if d != steps[-1] else (*following, steps[0])
            now, ahead = pieces(spans[d]), pieces(spans[later[2]])
            for slot in range(max(len(now), len(ahead))):
                if slot < len(ahead):
                    score(*later, *ahead[slot], next_top, buffers[later[2]])
                if slot >= len(now):
                    continue
                k, g = now[slot]
                if top[g] is not None:
                    newmax = jnp.max(top[g], axis=0, keepdims=True)
                    if d:
                        newmax = jnp.maximum(running[g], newmax)
                        factor = jnp.exp2((running[g] - newmax) * LOG2E_SCALE)
                        total[g] = total[g] * factor
                        accum[g] = accum[g] * factor
                    running[g] = newmax
                    top[g] = None
                scores = s_buf[buffers[d], k:k + half, rows_of[g]]
                weights = jnp.exp2((scores - running[g]) * LOG2E_SCALE)
                sums = jnp.sum(weights.reshape(half // 8, 8, half), axis=0)
                product = jnp.dot(values_of(d, k), weights.astype(BF16), preferred_element_type=F32)
                total[g] = sums if total[g] is None else total[g] + sums
                accum[g] = product if accum[g] is None else accum[g] + product
            top = next_top
        for g in range(2):
            top_s[:, rows_of[g]] = top[g]
            if steps[-1] < STEPS:
                m_s[n, :, rows_of[g]], l_s[n, :, rows_of[g]], o_s[n, :, rows_of[g]] = running[g], total[g], accum[g]
                continue
            attended = accum[g] * (1.0 / jnp.sum(total[g], axis=0, keepdims=True))
            attended = attended.T.astype(BF16)
            for member in range(GROUP // 2):
                column = (g * GROUP // 2 + member) * D
                ob[p, :, column:column + D] = attended[member * ROWS:(member + 1) * ROWS]
        if steps[-1] == STEPS:
            out_copy(p).start()

    def await_queries(turn, n):
        p = partner(turn, n)
        pltpu.make_async_remote_copy(
            src_ref=q_columns(h), dst_ref=qb.at[p],
            send_sem=q_send.at[0], recv_sem=q_recv.at[p],
            device_id=(c, lax.rem(h + 1, PEERS)), device_id_type=MESH,
        ).wait_recv()

    def four_chunks(turn, steps, spans, buffers):
        if not steps[0]:
            turn_queries(0, partner(turn, 0))
        top = [None, None]
        for k, g in pieces(spans[steps[0]]):
            score(0, partner(turn, 0), steps[0], k, g, top, buffers[steps[0]])
        for g in range(2):
            top_s[:, rows_of[g]] = top[g]

        def body(n, carry):
            if steps == (0, 1, 2):
                @pl.when((n == 2) & (core == 1))
                def _():
                    pass_on_farther_block()

            if not steps[0]:
                @pl.when(n < 3)
                def _():
                    await_queries(turn, n + 1)
                    turn_queries(n + 1, partner(turn, n + 1))

            after = jnp.minimum(n + 1, 3)
            attend(n, partner(turn, n), (after, partner(turn, after)), steps, spans, buffers)
            return carry

        lax.fori_loop(0, 4, body, 0)

    whole = (0, BLOCK)
    early = {0: (0, half), 1: whole, 2: whole, 3: whole, 4: whole}
    late = {0: whole, 1: whole, 2: whole, 3: whole, 4: (half, BLOCK)}
    own_early = hy < 2

    def either(first, *arguments):
        @pl.when(first)
        def _():
            four_chunks(*arguments[:2], early, arguments[2])

        @pl.when(jnp.logical_not(first))
        def _():
            four_chunks(*arguments[:2], late, arguments[2])

    own_q.wait()
    either(own_early, 0, (0, 1, 2), {0: 0, 1: 1, 2: 2})
    receive_farther_blocks()
    either(own_early, 0, (3, 4), {3: 0, 4: 1})
    await_queries(1, 0)
    either(jnp.logical_not(own_early), 1, (0, 1, 2, 3, 4), {0: 0, 1: 1, 2: 0, 3: 1, 4: 2})

    for p in range(PEERS):
        out_copy(p).wait()
    for r in range(1, PEERS):
        kv_copies[r].wait_send()
        q_copies[r].wait_send()
    for step in (1, 3):
        c_copies[step].wait_send()

    @pl.when(c < N_CTX - 2)
    def _():
        for copy in a_copies:
            copy.wait_send()

    @pl.when(c < N_CTX - 4)
    def _():
        c_copies[4].wait_send()


def hand_over(source, target, held, in_sem, out_sem):
    rows = [pl.ds(p * ROWS, ROWS) for p in range(PEERS)]
    arrive = [pltpu.make_async_copy(source.at[r], held.at[r], in_sem.at[n]) for n, r in enumerate(rows)]
    leave = [pltpu.make_async_copy(held.at[r], target.at[r], out_sem.at[n]) for n, r in enumerate(rows)]
    for copy in arrive:
        copy.start()
    for n in range(PEERS):
        arrive[n].wait()
        leave[n].start()
    for copy in leave:
        copy.wait()


def per_device(queries, key_codes, value_codes, key_exponents, value_exponents, trace_ids):
    hbm = pl.BlockSpec(memory_space=pl.ANY)
    dma = pltpu.SemaphoreType.DMA
    attended = pl.pallas_call(
        kernel,
        out_shape=jax.ShapeDtypeStruct((BLOCK, GROUP * D), BF16),
        in_specs=[hbm] * 6,
        out_specs=hbm,
        scratch_shapes=[
            pltpu.VMEM((ROWS, PEERS * GROUP * D), BF16),
            pltpu.VMEM((ROWS, PEERS * D), BF16),
            pltpu.VMEM((ROWS, PEERS * D), BF16),
            pltpu.VMEM((PEERS, ROWS), jnp.int32),
            pltpu.VMEM((PEERS, ROWS), jnp.int32),
            pltpu.VMEM((1, BLOCK), jnp.int32),
            pltpu.VMEM((PEERS, ROWS, 2 * D), BF16),
            pltpu.VMEM((BLOCK, 2 * D), BF16),
            pltpu.VMEM((BLOCK, 2 * D), BF16),
            pltpu.VMEM((STEPS + 1, KV_ROWS, D), BF16),
            pltpu.VMEM((PEERS, ROWS, GROUP * D), BF16),
            pltpu.VMEM((4, 3, D, BLOCK // 2), BF16),
            pltpu.VMEM((BLOCK, D), BF16),
            pltpu.VMEM((STEPS + 1, BLOCK, D), BF16),
            pltpu.VMEM((3, BLOCK, BLOCK), F32),
            pltpu.VMEM((8, BLOCK), F32),
            pltpu.VMEM((4, 1, BLOCK), F32),
            pltpu.VMEM((4, 8, BLOCK), F32),
            pltpu.VMEM((4, D, BLOCK), F32),
            pltpu.VMEM((PEERS, ROWS, GROUP * D), BF16),
            dma((7,)), dma((PEERS,)), dma((PEERS,)), dma((PEERS,)), dma((PEERS,)),
            dma((PEERS + 1,)), dma((PEERS + 1,)), dma((STEPS + 1,)), dma((STEPS + 1,)), dma((PEERS,)),
        ],
        compiler_params=pltpu.CompilerParams(
            collective_id=0, has_side_effects=True, vmem_limit_bytes=62 * 1024 * 1024
        ),
        cost_estimate=pl.CostEstimate(flops=9_000_000_000, bytes_accessed=4_000_000, transcendentals=8_700_000),
    )(
        queries, key_codes, value_codes, key_exponents.T, value_exponents.T, trace_ids.reshape(1, BLOCK)
    )
    return pl.pallas_call(
        hand_over,
        out_shape=jax.ShapeDtypeStruct((BLOCK, GROUP * D), BF16),
        in_specs=[hbm],
        out_specs=hbm,
        scratch_shapes=[pltpu.VMEM((BLOCK, GROUP * D), BF16), dma((PEERS,)), dma((PEERS,))],
        compiler_params=pltpu.CompilerParams(vmem_limit_bytes=62 * 1024 * 1024),
    )(attended)


def solution(mesh):
    placed = (
        P(("ctx", "head"), None),
        P(("ctx", "head"), None),
        P(("ctx", "head"), None),
        P(("ctx", "head"), None),
        P(("ctx", "head"), None),
        P("ctx"),
    )
    return jax.shard_map(
        per_device, mesh=mesh, in_specs=placed, out_specs=P("ctx", "head"), check_vma=False
    )
```

```python
import math

import jax
import jax.numpy as jnp
from jax import lax
from jax.experimental import pallas as pl
from jax.experimental.pallas import tpu as pltpu
from jax.sharding import PartitionSpec as P

BLOCK = 512
ROWS = 64
PEERS = 8
GROUP = 8
D = 128
STEPS = 4
N_CTX = 32
SCALE = 1.0 / math.sqrt(D)
LOG2E_SCALE = SCALE * math.log2(math.e)
BIG = -1e30
META = BLOCK + 4 * D
KV_ROWS = META + 16
MESH = pl.DeviceIdType.MESH
F32 = jnp.float32
BF16 = jnp.bfloat16


def iota(shape, dimension):
    return lax.broadcasted_iota(jnp.int32, shape, dimension)


def nt_dot(a, b):
    return lax.dot_general(a, b, (((1,), (1,)), ((), ())), preferred_element_type=F32)


def kernel(
    q_hbm, kc_hbm, vc_hbm, ke_hbm, ve_hbm, ids_hbm, out_hbm,
    q_ref, kc_ref, vc_ref, ke_ref, ve_ref, ids_ref,
    kvs, kvr, kvr2, kvb, qb, qt, aug_q, aug_k, s_buf, top_s, m_s, l_s, o_s, ob,
    in_sem, kv_send, kv_recv, q_send, q_recv, a_send, a_recv, c_send, c_recv, out_sem,
):
    c = lax.axis_index("ctx")
    h = lax.axis_index("head")
    core = lax.rem(c, 2)
    hy, hx = h // 2, lax.rem(h, 2)

    y_low = lax.rem(hy, 2)

    def partner(turn, n):
        base = lax.rem(hy - y_low + 2 * turn, 4)
        flip = lax.rem(turn + n, 2)
        y = base + y_low + flip * (1 - 2 * y_low)
        return y * 2 + lax.rem(hx + n // 2, 2)

    others = [(turn, n) for turn in range(2) for n in range(4)][1:]
    peers = {r: partner(*others[r - 1]) for r in range(1, PEERS)}

    sibling = c + 1 - 2 * core

    barrier = pltpu.get_barrier_semaphore()
    for r in range(1, PEERS):
        pl.semaphore_signal(barrier, inc=1, device_id=(c, peers[r]), device_id_type=MESH)
    pl.semaphore_signal(barrier, inc=1, device_id=(sibling, h), device_id_type=MESH)
    @pl.when(c >= 2)
    def _():
        for j in range(PEERS):
            pl.semaphore_signal(barrier, inc=1, device_id=(c - 2, j), device_id_type=MESH)

    @pl.when(c < N_CTX - 2)
    def _():
        for j in range(PEERS):
            pl.semaphore_signal(barrier, inc=1, device_id=(c + 2, j), device_id_type=MESH)

    @pl.when(c >= 4)
    def _():
        pl.semaphore_signal(barrier, inc=1, device_id=(c - 4, h), device_id_type=MESH)

    @pl.when(c < N_CTX - 4)
    def _():
        pl.semaphore_signal(barrier, inc=1, device_id=(c + 4, h), device_id_type=MESH)

    fetches = [
        pltpu.make_async_copy(source, target, in_sem.at[number])
        for number, (source, target) in enumerate(
            (
                (ke_hbm, ke_ref), (ve_hbm, ve_ref), (kc_hbm, kc_ref), (vc_hbm, vc_ref), (ids_hbm, ids_ref),
                (q_hbm, q_ref),
            )
        )
    ]
    for fetch in fetches:
        fetch.start()

    def q_columns(peer):
        return q_ref.at[:, pl.ds(pl.multiple_of(peer * GROUP * D, GROUP * D), GROUP * D)]

    own_q = pltpu.make_async_copy(q_columns(h), qb.at[h], in_sem.at[6])

    bits = iota((D, D), 0) & iota((D, D), 1)
    bits = bits ^ (bits >> 4)
    bits = bits ^ (bits >> 2)
    bits = bits ^ (bits >> 1)
    signs = (1 - 2 * (bits & 1)).astype(F32).astype(BF16)

    for fetch in fetches[:5]:
        fetch.wait()
    k_powers = jnp.exp2(ke_ref[...].astype(F32)).astype(BF16).astype(F32).T
    v_powers = jnp.exp2(ve_ref[...].astype(F32)).astype(BF16).astype(F32).T
    for j in range(PEERS):
        columns = slice(j * D, (j + 1) * D)
        kvs[j, :, 0:D] = (kc_ref[:, columns].astype(F32) * k_powers[:, j:j + 1]).astype(BF16)
        kvs[j, :, D:2 * D] = (vc_ref[:, columns].astype(F32) * v_powers[:, j:j + 1]).astype(BF16)

    ids = ids_ref[...]
    term = iota((D, BLOCK), 0)
    below = jnp.where(ids < term, 1.0, 0.0).astype(F32).astype(BF16)
    upto = jnp.where(ids <= term, 1.0, 0.0).astype(F32).astype(BF16)
    ones = jnp.ones((16, BLOCK), BF16)
    lo, hi = nt_dot(ones, below), nt_dot(ones, upto)
    lo_part, hi_part = jnp.floor(lo * (1.0 / 16)), jnp.floor(hi * (1.0 / 16))
    row = iota((16, D), 0)
    meta = jnp.where(
        row < 4, lo_part,
        jnp.where(row < 8, lo - 16 * lo_part, jnp.where(row < 12, hi_part, hi - 16 * hi_part)),
    )
    kvb[0, META:KV_ROWS] = meta.astype(BF16)

    pl.semaphore_wait(
        barrier,
        PEERS
        + PEERS * (c >= 2).astype(jnp.int32) + (c >= 4).astype(jnp.int32)
        + PEERS * (c < N_CTX - 2).astype(jnp.int32) + (c < N_CTX - 4).astype(jnp.int32),
    )

    my_rows = pl.ds(pl.multiple_of(h * ROWS, ROWS), ROWS)
    kv_copies = {}
    for r in range(1, PEERS):
        peer = peers[r]
        kv_copies[r] = pltpu.make_async_remote_copy(
            src_ref=kvs.at[peer], dst_ref=kvr.at[my_rows],
            send_sem=kv_send.at[r], recv_sem=kv_recv.at[r],
            device_id=(c, peer), device_id_type=MESH,
        )
        kv_copies[r].start()

    after2 = lax.rem(c + 2, N_CTX)
    a_copies = [
        pltpu.make_async_remote_copy(
            src_ref=kvs.at[j], dst_ref=kvr2.at[my_rows],
            send_sem=a_send.at[j], recv_sem=a_recv.at[h],
            device_id=(after2, j), device_id_type=MESH,
        )
        for j in range(PEERS)
    ]
    a_copies.append(
        pltpu.make_async_remote_copy(
            src_ref=kvb.at[0, META:KV_ROWS], dst_ref=kvb.at[2, META:KV_ROWS],
            send_sem=a_send.at[PEERS], recv_sem=a_recv.at[PEERS],
            device_id=(after2, h), device_id_type=MESH,
        )
    )

    @pl.when(c < N_CTX - 2)
    def _():
        for copy in a_copies:
            copy.start()

    def q_copy(r):
        peer = peers[r]
        return pltpu.make_async_remote_copy(
            src_ref=q_columns(peer), dst_ref=qb.at[h],
            send_sem=q_send.at[r], recv_sem=q_recv.at[h],
            device_id=(c, peer), device_id_type=MESH,
        )

    q_copies = {r: q_copy(r) for r in range(1, PEERS)}
    fetches[5].wait()
    own_q.start()
    for r in (1,):
        q_copies[r].start()
    kvr[my_rows] = kvs[h]

    token = iota((BLOCK, D), 0).astype(F32)
    lane = iota((BLOCK, D), 1)
    inside = (token >= lo[0:1]) & (token < hi[0:1])
    diagonal = (lane >= D - ROWS) & (lax.rem(iota((BLOCK, D), 0), ROWS) == lane - (D - ROWS))
    aug_q[...] = jnp.where(inside | diagonal, 1.0, 0.0).astype(F32).astype(BF16)

    def key_spans(d):
        spans = kvb[d, META:KV_ROWS].astype(F32)
        first = spans[0:1] * 16 + spans[4:5]
        last = spans[8:9] * 16 + spans[12:13]
        member = (token >= first) & (token < last)
        aug_k[d] = jnp.where(member | (lane >= D - ROWS), 0.0, BIG).astype(F32).astype(BF16)

    for r in range(1, PEERS):
        kv_copies[r].wait_recv()

    def rotate(codes, slot):
        keys = jnp.dot(codes[:, 0:D], signs, preferred_element_type=F32) * SCALE
        kvb[slot, 0:BLOCK] = keys.astype(BF16)
        values = (nt_dot(signs, codes[:, D:2 * D]) * SCALE).astype(BF16)
        for part in range(4):
            kvb[slot, BLOCK + part * D:BLOCK + (part + 1) * D] = values[:, part * D:(part + 1) * D]

    def c_copy(source, slot, target):
        return pltpu.make_async_remote_copy(
            src_ref=kvb.at[source], dst_ref=kvb.at[slot],
            send_sem=c_send.at[slot], recv_sem=c_recv.at[slot],
            device_id=(target, h), device_id_type=MESH,
        )

    c_copies = {
        1: c_copy(2 * core, 1, sibling),
        3: c_copy(2 + 2 * core, 3, sibling),
        4: c_copy(0, 4, lax.rem(c + 4, N_CTX)),
    }
    rotate(kvr, 0)

    @pl.when(c < N_CTX - 4)
    def _():
        c_copies[4].start()

    @pl.when(core == 0)
    def _():
        c_copies[1].start()

    for r in (2, 3, 4, 6, 5, 7):
        q_copies[r].start()
    key_spans(0)

    @pl.when(c >= 2)
    def _():
        for j in range(PEERS):
            pltpu.make_async_remote_copy(
                src_ref=kvs.at[0], dst_ref=kvr2.at[j * ROWS:(j + 1) * ROWS],
                send_sem=a_send.at[0], recv_sem=a_recv.at[j],
                device_id=(after2, h), device_id_type=MESH,
            ).wait_recv()
        a_copies[PEERS].wait_recv()
        rotate(kvr2, 2)

    @pl.when(c < 2)
    def _():
        kvb[2] = jnp.zeros((KV_ROWS, D), BF16)

    @pl.when(c < 4)
    def _():
        kvb[4] = jnp.zeros((KV_ROWS, D), BF16)

    @pl.when(core == 0)
    def _():
        c_copies[3].start()

    @pl.when(core == 1)
    def _():
        c_copies[1].start()

    key_spans(2)
    c_copies[1].wait_recv()
    key_spans(1)

    def pass_on_farther_block():
        @pl.when(c >= 4)
        def _():
            c_copies[4].wait_recv()

        c_copies[3].start()

    def receive_farther_blocks():
        @pl.when((core == 0) & (c >= 4))
        def _():
            c_copies[4].wait_recv()

        key_spans(4)
        c_copies[3].wait_recv()
        key_spans(3)

    half = BLOCK // 2

    rows_of = [slice(0, half), slice(half, BLOCK)]

    def turn_queries(n, p):
        for g in range(2):
            heads = [qb[p, :, m * D:(m + 1) * D] for m in range(g * GROUP // 2, (g + 1) * GROUP // 2)]
            qt[n, g] = jnp.concatenate(heads, axis=0).T
        extra = aug_q[pl.ds(pl.multiple_of(p * ROWS, ROWS), ROWS)]
        qt[n, 2] = jnp.concatenate([extra] * (GROUP // 2), axis=0).T

    def score(n, p, d, k, g, top, buffer):
        queries = jnp.concatenate([qt[n, g], qt[n, 2]], axis=0)
        extra_keys = aug_k[d, k:k + half]
        if d == 0:
            column = iota((half, D), 1)
            late = (iota((half, D), 0) + k - p * ROWS > column - (D - ROWS)) & (column >= D - ROWS)
            extra_keys = jnp.where(late, BIG, extra_keys.astype(F32)).astype(BF16)
        keys = jnp.concatenate([kvb[d, k:k + half], extra_keys], axis=1)
        scores = jnp.dot(keys, queries, preferred_element_type=F32)
        s_buf[buffer, k:k + half, rows_of[g]] = scores
        here = jnp.max(scores.reshape(half // 8, 8, half), axis=0)
        top[g] = here if top[g] is None else jnp.maximum(top[g], here)

    def values_of(d, k):
        parts = [kvb[d, BLOCK + part * D:BLOCK + (part + 1) * D] for part in range(k // D, (k + half) // D)]
        return jnp.concatenate(parts, axis=1)

    def out_copy(p):
        rows = pl.ds(pl.multiple_of(p * ROWS, ROWS), ROWS)
        return pltpu.make_async_copy(ob.at[p], out_hbm.at[rows], out_sem.at[p])

    def pieces(span):
        return [(k, g) for g in range(2) for k in range(*span, half)]

    def attend(n, p, following, steps, spans, buffers):
        top = [top_s[:, rows_of[g]] for g in range(2)]
        if steps[0]:
            running = [m_s[n, :, rows_of[g]] for g in range(2)]
            total = [l_s[n, :, rows_of[g]] for g in range(2)]
            accum = [o_s[n, :, rows_of[g]] for g in range(2)]
        else:
            running, total, accum = [None, None], [None, None], [None, None]
        for place, d in enumerate(steps):
            next_top = [None, None]
            later = (n, p, steps[place + 1]) if d != steps[-1] else (*following, steps[0])
            now, ahead = pieces(spans[d]), pieces(spans[later[2]])
            for slot in range(max(len(now), len(ahead))):
                if slot < len(ahead):
                    score(*later, *ahead[slot], next_top, buffers[later[2]])
                if slot >= len(now):
                    continue
                k, g = now[slot]
                if top[g] is not None:
                    newmax = jnp.max(top[g], axis=0, keepdims=True)
                    if d:
                        newmax = jnp.maximum(running[g], newmax)
                        factor = jnp.exp2((running[g] - newmax) * LOG2E_SCALE)
                        total[g] = total[g] * factor
                        accum[g] = accum[g] * factor
                    running[g] = newmax
                    top[g] = None
                scores = s_buf[buffers[d], k:k + half, rows_of[g]]
                weights = jnp.exp2((scores - running[g]) * LOG2E_SCALE)
                sums = jnp.sum(weights.reshape(half // 8, 8, half), axis=0)
                product = jnp.dot(values_of(d, k), weights.astype(BF16), preferred_element_type=F32)
                total[g] = sums if total[g] is None else total[g] + sums
                accum[g] = product if accum[g] is None else accum[g] + product
            top = next_top
        for g in range(2):
            top_s[:, rows_of[g]] = top[g]
            if steps[-1] < STEPS:
                m_s[n, :, rows_of[g]], l_s[n, :, rows_of[g]], o_s[n, :, rows_of[g]] = running[g], total[g], accum[g]
                continue
            attended = accum[g] * (1.0 / jnp.sum(total[g], axis=0, keepdims=True))
            attended = attended.T.astype(BF16)
            for member in range(GROUP // 2):
                column = (g * GROUP // 2 + member) * D
                ob[p, :, column:column + D] = attended[member * ROWS:(member + 1) * ROWS]
        if steps[-1] == STEPS:
            out_copy(p).start()

    def await_queries(turn, n):
        p = partner(turn, n)
        pltpu.make_async_remote_copy(
            src_ref=q_columns(h), dst_ref=qb.at[p],
            send_sem=q_send.at[0], recv_sem=q_recv.at[p],
            device_id=(c, lax.rem(h + 1, PEERS)), device_id_type=MESH,
        ).wait_recv()

    def four_chunks(turn, steps, spans, buffers):
        if not steps[0]:
            turn_queries(0, partner(turn, 0))
        top = [None, None]
        for k, g in pieces(spans[steps[0]]):
            score(0, partner(turn, 0), steps[0], k, g, top, buffers[steps[0]])
        for g in range(2):
            top_s[:, rows_of[g]] = top[g]

        def body(n, carry):
            if steps == (0, 1, 2):
                @pl.when((n == 2) & (core == 1))
                def _():
                    pass_on_farther_block()

            if not steps[0]:
                @pl.when(n < 3)
                def _():
                    await_queries(turn, n + 1)
                    turn_queries(n + 1, partner(turn, n + 1))

            after = jnp.minimum(n + 1, 3)
            attend(n, partner(turn, n), (after, partner(turn, after)), steps, spans, buffers)
            return carry

        lax.fori_loop(0, 4, body, 0)

    whole = (0, BLOCK)
    early = {0: (0, half), 1: whole, 2: whole, 3: whole, 4: whole}
    late = {0: whole, 1: whole, 2: whole, 3: whole, 4: (half, BLOCK)}
    own_early = hy < 2

    def either(first, *arguments):
        @pl.when(first)
        def _():
            four_chunks(*arguments[:2], early, arguments[2])

        @pl.when(jnp.logical_not(first))
        def _():
            four_chunks(*arguments[:2], late, arguments[2])

    own_q.wait()
    either(own_early, 0, (0, 1, 2), {0: 0, 1: 1, 2: 2})
    receive_farther_blocks()
    either(own_early, 0, (3, 4), {3: 0, 4: 1})
    await_queries(1, 0)
    either(jnp.logical_not(own_early), 1, (0, 1, 2, 3, 4), {0: 0, 1: 1, 2: 0, 3: 1, 4: 2})

    for p in range(PEERS):
        out_copy(p).wait()
    for r in range(1, PEERS):
        kv_copies[r].wait_send()
        q_copies[r].wait_send()
    for step in (1, 3):
        c_copies[step].wait_send()

    @pl.when(c < N_CTX - 2)
    def _():
        for copy in a_copies:
            copy.wait_send()

    @pl.when(c < N_CTX - 4)
    def _():
        c_copies[4].wait_send()


def hand_over(source, target, held, in_sem, out_sem):
    rows = [pl.ds(p * ROWS, ROWS) for p in range(PEERS)]
    arrive = [pltpu.make_async_copy(source.at[r], held.at[r], in_sem.at[n]) for n, r in enumerate(rows)]
    leave = [pltpu.make_async_copy(held.at[r], target.at[r], out_sem.at[n]) for n, r in enumerate(rows)]
    for copy in arrive:
        copy.start()
    for n in range(PEERS):
        arrive[n].wait()
        leave[n].start()
    for copy in leave:
        copy.wait()


def per_device(queries, key_codes, value_codes, key_exponents, value_exponents, trace_ids):
    hbm = pl.BlockSpec(memory_space=pl.ANY)
    dma = pltpu.SemaphoreType.DMA
    attended = pl.pallas_call(
        kernel,
        out_shape=jax.ShapeDtypeStruct((BLOCK, GROUP * D), BF16),
        in_specs=[hbm] * 6,
        out_specs=hbm,
        scratch_shapes=[
            pltpu.VMEM((ROWS, PEERS * GROUP * D), BF16),
            pltpu.VMEM((ROWS, PEERS * D), BF16),
            pltpu.VMEM((ROWS, PEERS * D), BF16),
            pltpu.VMEM((PEERS, ROWS), jnp.int32),
            pltpu.VMEM((PEERS, ROWS), jnp.int32),
            pltpu.VMEM((1, BLOCK), jnp.int32),
            pltpu.VMEM((PEERS, ROWS, 2 * D), BF16),
            pltpu.VMEM((BLOCK, 2 * D), BF16),
            pltpu.VMEM((BLOCK, 2 * D), BF16),
            pltpu.VMEM((STEPS + 1, KV_ROWS, D), BF16),
            pltpu.VMEM((PEERS, ROWS, GROUP * D), BF16),
            pltpu.VMEM((4, 3, D, BLOCK // 2), BF16),
            pltpu.VMEM((BLOCK, D), BF16),
            pltpu.VMEM((STEPS + 1, BLOCK, D), BF16),
            pltpu.VMEM((3, BLOCK, BLOCK), F32),
            pltpu.VMEM((8, BLOCK), F32),
            pltpu.VMEM((4, 1, BLOCK), F32),
            pltpu.VMEM((4, 8, BLOCK), F32),
            pltpu.VMEM((4, D, BLOCK), F32),
            pltpu.VMEM((PEERS, ROWS, GROUP * D), BF16),
            dma((7,)), dma((PEERS,)), dma((PEERS,)), dma((PEERS,)), dma((PEERS,)),
            dma((PEERS + 1,)), dma((PEERS + 1,)), dma((STEPS + 1,)), dma((STEPS + 1,)), dma((PEERS,)),
        ],
        compiler_params=pltpu.CompilerParams(
            collective_id=0, has_side_effects=True, vmem_limit_bytes=62 * 1024 * 1024
        ),
        cost_estimate=pl.CostEstimate(flops=9_000_000_000, bytes_accessed=4_000_000, transcendentals=8_700_000),
    )(
        queries, key_codes, value_codes, key_exponents.T, value_exponents.T, trace_ids.reshape(1, BLOCK)
    )
    return pl.pallas_call(
        hand_over,
        out_shape=jax.ShapeDtypeStruct((BLOCK, GROUP * D), BF16),
        in_specs=[hbm],
        out_specs=hbm,
        scratch_shapes=[pltpu.VMEM((BLOCK, GROUP * D), BF16), dma((PEERS,)), dma((PEERS,))],
        compiler_params=pltpu.CompilerParams(vmem_limit_bytes=62 * 1024 * 1024),
    )(attended)


def solution(mesh):
    placed = (
        P(("ctx", "head"), None),
        P(("ctx", "head"), None),
        P(("ctx", "head"), None),
        P(("ctx", "head"), None),
        P(("ctx", "head"), None),
        P("ctx"),
    )
    return jax.shard_map(
        per_device, mesh=mesh, in_specs=placed, out_specs=P("ctx", "head"), check_vma=False
    )
```
